128 devices in a mesh: dp: 16 (over z, x), seq: 8 (over y, core).
Axes of the slice: x: 4, y: 4, z: 4, core: 2. Of those that a mesh axis runs over, the one named last changes fastest.
Arguments:
- features: bfloat16 [16, 4096, 512], P('dp', 'seq'), may hold values from -16 to 16
- input_weight: bfloat16 [512, 1536], replicated, may hold values from -1 to 1
- output_weight: bfloat16 [512, 512], replicated, may hold values from -0.25 to 0.25
- key_blocks: int32 [16, 8, 32, 8], P('dp', 'seq'), may hold values from 0 to 31, as said below
- key_count: int32 [16, 8, 32], P('dp', 'seq'), may hold values from 1 to 8, as said below
- cotangent: bfloat16 [16, 4096, 512], P('dp', 'seq'), may hold values from -6 to 6
Outputs:
- layer_out: bfloat16 [16, 4096, 512], P('dp', 'seq')
- grad_features: bfloat16 [16, 4096, 512], P('dp', 'seq')
- input_weight_grad: float32 [512, 1536], replicated
- output_weight_grad: float32 [512, 512], replicated
The draws below stay inside these ranges and needn't reach their ends.
Inputs may be any that keep to these rules, and one draw needn't show every extreme that they name: `key_blocks`: slot 0 of query block i holds i; the other slots of one query block hold distinct blocks other than i. `key_count`: some query block of some head has 8 live slots in every draw.
All inputs are finite; a program needn't handle non-finite values.
Results may differ from the reference program's by a relative error of at most 0.029.
The reference program's roundings to bfloat16 on the way (of `qkv`, `weights`, `attended`, `grad_attended`, `grad_scores` and `grad_qkv_rows`) count: a program that leaves them out, or rounds other values in their place, can miss the bound.
Values may be sent and summed in bfloat16 or wider, within the bound.
A program may use at most 64 MiB of HBM per device.

```python
import math
import jax
import jax.numpy as jnp
from jax import lax

D = 512
H = 8
HD = 64
B = 128
KMAX = 8
GROUPS = 16
SPAN = 4096
NB = 32


def draw_features(key, part):
    key = jax.random.fold_in(key, 21)
    first_key = jax.random.fold_in(key, 0)
    values = jnp.clip(jax.random.normal(first_key, (GROUPS, SPAN, D), jnp.float32), -6.0, 6.0)
    return values.astype(jnp.bfloat16)


def draw_input_weight(key, part):
    key = jax.random.fold_in(key, 22)
    first_key = jax.random.fold_in(key, 0)
    spread = D ** (-0.5)
    matrix = jnp.clip(jax.random.normal(first_key, (D, 3 * D), jnp.float32), -6.0, 6.0) * spread
    return matrix.astype(jnp.bfloat16)


def draw_key_blocks(key, part):
    key = jax.random.fold_in(key, 23)
    ranks = jax.random.randint(key, (GROUPS, H, NB, NB - 1), 0, 1 << 20) * (NB - 1) + jnp.arange(NB - 1, dtype=jnp.int32)
    offsets = jnp.argsort(ranks, axis=-1)[..., :KMAX - 1].astype(jnp.int32) + 1
    diagonal = jnp.broadcast_to(jnp.arange(NB, dtype=jnp.int32)[:, None], (GROUPS, H, NB, 1))
    others = (diagonal + offsets) % NB
    return jnp.concatenate([diagonal, others], axis=-1).astype(jnp.int32)


def draw_key_count(key, part):
    key = jax.random.fold_in(key, 24)
    first_key, second_key, third_key = jax.random.split(key, 3)
    levels = KMAX.bit_length() - 1
    exponents = jax.random.randint(first_key, (GROUPS, H, 1), 0, levels + 1)
    limits = jnp.minimum(jnp.power(2, exponents), KMAX).astype(jnp.int32)
    counts = jax.random.randint(second_key, (GROUPS, H, NB), 0, 1 << 30) % limits + 1
    location = jax.random.randint(third_key, (), 0, GROUPS * H * NB)
    counts = counts.reshape(-1).at[location].set(KMAX).reshape(GROUPS, H, NB)
    return counts.astype(jnp.int32)


def block_levels(stream_key, dims, shards, least, largest):
    factor_of, own = 1.0, jax.random.fold_in(stream_key, 6)
    for position, parts in shards:
        heights = jnp.exp(jax.random.uniform(jax.random.fold_in(own, position), (parts,), jnp.float32, least / len(shards), largest / len(shards)))
        factor_of = factor_of * jnp.repeat(heights, dims[position] // parts).reshape([-1 if axis == position else 1 for axis in range(len(dims))])
    return factor_of


def centred(own_key, shape, deviation, reach, pieces=(), kind=jnp.bfloat16):
    values = jax.random.normal(own_key, shape, jnp.float32) * deviation
    if len(pieces) > 0:
        values = block_levels(own_key, shape, pieces, -0.22, 0.18) * values
    return jnp.clip(values, min=-reach, max=reach).astype(kind)


def setup_inputs(seed: int = 0) -> dict:
    seeds = jax.random.split(jax.random.key(seed), 7)
    features = draw_features(jax.random.fold_in(seeds[6], 71), 0)
    input_weight = draw_input_weight(jax.random.fold_in(seeds[6], 71), 0)
    output_weight = centred(seeds[2], (D, D), D ** -0.5, 0.25)
    key_blocks = draw_key_blocks(jax.random.fold_in(seeds[6], 71), 0)
    key_count = draw_key_count(jax.random.fold_in(seeds[6], 71), 0)
    cotangent = centred(seeds[5], (GROUPS, SPAN, D), 1.0, 6.0, ((0, 16), (1, 8)))
    return dict(features=features, input_weight=input_weight, output_weight=output_weight, key_blocks=key_blocks, key_count=key_count, cotangent=cotangent)


NEGATIVE = -1e+30

def block_probs(queries, key_tiles, live_count):
    scaling = queries.shape[0] ** (-0.5)
    scores = jnp.einsum('eqr,eqjc->qrjc', queries.astype(jnp.float32), key_tiles.astype(jnp.float32)) * scaling
    slot_ids = jnp.arange(key_tiles.shape[2])
    live_mask = (slot_ids[None, :] < live_count[:, None])[:, None, :, None]
    scores = jnp.where(live_mask, scores, NEGATIVE)
    highest = lax.optimization_barrier(jnp.max(scores, axis=(2, 3), keepdims=True))
    raised = jnp.exp(scores - highest)
    return raised / lax.optimization_barrier(jnp.sum(raised, axis=(2, 3), keepdims=True))

def head_pass(packed):
    queries, keys_all, values_all, grad_attended, blocks, counts = packed
    scaling = queries.shape[0] ** (-0.5)
    key_tiles = jnp.take(keys_all, blocks, axis=1)
    value_tiles = jnp.take(values_all, blocks, axis=1)
    weights_full = block_probs(queries, key_tiles, counts)
    weights = weights_full.astype(jnp.bfloat16)
    attended = jnp.einsum('qrjc,eqjc->eqr', weights.astype(jnp.float32), value_tiles.astype(jnp.float32)).astype(jnp.bfloat16)
    row_delta = lax.optimization_barrier(jnp.sum(attended.astype(jnp.float32) * grad_attended.astype(jnp.float32), axis=0))
    grad_probs = jnp.einsum('eqr,eqjc->qrjc', grad_attended.astype(jnp.float32), value_tiles.astype(jnp.float32))
    grad_scores = (weights_full * (grad_probs - row_delta[:, :, None, None]) * scaling).astype(jnp.bfloat16)
    grad_query = jnp.einsum('qrjc,eqjc->eqr', grad_scores.astype(jnp.float32), key_tiles.astype(jnp.float32)).astype(jnp.bfloat16)
    key_terms = jnp.einsum('qrjc,eqr->eqjc', grad_scores.astype(jnp.float32), queries.astype(jnp.float32))
    value_terms = jnp.einsum('qrjc,eqr->eqjc', weights.astype(jnp.float32), grad_attended.astype(jnp.float32))
    grad_keys = jnp.zeros(keys_all.shape, jnp.float32).at[:, blocks].add(key_terms).astype(jnp.bfloat16)
    grad_values = jnp.zeros(values_all.shape, jnp.float32).at[:, blocks].add(value_terms).astype(jnp.bfloat16)
    return (attended, grad_query, grad_keys, grad_values)

def reference(features, input_weight, output_weight, key_blocks, key_count, cotangent):

    def group_pass(totals, inputs):
        node_rows, grad_rows, blocks, counts = inputs
        qkv = jnp.dot(node_rows, input_weight, preferred_element_type=jnp.float32).astype(jnp.bfloat16)
        columns = qkv.T.reshape(3, H, HD, NB, B)
        grad_attended = jnp.dot(grad_rows, output_weight.T, preferred_element_type=jnp.float32).astype(jnp.bfloat16)
        grad_columns = grad_attended.T.reshape(H, HD, NB, B)
        attended, grad_query, grad_keys, grad_values = lax.map(head_pass, (columns[0], columns[1], columns[2], grad_columns, blocks, counts))
        attended_rows = attended.reshape(D, SPAN).T
        layer_out = (node_rows.astype(jnp.float32) + jnp.dot(attended_rows, output_weight, preferred_element_type=jnp.float32)).astype(jnp.bfloat16)
        grad_qkv_rows = jnp.stack([grad_query, grad_keys, grad_values]).reshape(3 * D, SPAN).T
        grad_features = (grad_rows.astype(jnp.float32) + jnp.dot(grad_qkv_rows, input_weight.T, preferred_element_type=jnp.float32)).astype(jnp.bfloat16)
        input_total = totals[0] + jnp.dot(node_rows.T, grad_qkv_rows, preferred_element_type=jnp.float32)
        output_total = totals[1] + jnp.dot(attended_rows.T, grad_rows, preferred_element_type=jnp.float32)
        return ((input_total, output_total), (layer_out, grad_features))
    start_totals = (jnp.zeros((D, 3 * D), jnp.float32), jnp.zeros((D, D), jnp.float32))
    totals, results = lax.scan(group_pass, start_totals, (features, cotangent, key_blocks, key_count))
    factor = 1.0 / math.sqrt(GROUPS * SPAN)
    return (results[0], results[1], totals[0] * factor, totals[1] * factor)
```

```python
from functools import partial

import jax
import jax.numpy as jnp
from jax import lax
from jax.experimental import pallas as pl
from jax.experimental.pallas import tpu as pltpu
from jax.sharding import PartitionSpec as P

H = 8
HD = 64
B = 128
KMAX = 8
NEGATIVE = -1e30
SCALE = HD**-0.5
MESH = pl.DeviceIdType.MESH
BF16 = jnp.bfloat16
F32 = jnp.float32
NN = (((1,), (0,)), ((), ()))
NT = (((1,), (1,)), ((), ()))
TN = (((0,), (0,)), ((), ()))
SIDE = 4


def dot(a, b, dims=NN):
    return lax.dot_general(a, b, dims, preferred_element_type=F32)


def seq_peers(seq):
    y, core = seq // 2, seq % 2
    peers = []
    for dy in (2, 1, 3):
        for flip in (0, 1):
            peers.append(((y + dy) % SIDE) * 2 + (core + flip) % 2)
    peers.append(y * 2 + (core + 1) % 2)
    return peers


def greet(devices):
    barrier = pltpu.get_barrier_semaphore()
    for device in devices:
        pl.semaphore_signal(barrier, inc=1, device_id=device, device_id_type=MESH)
    return lambda: pl.semaphore_wait(barrier, len(devices))


def project_kernel(
    x_ref, g_ref, wi_ref, wo_ref, kv_ref, qg_ref, kvt_ref, qgt_ref, kv_out, qg_out, send_sem, recv_sem
):
    dp, seq = lax.axis_index("dp"), lax.axis_index("seq")
    y, core = seq // 2, seq % 2
    nodes, width = x_ref.shape
    peers = seq_peers(seq)
    ready = greet([(dp, peer) for peer in peers])
    mine = pl.ds(pl.multiple_of(seq * nodes, nodes), nodes)

    def exchange(place, peer):
        copies = []
        for kind, (source, target) in enumerate(((kv_out, kv_ref), (qg_out, qg_ref))):
            copies.append(
                pltpu.make_async_remote_copy(
                    src_ref=source.at[place],
                    dst_ref=target.at[mine, :],
                    send_sem=send_sem.at[place, kind],
                    recv_sem=recv_sem.at[place, kind],
                    device_id=(dp, peer),
                    device_id_type=MESH,
                )
            )
        return copies

    copies = [exchange(place, peer) for place, peer in enumerate(peers)]
    for step, dy in enumerate((2, 1, 3, 0)):
        chip = (y + dy) % SIDE
        first = pl.multiple_of(chip * 2 * HD, 2 * HD)
        weights = jnp.concatenate(
            [wi_ref[:, pl.ds(pl.multiple_of(kind * width + first, 2 * HD), 2 * HD)] for kind in range(3)], 1
        )
        qkv = dot(x_ref[...], weights)
        q = (qkv[:, : 2 * HD] * SCALE).astype(BF16)
        k = qkv[:, 2 * HD : 4 * HD].astype(BF16)
        v = qkv[:, 4 * HD :].astype(BF16)
        g = dot(g_ref[...], wo_ref[pl.ds(first, 2 * HD), :], NT).astype(BF16)
        kv = [jnp.concatenate([k[:, :HD], v[:, :HD]], 1), jnp.concatenate([k[:, HD:], v[:, HD:]], 1)]
        qg = [jnp.concatenate([q[:, :HD], g[:, :HD]], 1), jnp.concatenate([q[:, HD:], g[:, HD:]], 1)]
        if dy:
            for c in (0, 1):
                place = 2 * step + (core + c) % 2
                kv_out[place], qg_out[place] = kv[c], qg[c]
            places = (2 * step, 2 * step + 1)
        else:
            same = core == 0
            kv_ref[mine, :], qg_ref[mine, :] = jnp.where(same, kv[0], kv[1]), jnp.where(same, qg[0], qg[1])
            kv_out[2 * step], qg_out[2 * step] = jnp.where(same, kv[1], kv[0]), jnp.where(same, qg[1], qg[0])
            places = (2 * step,)
        if step == 0:
            ready()
        for place in places:
            for copy in copies[place]:
                copy.start()

    def turn(source):
        here = pl.ds(pl.multiple_of(source * nodes, nodes), nodes)
        kvt_ref[:, here] = kv_ref[here, :].T
        qgt_ref[:, here] = qg_ref[here, :].T

    turn(seq)
    for place in (6, 2, 3, 4, 5, 0, 1):
        dy = (2, 2, 1, 1, 3, 3, 0)[place]
        flip = (0, 1, 0, 1, 0, 1, 1)[place]
        for copy in copies[place]:
            copy.wait_recv()
        turn(((y + SIDE - dy) % SIDE) * 2 + (core + flip) % 2)
    for pair in copies:
        for copy in pair:
            copy.wait_send()


def project(x, g, wi, wo):
    nodes, _ = x.shape
    span = nodes * H
    vm = pl.BlockSpec(memory_space=pltpu.VMEM)
    rows = jax.ShapeDtypeStruct((span, 2 * HD), BF16)
    cols = jax.ShapeDtypeStruct((2 * HD, span), BF16)
    return pl.pallas_call(
        project_kernel,
        out_shape=(rows, rows, cols, cols),
        in_specs=[vm] * 4,
        out_specs=(vm,) * 4,
        scratch_shapes=[
            pltpu.VMEM((H - 1, nodes, 2 * HD), BF16),
            pltpu.VMEM((H - 1, nodes, 2 * HD), BF16),
            pltpu.SemaphoreType.DMA((H - 1, 2)),
            pltpu.SemaphoreType.DMA((H - 1, 2)),
        ],
        compiler_params=pltpu.CompilerParams(collective_id=0, has_side_effects=True, vmem_limit_bytes=48 << 20),
        name="project",
    )(x, g, wi, wo)


def attention_kernel(group, blocks_ref, counts_ref, kv_ref, qg_ref, kvt_ref, qgt_ref, qa_ref, dkv_ref, total_ref):
    block_count = qg_ref.shape[0] // B
    total_ref[...] = jnp.zeros_like(total_ref)
    zero = jnp.zeros((HD, B), BF16)
    lane = lax.broadcasted_iota(jnp.int32, (B, B), 1)

    def query_block(i, live):
        here = pl.ds(pl.multiple_of(i * B, B), B)
        count = counts_ref[i]
        qg, qgt = qg_ref[here, :], qgt_ref[:, here]
        apart = jnp.concatenate(
            [jnp.concatenate([qgt[:HD], zero], 1), jnp.concatenate([zero, qgt[HD:]], 1)], 0
        )
        spots = [pl.ds(pl.multiple_of(blocks_ref[i, j] * B, B), B) for j in range(live)]
        kv = jnp.concatenate([kv_ref[spot, :] for spot in spots], 0)
        both = dot(kv, apart)
        scores = [both[:B, :B]]
        for j in range(1, live):
            scores.append(both[j * B : (j + 1) * B, :B] + jnp.where(j < count, 0.0, NEGATIVE))
        scores = jnp.concatenate(scores, 0)
        grad_probs = both[:, B:]
        raised = jnp.exp(scores - jnp.max(scores, 0, keepdims=True))
        inverse = 1.0 / jnp.sum(raised, 0, keepdims=True)
        row_delta = jnp.sum(raised * grad_probs, 0, keepdims=True) * inverse
        probs = raised * inverse
        weights = probs.astype(BF16)
        grad_scores = (probs * (grad_probs - row_delta)).astype(BF16)
        pair = jnp.concatenate([grad_scores, weights], 1)
        kvt = jnp.concatenate([kvt_ref[:, spot] for spot in spots], 1)
        out = dot(kvt, pair)
        out = jnp.concatenate([out[:HD, :B] * SCALE, out[HD:, B:]], 0)
        qa_ref[here, :] = out.T.astype(BF16)
        nothing = jnp.zeros_like(qg)
        split = jnp.concatenate([jnp.where(lane < HD, qg, nothing), jnp.where(lane < HD, nothing, qg)], 0)
        return spots, dot(pair, split)

    def step(index, carry):
        ids = [index * group + t for t in range(group)]
        most = counts_ref[ids[0]]
        for i in ids[1:]:
            most = jnp.maximum(most, counts_ref[i])
        for live in range(1, KMAX + 1):

            @pl.when(most == live)
            def _():
                for spots, terms in [query_block(i, live) for i in ids]:
                    for j, spot in enumerate(spots):
                        total_ref[spot, :] += terms[j * B : (j + 1) * B]

        return carry

    lax.fori_loop(0, block_count // group, step, 0)
    dkv_ref[...] = total_ref[...].astype(BF16)


def attention(blocks, counts, kv, qg, kvt, qgt):
    vm = pl.BlockSpec(memory_space=pltpu.VMEM)
    sm = pl.BlockSpec(memory_space=pltpu.SMEM)
    out = jax.ShapeDtypeStruct(kv.shape, BF16)
    return pl.pallas_call(
        partial(attention_kernel, 2),
        out_shape=(out, out),
        in_specs=[sm, sm, vm, vm, vm, vm],
        out_specs=(vm, vm),
        scratch_shapes=[pltpu.VMEM(kv.shape, F32)],
        compiler_params=pltpu.CompilerParams(vmem_limit_bytes=48 << 20),
        name="attention",
    )(blocks, counts, kv, qg, kvt, qgt)


ORDERS = (("x", "z", "y"), ("z", "x", "y"), ("y", "z", "x"), ("x", "y", "z"))
ROWS = (256, 64, 16, 16)


def finish_kernel(
    qa_ref, dkv_ref, x_ref, g_ref, wi_ref, wo_ref,
    layer_ref, gradf_ref, sums_ref,
    qa_in, dkv_in, grads, half_out, half_in, quarter_out, quarter_in, part_out, part_in, piece_out, piece_in,
    seq_send, seq_recv, core_send, core_recv, axis_send, axis_recv,
):
    dp, seq = lax.axis_index("dp"), lax.axis_index("seq")
    z, x, y, core = dp // SIDE, dp % SIDE, seq // 2, seq % 2
    place_of = {"x": x, "y": y, "z": z}
    nodes, width = x_ref.shape
    other = (dp, y * 2 + (core + 1) % 2)

    def along(axis, offset):
        if axis == "y":
            return (dp, ((y + offset) % SIDE) * 2 + core)
        if axis == "x":
            return (z * SIDE + (x + offset) % SIDE, seq)
        return (((z + offset) % SIDE) * SIDE + x, seq)

    peers = seq_peers(seq)
    greeted = [(dp, peer) for peer in peers]
    greeted += [along(axis, offset) for axis in ("x", "z") for offset in (1, 2, 3)]
    ready = greet(greeted)

    def remote(source, target, send, recv, device):
        return pltpu.make_async_remote_copy(
            src_ref=source, dst_ref=target, send_sem=send, recv_sem=recv, device_id=device, device_id_type=MESH
        )

    back = []
    for kind, (source, target) in enumerate(((qa_ref, qa_in), (dkv_ref, dkv_in))):
        for place, peer in enumerate(peers):
            rows = pl.ds(pl.multiple_of(peer * nodes, nodes), nodes)
            back.append(
                remote(
                    source.at[rows, :], target.at[seq], seq_send.at[kind, place], seq_recv.at[kind, place], (dp, peer)
                )
            )
    ready()
    for copy in back:
        copy.start()
    started = list(back)
    mine = pl.ds(pl.multiple_of(seq * nodes, nodes), nodes)
    qa_in[seq] = qa_ref[mine, :]
    dkv_in[seq] = dkv_ref[mine, :]
    turned = x_ref[...].T

    def heads(source, second):
        first = HD if second else 0
        return jnp.concatenate([source[head][:, first : first + HD] for head in range(H)], 1)

    def core_rows(c):
        return pl.ds(pl.multiple_of(c * ROWS[0], ROWS[0]), ROWS[0])

    def phase_core(m):
        half_out[m] = grads[m, core_rows(1 - core), :].astype(BF16)
        copy = remote(half_out.at[m], half_in.at[m], core_send.at[m, 0], core_recv.at[m, 0], other)
        copy.start()
        started.append(copy)
        return copy

    def start_axis(m, phase, sources, targets):
        copies = []
        for offset in (2, 1, 3):
            copy = remote(
                sources(offset),
                targets(offset),
                axis_send.at[m, phase, offset - 1],
                axis_recv.at[m, phase, offset - 1],
                along(ORDERS[m][min(phase, 5 - phase)], offset),
            )
            copy.start()
            copies.append(copy)
        started.extend(copies)
        return copies

    def phase_scatter(m, phase, waiting):
        place = place_of[ORDERS[m][phase]] if phase < 3 else None
        for copy in waiting:
            copy.wait_recv()
        if phase == 0:
            total = grads[m, core_rows(core), :] + half_in[m].astype(F32)
        elif phase == 1:
            total = (quarter_out_own[m] + quarter_in[m, 0].astype(F32)) + (
                quarter_in[m, 1].astype(F32) + quarter_in[m, 2].astype(F32)
            )
        elif phase == 2:
            total = (part_out_own[m] + part_in[m, 0].astype(F32)) + (
                part_in[m, 1].astype(F32) + part_in[m, 2].astype(F32)
            )
        else:
            return (piece_out_own[m] + piece_in[m, 0].astype(F32)) + (
                piece_in[m, 1].astype(F32) + piece_in[m, 2].astype(F32)
            )
        if phase == 0:
            grads[m, 0 : ROWS[0], :] = total
            rows = lambda p: pl.ds(pl.multiple_of(p * ROWS[1], ROWS[1]), ROWS[1])
            quarter_out[m] = total.astype(BF16)
            quarter_out_own[m] = grads[m, rows(place), :]
            return start_axis(
                m, 0, lambda o: quarter_out.at[m, rows((place + o) % SIDE), :], lambda o: quarter_in.at[m, o - 1]
            )
        if phase == 1:
            grads[m, 0 : ROWS[1], :] = total
            rows = lambda p: pl.ds(pl.multiple_of(p * ROWS[2], ROWS[2]), ROWS[2])
            part_out[m] = total.astype(BF16)
            part_out_own[m] = grads[m, rows(place), :]
            return start_axis(
                m, 1, lambda o: part_out.at[m, rows((place + o) % SIDE), :], lambda o: part_in.at[m, o - 1]
            )
        grads[m, 0 : ROWS[2], :] = total
        cols = lambda p: pl.ds(pl.multiple_of(p * B, B), B)
        piece_out[m] = total.astype(BF16)
        piece_out_own[m] = grads[m, 0 : ROWS[2], cols(place)]
        return start_axis(
            m, 2, lambda o: piece_out.at[m, :, cols((place + o) % SIDE)], lambda o: piece_in.at[m, o - 1]
        )

    quarter_out_own, part_out_own, piece_out_own = {}, {}, {}

    def spot(m, level):
        a, b, c = (place_of[axis] for axis in ORDERS[m])
        first = core * ROWS[0]
        if level >= 1:
            first = first + a * ROWS[1]
        if level >= 2:
            first = first + b * ROWS[2]
        rows = pl.ds(pl.multiple_of(first, ROWS[2]), ROWS[level])
        return (rows, pl.ds(pl.multiple_of(c * B, B), B)) if level == 3 else (rows, slice(None))

    def phase_gather(m, phase, waiting):
        for copy in waiting:
            copy.wait_recv()
        rows, cols = spot(m, 6 - phase)
        here = sums_ref.at[m, rows, cols]
        if phase < 6:
            return start_axis(m, phase, lambda o: here, lambda o: here)
        copy = remote(here, here, core_send.at[m, 1], core_recv.at[m, 1], other)
        copy.start()
        started.append(copy)
        return [copy]

    def advance(m, phase, waiting):
        if phase < 3:
            return phase_scatter(m, phase, waiting)
        if phase == 3:
            total = phase_scatter(m, 3, waiting)
            rows, cols = spot(m, 3)
            sums_ref[m, rows, cols] = total.astype(BF16)
            return phase_gather(m, 3, [])
        return phase_gather(m, phase, waiting)

    for copy in back[: H - 1]:
        copy.wait_recv()
    attended = heads(qa_in, True)
    grads[0] = dot(attended, g_ref[...], TN)
    waits = {0: [phase_core(0)]}
    grad_query = heads(qa_in, False)
    grads[1] = dot(turned, grad_query)
    waits[1] = [phase_core(1)]
    layer_ref[...] = (x_ref[...].astype(F32) + dot(attended, wo_ref[...])).astype(BF16)
    for m in (0, 1):
        waits[m] = advance(m, 0, waits[m])
    partial_grad = g_ref[...].astype(F32) + dot(grad_query, wi_ref[:, :width], NT)
    for copy in back[H - 1 :]:
        copy.wait_recv()
    grad_keys = heads(dkv_in, False)
    grads[2] = dot(turned, grad_keys)
    waits[2] = [phase_core(2)]
    grad_values = heads(dkv_in, True)
    grads[3] = dot(turned, grad_values)
    waits[3] = [phase_core(3)]
    partial_grad += dot(grad_keys, wi_ref[:, width : 2 * width], NT)
    for m in (2, 3):
        waits[m] = advance(m, 0, waits[m])
    partial_grad += dot(grad_values, wi_ref[:, 2 * width :], NT)
    gradf_ref[...] = partial_grad.astype(BF16)
    for phase in range(1, 7):
        for m in range(4):
            waits[m] = advance(m, phase, waits[m])
    for m in range(4):
        for copy in waits[m]:
            copy.wait_recv()
    for copy in started:
        copy.wait_send()


def finish(qa, dkv, x, g, wi, wo):
    nodes, width = x.shape
    vm = pl.BlockSpec(memory_space=pltpu.VMEM)
    rows = jax.ShapeDtypeStruct((nodes, width), BF16)
    return pl.pallas_call(
        finish_kernel,
        out_shape=(rows, rows, jax.ShapeDtypeStruct((4, width, width), BF16)),
        in_specs=[vm] * 6,
        out_specs=(vm,) * 3,
        scratch_shapes=[
            pltpu.VMEM((H, nodes, 2 * HD), BF16),
            pltpu.VMEM((H, nodes, 2 * HD), BF16),
            pltpu.VMEM((4, width, width), F32),
            pltpu.VMEM((4, ROWS[0], width), BF16),
            pltpu.VMEM((4, ROWS[0], width), BF16),
            pltpu.VMEM((4, ROWS[0], width), BF16),
            pltpu.VMEM((4, 3, ROWS[1], width), BF16),
            pltpu.VMEM((4, ROWS[1], width), BF16),
            pltpu.VMEM((4, 3, ROWS[2], width), BF16),
            pltpu.VMEM((4, ROWS[2], width), BF16),
            pltpu.VMEM((4, 3, ROWS[2], B), BF16),
            pltpu.SemaphoreType.DMA((2, H - 1)),
            pltpu.SemaphoreType.DMA((2, H - 1)),
            pltpu.SemaphoreType.DMA((4, 2)),
            pltpu.SemaphoreType.DMA((4, 2)),
            pltpu.SemaphoreType.DMA((4, 6, 3)),
            pltpu.SemaphoreType.DMA((4, 6, 3)),
        ],
        compiler_params=pltpu.CompilerParams(collective_id=1, has_side_effects=True, vmem_limit_bytes=48 << 20),
        name="finish",
    )(qa, dkv, x, g, wi, wo)


def shards(features, input_weight, output_weight, key_blocks, key_count, cotangent):
    x, g = features[0], cotangent[0]
    kv, qg, kvt, qgt = project(x, g, input_weight, output_weight)
    qa, dkv = attention(key_blocks[0, 0], key_count[0, 0], kv, qg, kvt, qgt)
    layer_out, grad_features, sums = finish(qa, dkv, x, g, input_weight, output_weight)
    factor = 1.0 / (lax.axis_size("dp") * lax.axis_size("seq") * x.shape[0]) ** 0.5
    input_total = jnp.concatenate([sums[1], sums[2], sums[3]], 1).astype(F32) * factor
    return (layer_out[None], grad_features[None], input_total, sums[0].astype(F32) * factor)


def solution(mesh):
    in_specs = (
        P("dp", "seq", None),
        P(),
        P(),
        P("dp", "seq", None, None),
        P("dp", "seq", None),
        P("dp", "seq", None),
    )
    out_specs = (P("dp", "seq", None), P("dp", "seq", None), P(), P())
    return jax.shard_map(shards, mesh=mesh, in_specs=in_specs, out_specs=out_specs, check_vma=False)
```

```python
from functools import partial

import jax
import jax.numpy as jnp
from jax import lax
from jax.experimental import pallas as pl
from jax.experimental.pallas import tpu as pltpu
from jax.sharding import PartitionSpec as P

H = 8
HD = 64
B = 128
KMAX = 8
NEGATIVE = -1e30
SCALE = HD**-0.5
MESH = pl.DeviceIdType.MESH
BF16 = jnp.bfloat16
F32 = jnp.float32
NN = (((1,), (0,)), ((), ()))
NT = (((1,), (1,)), ((), ()))
TN = (((0,), (0,)), ((), ()))
SIDE = 4


def dot(a, b, dims=NN):
    return lax.dot_general(a, b, dims, preferred_element_type=F32)


def seq_peers(seq):
    y, core = seq // 2, seq % 2
    peers = []
    for dy in (2, 1, 3):
        for flip in (0, 1):
            peers.append(((y + dy) % SIDE) * 2 + (core + flip) % 2)
    peers.append(y * 2 + (core + 1) % 2)
    return peers


def greet(devices):
    barrier = pltpu.get_barrier_semaphore()
    for device in devices:
        pl.semaphore_signal(barrier, inc=1, device_id=device, device_id_type=MESH)
    return lambda: pl.semaphore_wait(barrier, len(devices))


def falling_order(counts):
    size = counts.shape[1]
    row = jnp.broadcast_to(counts.astype(F32), (size, size))
    here = lax.broadcasted_iota(jnp.int32, (size, size), 0)
    there = lax.broadcasted_iota(jnp.int32, (size, size), 1)
    column = jnp.sum(jnp.where(here == there, row, 0.0), 1, keepdims=True)
    ahead = (row > column) | ((row == column) & (there < here))
    rank = jnp.sum(jnp.where(ahead, 1.0, 0.0), 1, keepdims=True)
    found = jnp.where(rank == there.astype(F32), here.astype(F32), 0.0)
    return jnp.sum(found, 0, keepdims=True).astype(jnp.int32)


def project_kernel(
    x_ref, g_ref, wi_ref, wo_ref, count_ref,
    kv_ref, qg_ref, kvt_ref, qgt_ref, order_ref,
    kv_out, qg_out, send_sem, recv_sem,
):
    dp, seq = lax.axis_index("dp"), lax.axis_index("seq")
    y, core = seq // 2, seq % 2
    nodes, width = x_ref.shape
    peers = seq_peers(seq)
    ready = greet([(dp, peer) for peer in peers])
    mine = pl.ds(pl.multiple_of(seq * nodes, nodes), nodes)

    def exchange(place, peer):
        copies = []
        for kind, (source, target) in enumerate(((kv_out, kv_ref), (qg_out, qg_ref))):
            copies.append(
                pltpu.make_async_remote_copy(
                    src_ref=source.at[place],
                    dst_ref=target.at[mine, :],
                    send_sem=send_sem.at[place, kind],
                    recv_sem=recv_sem.at[place, kind],
                    device_id=(dp, peer),
                    device_id_type=MESH,
                )
            )
        return copies

    copies = [exchange(place, peer) for place, peer in enumerate(peers)]
    for step, dy in enumerate((2, 1, 3, 0)):
        chip = (y + dy) % SIDE
        first = pl.multiple_of(chip * 2 * HD, 2 * HD)
        weights = jnp.concatenate(
            [wi_ref[:, pl.ds(pl.multiple_of(kind * width + first, 2 * HD), 2 * HD)] for kind in range(3)], 1
        )
        qkv = dot(x_ref[...], weights)
        q = (qkv[:, : 2 * HD] * SCALE).astype(BF16)
        k = qkv[:, 2 * HD : 4 * HD].astype(BF16)
        v = qkv[:, 4 * HD :].astype(BF16)
        g = dot(g_ref[...], wo_ref[pl.ds(first, 2 * HD), :], NT).astype(BF16)
        kv = [jnp.concatenate([k[:, :HD], v[:, :HD]], 1), jnp.concatenate([k[:, HD:], v[:, HD:]], 1)]
        qg = [jnp.concatenate([q[:, :HD], g[:, :HD]], 1), jnp.concatenate([q[:, HD:], g[:, HD:]], 1)]
        if dy:
            for c in (0, 1):
                place = 2 * step + (core + c) % 2
                kv_out[place], qg_out[place] = kv[c], qg[c]
            places = (2 * step, 2 * step + 1)
        else:
            same = core == 0
            kv_ref[mine, :], qg_ref[mine, :] = jnp.where(same, kv[0], kv[1]), jnp.where(same, qg[0], qg[1])
            kv_out[2 * step], qg_out[2 * step] = jnp.where(same, kv[1], kv[0]), jnp.where(same, qg[1], qg[0])
            places = (2 * step,)
        if step == 0:
            ready()
        for place in places:
            for copy in copies[place]:
                copy.start()

    def turn(source):
        here = pl.ds(pl.multiple_of(source * nodes, nodes), nodes)
        kvt_ref[:, here] = kv_ref[here, :].T
        qgt_ref[:, here] = qg_ref[here, :].T

    turn(seq)
    order_ref[...] = falling_order(count_ref[...])
    for place in (6, 2, 3, 4, 5, 0, 1):
        dy = (2, 2, 1, 1, 3, 3, 0)[place]
        flip = (0, 1, 0, 1, 0, 1, 1)[place]
        for copy in copies[place]:
            copy.wait_recv()
        turn(((y + SIDE - dy) % SIDE) * 2 + (core + flip) % 2)
    for pair in copies:
        for copy in pair:
            copy.wait_send()


def project(x, g, wi, wo, counts):
    nodes, _ = x.shape
    span = nodes * H
    vm = pl.BlockSpec(memory_space=pltpu.VMEM)
    rows = jax.ShapeDtypeStruct((span, 2 * HD), BF16)
    cols = jax.ShapeDtypeStruct((2 * HD, span), BF16)
    return pl.pallas_call(
        project_kernel,
        out_shape=(rows, rows, cols, cols, jax.ShapeDtypeStruct(counts.shape, jnp.int32)),
        in_specs=[vm] * 5,
        out_specs=(vm,) * 5,
        scratch_shapes=[
            pltpu.VMEM((H - 1, nodes, 2 * HD), BF16),
            pltpu.VMEM((H - 1, nodes, 2 * HD), BF16),
            pltpu.SemaphoreType.DMA((H - 1, 2)),
            pltpu.SemaphoreType.DMA((H - 1, 2)),
        ],
        compiler_params=pltpu.CompilerParams(collective_id=0, has_side_effects=True, vmem_limit_bytes=48 << 20),
        name="project",
    )(x, g, wi, wo, counts)


def attention_kernel(
    group, order_ref, blocks_ref, counts_ref, kv_ref, qg_ref, kvt_ref, qgt_ref, qa_ref, dkv_ref, total_ref
):
    block_count = qg_ref.shape[0] // B
    total_ref[...] = jnp.zeros_like(total_ref)
    zero = jnp.zeros((HD, B), BF16)
    lane = lax.broadcasted_iota(jnp.int32, (B, B), 1)

    def query_blocks(ids, live):
        heres = [pl.ds(pl.multiple_of(i * B, B), B) for i in ids]
        spots = [[pl.ds(pl.multiple_of(blocks_ref[i, j] * B, B), B) for j in range(live)] for i in ids]
        products = []
        for here, chosen in zip(heres, spots):
            qgt = qgt_ref[:, here]
            apart = jnp.concatenate(
                [jnp.concatenate([qgt[:HD], zero], 1), jnp.concatenate([zero, qgt[HD:]], 1)], 0
            )
            products.append(dot(jnp.concatenate([kv_ref[spot, :] for spot in chosen], 0), apart))
        pairs = []
        for i, product in zip(ids, products):
            count = counts_ref[i]
            scores = [product[:B, :B]]
            for j in range(1, live):
                scores.append(product[j * B : (j + 1) * B, :B] + jnp.where(j < count, 0.0, NEGATIVE))
            scores = jnp.concatenate(scores, 0)
            grad_probs = product[:, B:]
            raised = jnp.exp(scores - jnp.max(scores, 0, keepdims=True))
            inverse = 1.0 / jnp.sum(raised, 0, keepdims=True)
            row_delta = jnp.sum(raised * grad_probs, 0, keepdims=True) * inverse
            probs = raised * inverse
            grad_scores = (probs * (grad_probs - row_delta)).astype(BF16)
            pairs.append(jnp.concatenate([grad_scores, probs.astype(BF16)], 1))
        outs = []
        for chosen, pair in zip(spots, pairs):
            outs.append(dot(jnp.concatenate([kvt_ref[:, spot] for spot in chosen], 1), pair))
        terms = []
        for here, pair in zip(heres, pairs):
            qg = qg_ref[here, :]
            nothing = jnp.zeros_like(qg)
            split = jnp.concatenate([jnp.where(lane < HD, qg, nothing), jnp.where(lane < HD, nothing, qg)], 0)
            terms.append(dot(pair, split))
        for here, out in zip(heres, outs):
            both = jnp.concatenate([out[:HD, :B] * SCALE, out[HD:, B:]], 0)
            qa_ref[here, :] = both.T.astype(BF16)
        for chosen, term in zip(spots, terms):
            for j, spot in enumerate(chosen):
                total_ref[spot, :] += term[j * B : (j + 1) * B]

    def step(index, carry):
        ids = [order_ref[0, index * group + t] for t in range(group)]
        most = counts_ref[ids[0]]
        for live in range(1, KMAX + 1):
            pl.when(most == live)(partial(query_blocks, ids, live))
        return carry

    lax.fori_loop(0, block_count // group, step, 0)
    dkv_ref[...] = total_ref[...].astype(BF16)


def attention(order, blocks, counts, kv, qg, kvt, qgt):
    vm = pl.BlockSpec(memory_space=pltpu.VMEM)
    sm = pl.BlockSpec(memory_space=pltpu.SMEM)
    out = jax.ShapeDtypeStruct(kv.shape, BF16)
    return pl.pallas_call(
        partial(attention_kernel, 4),
        out_shape=(out, out),
        in_specs=[sm, sm, sm, vm, vm, vm, vm],
        out_specs=(vm, vm),
        scratch_shapes=[pltpu.VMEM(kv.shape, F32)],
        compiler_params=pltpu.CompilerParams(vmem_limit_bytes=56 << 20),
        name="attention",
    )(order, blocks, counts, kv, qg, kvt, qgt)


ORDERS = (("x", "z", "y"), ("z", "x", "y"), ("y", "z", "x"), ("x", "y", "z"))
ROWS = (256, 64, 16)


def finish_kernel(
    qa_ref, dkv_ref, x_ref, g_ref, wi_ref, wo_ref,
    layer_ref, gradf_ref, osum_ref, isum_ref,
    qa_in, dkv_in, grads, half_out, half_in, quarter_out, quarter_in, part_out, part_in, piece_out, piece_in,
    seq_send, seq_recv, core_send, core_recv, axis_send, axis_recv,
):
    dp, seq = lax.axis_index("dp"), lax.axis_index("seq")
    z, x, y, core = dp // SIDE, dp % SIDE, seq // 2, seq % 2
    place_of = {"x": x, "y": y, "z": z}
    nodes, width = x_ref.shape
    other = (dp, y * 2 + (core + 1) % 2)

    def along(axis, offset):
        if axis == "y":
            return (dp, ((y + offset) % SIDE) * 2 + core)
        if axis == "x":
            return (z * SIDE + (x + offset) % SIDE, seq)
        return (((z + offset) % SIDE) * SIDE + x, seq)

    peers = seq_peers(seq)
    greeted = [(dp, peer) for peer in peers]
    greeted += [along(axis, offset) for axis in ("x", "z") for offset in (1, 2, 3)]
    ready = greet(greeted)

    def remote(source, target, send, recv, device):
        return pltpu.make_async_remote_copy(
            src_ref=source, dst_ref=target, send_sem=send, recv_sem=recv, device_id=device, device_id_type=MESH
        )

    back = []
    for kind, (source, target) in enumerate(((qa_ref, qa_in), (dkv_ref, dkv_in))):
        for place, peer in enumerate(peers):
            rows = pl.ds(pl.multiple_of(peer * nodes, nodes), nodes)
            back.append(
                remote(
                    source.at[rows, :], target.at[seq], seq_send.at[kind, place], seq_recv.at[kind, place], (dp, peer)
                )
            )
    ready()
    for copy in back:
        copy.start()
    started = list(back)
    mine = pl.ds(pl.multiple_of(seq * nodes, nodes), nodes)
    qa_in[seq] = qa_ref[mine, :]
    dkv_in[seq] = dkv_ref[mine, :]
    turned = x_ref[...].T

    def heads(source, second):
        first = HD if second else 0
        return jnp.concatenate([source[head][:, first : first + HD] for head in range(H)], 1)

    def core_rows(c):
        return pl.ds(pl.multiple_of(c * ROWS[0], ROWS[0]), ROWS[0])

    def phase_core(m):
        half_out[m] = grads[m, core_rows(1 - core), :].astype(BF16)
        copy = remote(half_out.at[m], half_in.at[m], core_send.at[m, 0], core_recv.at[m, 0], other)
        copy.start()
        started.append(copy)
        return copy

    def start_axis(m, phase, level, sources, targets):
        copies = []
        for offset in (2, 1, 3):
            copy = remote(
                sources(offset),
                targets(offset),
                axis_send.at[m, phase, offset - 1],
                axis_recv.at[m, phase, offset - 1],
                along(ORDERS[m][level], offset),
            )
            copy.start()
            copies.append(copy)
        started.extend(copies)
        return copies

    def phase_scatter(m, phase, waiting):
        place = place_of[ORDERS[m][phase]] if phase < 3 else None
        for copy in waiting:
            copy.wait_recv()
        if phase == 0:
            total = grads[m, core_rows(core), :] + half_in[m].astype(F32)
        elif phase == 1:
            total = (quarter_out_own[m] + quarter_in[m, 0].astype(F32)) + (
                quarter_in[m, 1].astype(F32) + quarter_in[m, 2].astype(F32)
            )
        elif phase == 2:
            total = (part_out_own[m] + part_in[m, 0].astype(F32)) + (
                part_in[m, 1].astype(F32) + part_in[m, 2].astype(F32)
            )
        else:
            return (piece_in[m, 0].astype(F32) + piece_in[m, 1].astype(F32)) + (
                piece_in[m, 2].astype(F32) + piece_in[m, 3].astype(F32)
            )
        if phase == 0:
            grads[m, 0 : ROWS[0], :] = total
            rows = lambda p: pl.ds(pl.multiple_of(p * ROWS[1], ROWS[1]), ROWS[1])
            quarter_out[m] = total.astype(BF16)
            quarter_out_own[m] = grads[m, rows(place), :]
            return start_axis(
                m, 0, 0, lambda o: quarter_out.at[m, rows((place + o) % SIDE), :], lambda o: quarter_in.at[m, o - 1]
            )
        if phase == 1:
            grads[m, 0 : ROWS[1], :] = total
            rows = lambda p: pl.ds(pl.multiple_of(p * ROWS[2], ROWS[2]), ROWS[2])
            part_out[m] = total.astype(BF16)
            part_out_own[m] = grads[m, rows(place), :]
            return start_axis(
                m, 1, 1, lambda o: part_out.at[m, rows((place + o) % SIDE), :], lambda o: part_in.at[m, o - 1]
            )
        piece_out[m] = total.astype(BF16)
        piece_in[m, place] = total.astype(BF16)
        return start_axis(m, 2, 2, lambda o: piece_out.at[m], lambda o: piece_in.at[m, place])

    quarter_out_own, part_out_own = {}, {}

    def region(m, level):
        a, b = (place_of[axis] for axis in ORDERS[m][:2])
        first = core * ROWS[0]
        if level >= 1:
            first = first + a * ROWS[1]
        if level >= 2:
            first = first + b * ROWS[2]
        rows = pl.ds(pl.multiple_of(first, ROWS[2]), ROWS[level])
        return osum_ref.at[rows, :] if m == 0 else isum_ref.at[rows, pl.ds((m - 1) * width, width)]

    def phase_gather(m, phase, waiting):
        for copy in waiting:
            copy.wait_recv()
        here = region(m, 5 - phase)
        if phase < 5:
            return start_axis(m, phase, 4 - phase, lambda o: here, lambda o: here)
        copy = remote(here, here, core_send.at[m, 1], core_recv.at[m, 1], other)
        copy.start()
        started.append(copy)
        return [copy]

    def advance(m, phase, waiting):
        if phase < 3:
            return phase_scatter(m, phase, waiting)
        if phase == 3:
            total = phase_scatter(m, 3, waiting)
            region(m, 2)[...] = total.astype(BF16)
            waiting = []
        return phase_gather(m, phase, waiting)

    for copy in back[: H - 1]:
        copy.wait_recv()
    attended = heads(qa_in, True)
    grads[0] = dot(attended, g_ref[...], TN)
    waits = {0: [phase_core(0)]}
    grad_query = heads(qa_in, False)
    grads[1] = dot(turned, grad_query)
    waits[1] = [phase_core(1)]
    layer_ref[...] = (x_ref[...].astype(F32) + dot(attended, wo_ref[...])).astype(BF16)
    for m in (0, 1):
        waits[m] = advance(m, 0, waits[m])
    for phase in (1, 2):
        for m in (0, 1):
            waits[m] = advance(m, phase, waits[m])
    partial_grad = g_ref[...].astype(F32) + dot(grad_query, wi_ref[:, :width], NT)
    for copy in back[H - 1 :]:
        copy.wait_recv()
    grad_keys = heads(dkv_in, False)
    grads[2] = dot(turned, grad_keys)
    waits[2] = [phase_core(2)]
    grad_values = heads(dkv_in, True)
    grads[3] = dot(turned, grad_values)
    waits[3] = [phase_core(3)]
    for m in (0, 1):
        waits[m] = advance(m, 3, waits[m])
    for m in (2, 3):
        waits[m] = advance(m, 0, waits[m])
    partial_grad += dot(grad_keys, wi_ref[:, width : 2 * width], NT)
    partial_grad += dot(grad_values, wi_ref[:, 2 * width :], NT)
    gradf_ref[...] = partial_grad.astype(BF16)
    for phase in range(1, 6):
        for m in (2, 3):
            waits[m] = advance(m, phase, waits[m])
        if phase in (1, 2):
            for m in (0, 1):
                waits[m] = advance(m, phase + 3, waits[m])
    for m in range(4):
        for copy in waits[m]:
            copy.wait_recv()
    for copy in started:
        copy.wait_send()


def finish(qa, dkv, x, g, wi, wo):
    nodes, width = x.shape
    vm = pl.BlockSpec(memory_space=pltpu.VMEM)
    rows = jax.ShapeDtypeStruct((nodes, width), BF16)
    return pl.pallas_call(
        finish_kernel,
        out_shape=(
            rows,
            rows,
            jax.ShapeDtypeStruct((width, width), BF16),
            jax.ShapeDtypeStruct((width, 3 * width), BF16),
        ),
        in_specs=[vm] * 6,
        out_specs=(vm,) * 4,
        scratch_shapes=[
            pltpu.VMEM((H, nodes, 2 * HD), BF16),
            pltpu.VMEM((H, nodes, 2 * HD), BF16),
            pltpu.VMEM((4, width, width), F32),
            pltpu.VMEM((4, ROWS[0], width), BF16),
            pltpu.VMEM((4, ROWS[0], width), BF16),
            pltpu.VMEM((4, ROWS[0], width), BF16),
            pltpu.VMEM((4, 3, ROWS[1], width), BF16),
            pltpu.VMEM((4, ROWS[1], width), BF16),
            pltpu.VMEM((4, 3, ROWS[2], width), BF16),
            pltpu.VMEM((4, ROWS[2], width), BF16),
            pltpu.VMEM((4, SIDE, ROWS[2], width), BF16),
            pltpu.SemaphoreType.DMA((2, H - 1)),
            pltpu.SemaphoreType.DMA((2, H - 1)),
            pltpu.SemaphoreType.DMA((4, 2)),
            pltpu.SemaphoreType.DMA((4, 2)),
            pltpu.SemaphoreType.DMA((4, 5, 3)),
            pltpu.SemaphoreType.DMA((4, 5, 3)),
        ],
        compiler_params=pltpu.CompilerParams(collective_id=1, has_side_effects=True, vmem_limit_bytes=48 << 20),
        name="finish",
    )(qa, dkv, x, g, wi, wo)


def shards(features, input_weight, output_weight, key_blocks, key_count, cotangent):
    x, g = features[0], cotangent[0]
    kv, qg, kvt, qgt, order = project(x, g, input_weight, output_weight, key_count[0])
    qa, dkv = attention(order, key_blocks[0, 0], key_count[0, 0], kv, qg, kvt, qgt)
    layer_out, grad_features, osum, isum = finish(qa, dkv, x, g, input_weight, output_weight)
    factor = 1.0 / (lax.axis_size("dp") * lax.axis_size("seq") * x.shape[0]) ** 0.5
    return (layer_out[None], grad_features[None], isum.astype(F32) * factor, osum.astype(F32) * factor)


def solution(mesh):
    in_specs = (
        P("dp", "seq", None),
        P(),
        P(),
        P("dp", "seq", None, None),
        P("dp", "seq", None),
        P("dp", "seq", None),
    )
    out_specs = (P("dp", "seq", None), P("dp", "seq", None), P(), P())
    return jax.shard_map(shards, mesh=mesh, in_specs=in_specs, out_specs=out_specs, check_vma=False)
```

```python
from functools import partial

import jax
import jax.numpy as jnp
from jax import lax
from jax.experimental import pallas as pl
from jax.experimental.pallas import tpu as pltpu
from jax.sharding import PartitionSpec as P

H = 8
HD = 64
B = 128
KMAX = 8
NEGATIVE = -1e30
SCALE = HD**-0.5
MESH = pl.DeviceIdType.MESH
BF16 = jnp.bfloat16
F32 = jnp.float32
NN = (((1,), (0,)), ((), ()))
NT = (((1,), (1,)), ((), ()))
TN = (((0,), (0,)), ((), ()))
SIDE = 4
VMEM_BYTES = 60 << 20


def dot(a, b, dims=NN):
    return lax.dot_general(a, b, dims, preferred_element_type=F32)


def part(index, size):
    return pl.ds(pl.multiple_of(index * size, size), size)


def seq_peers(seq):
    y, core = seq // 2, seq % 2
    peers = []
    for dy in (2, 1, 3):
        for flip in (0, 1):
            peers.append(((y + dy) % SIDE) * 2 + (core + flip) % 2)
    peers.append(y * 2 + (core + 1) % 2)
    return peers


def greet(devices):
    barrier = pltpu.get_barrier_semaphore()
    for device in devices:
        pl.semaphore_signal(barrier, inc=1, device_id=device, device_id_type=MESH)
    pl.semaphore_wait(barrier, len(devices))


def remote(source, target, sems, index, device):
    return pltpu.make_async_remote_copy(
        src_ref=source,
        dst_ref=target,
        send_sem=sems[0].at[index],
        recv_sem=sems[1].at[index],
        device_id=device,
        device_id_type=MESH,
    )


def falling_order(counts):
    size = counts.shape[1]
    row = jnp.broadcast_to(counts.astype(F32), (size, size))
    here = lax.broadcasted_iota(jnp.int32, (size, size), 0)
    there = lax.broadcasted_iota(jnp.int32, (size, size), 1)
    column = jnp.sum(jnp.where(here == there, row, 0.0), 1, keepdims=True)
    ahead = (row > column) | ((row == column) & (there < here))
    rank = jnp.sum(jnp.where(ahead, 1.0, 0.0), 1, keepdims=True)
    found = jnp.where(rank == there.astype(F32), here.astype(F32), 0.0)
    return jnp.sum(found, 0, keepdims=True).astype(jnp.int32)


def project_kernel(
    x_hbm, g_hbm, wi_hbm, wo_hbm, count_ref,
    kv_ref, kvt_ref, qgt_ref, order_ref, all_hbm,
    x_ref, g_ref, wi_ref, wo_ref, gt_ref, send_sem, recv_sem, load_sem, store_sem,
):
    dp, seq = lax.axis_index("dp"), lax.axis_index("seq")
    y, core = seq // 2, seq % 2
    nodes, width = g_ref.shape
    half = nodes // 2
    sems = (send_sem, recv_sem)
    other = (dp, y * 2 + (core + 1) % 2)

    def at(dy, flip=0):
        return ((y + dy) % SIDE) * 2 + (core + flip) % 2

    loads = [
        pltpu.make_async_copy(source, target, load_sem.at[k])
        for k, (source, target) in enumerate(
            ((x_hbm, x_ref.at[seq]), (g_hbm, g_ref), (wi_hbm, wi_ref), (wo_hbm, wo_ref))
        )
    ]
    for load in loads:
        load.start()
    peers = seq_peers(seq)
    greet([(dp, peer) for peer in peers])
    up, down = (dp, at(1)), (dp, at(3))

    def rows(h):
        return pl.ds(h * half, half)

    def pass_on(source, h, index, device):
        piece = x_ref.at[source, rows(h)]
        return remote(piece, piece, sems, index, device)

    def own(h, index, device):
        return remote(x_hbm.at[rows(h)], x_ref.at[seq, rows(h)], sems, index, device)

    sent = [own(0, 0, up), own(1, 3, down), own(1, 1, up), own(0, 4, down), own(0, 6, other), own(1, 7, other)]
    for copy in sent:
        copy.start()

    loads[1].wait()
    loads[3].wait()
    gt_ref[...] = dot(wo_ref[...], g_ref[...], NT).astype(BF16)
    head_rows = pl.ds(HD, HD)
    given = []
    for place, peer in enumerate(peers):
        given.append(
            remote(gt_ref.at[part(peer, HD), :], qgt_ref.at[head_rows, part(seq, nodes)], sems, 14 + place, (dp, peer))
        )
        given[-1].start()
    qgt_ref[head_rows, part(seq, nodes)] = gt_ref[part(seq, HD), :]
    loads[2].wait()
    loads[0].wait()
    chosen = []
    for kind in (1, 2, 0):
        block = wi_ref[:, pl.ds(pl.multiple_of(kind * width + y * 2 * HD, 2 * HD), 2 * HD)]
        chosen.append(jnp.where(core == 0, block[:, :HD], block[:, HD:]))
    chosen[2] = chosen[2] * jnp.asarray(SCALE, BF16)
    weights = jnp.concatenate(chosen + [jnp.zeros_like(chosen[0])], 1)
    stores = []

    def project_half(source, h):
        place = 2 * source + h
        here = part(place, half)
        product = dot(x_ref[source, rows(h), :], weights)
        kv = product[:, : 2 * HD].astype(BF16)
        kv_ref[here, :] = kv
        kvt_ref[:, here] = kv.T
        qgt_ref[:HD, here] = product[:, 2 * HD :].T[:HD].astype(BF16)
        store = pltpu.make_async_copy(x_ref.at[source, rows(h)], all_hbm.at[here, :], store_sem.at[len(stores)])
        store.start()
        stores.append(store)

    project_half(seq, 0)
    project_half(seq, 1)
    order_ref[...] = falling_order(count_ref[...])
    low, high, far = at(3), at(1), at(2)
    forwards = {0: pass_on(low, 0, 2, up), 3: pass_on(high, 1, 5, down)}
    shares = {0: (low, 0, 8), 3: (high, 1, 9), 1: (low, 1, 10), 4: (high, 0, 11), 2: (far, 0, 12), 5: (far, 1, 13)}
    ring = {index: own(0, index, up) for index in (0, 1, 2, 3, 4, 5)}
    near = {index: own(0, index, other) for index in range(6, 14)}

    def arrive(index):
        ring[index].wait_recv()
        source, h, share = shares[index]
        for copy in [forwards[index]] if index in forwards else []:
            copy.start()
            sent.append(copy)
        sent.append(pass_on(source, h, share, other))
        sent[-1].start()
        project_half(source, h)

    def arrive_near(share, source, h):
        near[share].wait_recv()
        project_half(source, h)

    arrive_near(6, at(0, 1), 0)
    arrive_near(7, at(0, 1), 1)
    arrive(0)
    arrive(3)
    arrive_near(8, at(3, 1), 0)
    arrive_near(9, at(1, 1), 1)
    arrive(1)
    arrive(4)
    arrive_near(10, at(3, 1), 1)
    arrive_near(11, at(1, 1), 0)
    arrive(2)
    arrive(5)
    arrive_near(12, at(2, 1), 0)
    arrive_near(13, at(2, 1), 1)
    for copy in given:
        copy.wait_recv()
    for copy in sent + given:
        copy.wait_send()
    for store in stores:
        store.wait()


def project(x, g, wi, wo, counts):
    nodes, width = x.shape
    span = nodes * H
    vm = pl.BlockSpec(memory_space=pltpu.VMEM)
    anywhere = pl.BlockSpec(memory_space=pl.ANY)
    cols = jax.ShapeDtypeStruct((2 * HD, span), BF16)
    return pl.pallas_call(
        project_kernel,
        out_shape=(
            jax.ShapeDtypeStruct((span, 2 * HD), BF16),
            cols,
            cols,
            jax.ShapeDtypeStruct(counts.shape, jnp.int32),
            jax.ShapeDtypeStruct((span, width), BF16),
        ),
        in_specs=[anywhere] * 4 + [vm],
        out_specs=(vm,) * 4 + (anywhere,),
        scratch_shapes=[
            pltpu.VMEM((H, nodes, width), BF16),
            pltpu.VMEM(g.shape, BF16),
            pltpu.VMEM(wi.shape, BF16),
            pltpu.VMEM(wo.shape, BF16),
            pltpu.VMEM((width, nodes), BF16),
            pltpu.SemaphoreType.DMA((21,)),
            pltpu.SemaphoreType.DMA((21,)),
            pltpu.SemaphoreType.DMA((4,)),
            pltpu.SemaphoreType.DMA((2 * H,)),
        ],
        compiler_params=pltpu.CompilerParams(collective_id=0, has_side_effects=True, vmem_limit_bytes=VMEM_BYTES),
        name="project",
    )(x, g, wi, wo, counts)


def attention_kernel(
    group, order_ref, blocks_ref, counts_ref, kv_ref, kvt_ref, qgt_ref, all_hbm, grads_ref, weight_ref,
    total_ref, all_ref, load_sem,
):
    block_count = kvt_ref.shape[1] // B
    load = pltpu.make_async_copy(all_hbm, all_ref, load_sem)
    load.start()
    total_ref[...] = jnp.zeros_like(total_ref)
    zero = jnp.zeros((HD, B), BF16)

    def query_blocks(ids, live):
        heres = [pl.ds(pl.multiple_of(i * B, B), B) for i in ids]
        spots = [[pl.ds(pl.multiple_of(blocks_ref[i, j] * B, B), B) for j in range(live)] for i in ids]
        aparts, products = [], []
        for here, chosen in zip(heres, spots):
            qgt = qgt_ref[:, here]
            apart = jnp.concatenate(
                [jnp.concatenate([qgt[:HD], zero], 1), jnp.concatenate([zero, qgt[HD:]], 1)], 0
            )
            aparts.append(apart)
            products.append(dot(jnp.concatenate([kv_ref[spot, :] for spot in chosen], 0), apart))
        pairs = []
        for i, product in zip(ids, products):
            count = counts_ref[i]
            scores = [product[:B, :B]]
            for j in range(1, live):
                scores.append(product[j * B : (j + 1) * B, :B] + jnp.where(j < count, 0.0, NEGATIVE))
            scores = jnp.concatenate(scores, 0)
            grad_probs = product[:, B:]
            raised = jnp.exp(scores - jnp.max(scores, 0, keepdims=True))
            inverse = 1.0 / jnp.sum(raised, 0, keepdims=True)
            row_delta = jnp.sum(raised * grad_probs, 0, keepdims=True) * inverse
            probs = raised * inverse
            grad_scores = (probs * (grad_probs - row_delta)).astype(BF16)
            pairs.append(jnp.concatenate([grad_scores, probs.astype(BF16)], 1))
        outs = []
        for chosen, pair in zip(spots, pairs):
            outs.append(dot(jnp.concatenate([kvt_ref[:, spot] for spot in chosen], 1), pair))
        terms = []
        for apart, pair in zip(aparts, pairs):
            terms.append(dot(apart, pair, NT))
        for here, out in zip(heres, outs):
            grads_ref[0:HD, here] = out[HD:, B:].astype(BF16)
            grads_ref[HD : 2 * HD, here] = (out[:HD, :B] * SCALE).astype(BF16)
        for chosen, term in zip(spots, terms):
            for j, spot in enumerate(chosen):
                total_ref[:, spot] += term[:, j * B : (j + 1) * B]

    def step(index, carry):
        ids = [order_ref[0, index * group + t] for t in range(group)]
        most = counts_ref[ids[0]]
        for live in range(1, KMAX + 1):
            pl.when(most == live)(partial(query_blocks, ids, live))
        return carry

    lax.fori_loop(0, block_count // group, step, 0)
    grads_ref[2 * HD :, :] = total_ref[...].astype(BF16)
    load.wait()
    weight_ref[...] = dot(grads_ref[HD:, :], all_ref[...])


def attention(order, blocks, counts, kv, kvt, qgt, everything):
    span, width = everything.shape
    vm = pl.BlockSpec(memory_space=pltpu.VMEM)
    sm = pl.BlockSpec(memory_space=pltpu.SMEM)
    return pl.pallas_call(
        partial(attention_kernel, 4),
        out_shape=(jax.ShapeDtypeStruct((4 * HD, span), BF16), jax.ShapeDtypeStruct((3 * HD, width), F32)),
        in_specs=[sm, sm, sm, vm, vm, vm, pl.BlockSpec(memory_space=pl.ANY)],
        out_specs=(vm, vm),
        scratch_shapes=[
            pltpu.VMEM((2 * HD, span), F32),
            pltpu.VMEM(everything.shape, BF16),
            pltpu.SemaphoreType.DMA,
        ],
        compiler_params=pltpu.CompilerParams(vmem_limit_bytes=VMEM_BYTES),
        name="attention",
    )(order, blocks, counts, kv, kvt, qgt, everything)


ROWS = (256, 64, 16)


class Sum:
    def __init__(self, number, axes, columns, whole, sems, scratch, along, place_of, core):
        self.number, self.axes, self.columns, self.whole, self.sems = number, axes, columns, whole, sems
        self.total, self.out, self.quarters, self.parts, self.levels = scratch
        self.along = along
        self.place = [place_of[axis] for axis in axes]
        self.core = core
        self.waiting, self.sent = [], []

    def send(self, phase, axis, source, target):
        self.waiting = []
        for offset in (2, 1, 3):
            copy = remote(
                source(offset), target(offset), self.sems, (self.number, phase, offset - 1), self.along(axis, offset)
            )
            copy.start()
            self.waiting.append(copy)
        self.sent += self.waiting

    def arrive(self):
        for copy in self.waiting:
            copy.wait_recv()

    def scatter_first(self, value):
        self.total[...] = value
        self.out[0 : ROWS[0], :] = value.astype(BF16)
        spot = lambda offset: part((self.place[0] + offset) % SIDE, ROWS[1])
        self.send(
            0, self.axes[0], lambda o: self.out.at[spot(o), :], lambda o: self.quarters.at[o - 1]
        )

    def scatter_second(self):
        self.arrive()
        value = self.total[part(self.place[0], ROWS[1]), :] + self.quarters[0].astype(F32)
        value += self.quarters[1].astype(F32) + self.quarters[2].astype(F32)
        self.total[0 : ROWS[1], :] = value
        self.out[ROWS[0] :, :] = value.astype(BF16)
        spot = lambda offset: part(ROWS[0] // ROWS[2] + (self.place[1] + offset) % SIDE, ROWS[2])
        self.send(1, self.axes[1], lambda o: self.out.at[spot(o), :], lambda o: self.parts.at[o - 1])

    def scattered(self):
        self.arrive()
        value = self.total[part(self.place[1], ROWS[2]), :] + self.parts[0].astype(F32)
        return (value + (self.parts[1].astype(F32) + self.parts[2].astype(F32))).astype(BF16)

    def exchange(self, axis, place):
        self.levels[place] = self.scattered()
        here = self.levels.at[place]
        self.send(2, axis, lambda o: here, lambda o: here)

    def exchanged(self):
        self.arrive()
        value = [self.levels[k].astype(F32) for k in range(SIDE)]
        self.region(2)[...] = ((value[0] + value[1]) + (value[2] + value[3])).astype(BF16)

    def region(self, level, columns=None):
        first = self.core * ROWS[0]
        if level >= 1:
            first = first + self.place[0] * ROWS[1]
        if level >= 2:
            first = first + self.place[1] * ROWS[2]
        rows = pl.ds(pl.multiple_of(first, ROWS[2]), ROWS[level])
        return self.whole.at[rows, self.columns if columns is None else columns]

    def gather(self, step):
        here = self.region(2 - step)
        self.send(3 + step, self.axes[1 - step], lambda o: here, lambda o: here)


def finish_kernel(
    grads_hbm, weight_hbm, x_hbm, g_hbm, wi_hbm, wo_hbm,
    layer_ref, gradf_ref, osum_ref, isum_ref,
    x_ref, g_ref, wi_ref, wo_ref, attended_ref, rows_ref, merged_ref, theirs_ref, half_ref, total_ref,
    tot_a, tot_b, tot_c, tot_d, out_a, out_b, out_c, out_d, quarters_a, quarters_b, quarters_c, quarters_d,
    parts_a, parts_b, parts_c, parts_d, levels_c, levels_d,
    seq_send, seq_recv, core_send, core_recv, sum_send, sum_recv, spread_send, spread_recv, load_sem,
):
    dp, seq = lax.axis_index("dp"), lax.axis_index("seq")
    z, x, y, core = dp // SIDE, dp % SIDE, seq // 2, seq % 2
    place_of = {"x": x, "y": y, "z": z}
    nodes, width = x_ref.shape
    half = nodes // 2
    other = (dp, y * 2 + (core + 1) % 2)
    seq_sems, core_sems = (seq_send, seq_recv), (core_send, core_recv)

    def along(axis, offset):
        if axis == "y":
            return (dp, ((y + offset) % SIDE) * 2 + core)
        if axis == "x":
            return (z * SIDE + (x + offset) % SIDE, seq)
        return (((z + offset) % SIDE) * SIDE + x, seq)

    loads = [
        pltpu.make_async_copy(source, target, load_sem.at[k])
        for k, (source, target) in enumerate(
            (
                (x_hbm, x_ref),
                (g_hbm, g_ref),
                (wi_hbm, wi_ref),
                (wo_hbm, wo_ref),
                (weight_hbm.at[:, :, part(core, ROWS[0])], merged_ref.at[:, part(core, HD), :]),
                (grads_hbm.at[0, :, part(seq, nodes)], attended_ref.at[part(seq, HD), :]),
                (grads_hbm.at[pl.ds(1, 3), :, part(seq, nodes)], rows_ref.at[:, part(seq, HD), :]),
            )
        )
    ]
    for load in loads:
        load.start()
    peers = seq_peers(seq)
    greet([(dp, peer) for peer in peers] + [along(axis, offset) for axis in ("x", "z") for offset in (1, 2, 3)])

    sent = []

    def back(piece, source, target):
        copies = []
        for place, peer in enumerate(peers):
            copies.append(remote(source(peer), target, seq_sems, (piece, place), (dp, peer)))
            copies[-1].start()
        sent.extend(copies)
        return copies

    def back_rows(kind, h):
        mine = pl.ds(h * half, half)
        return back(
            1 + 2 * kind + h,
            lambda peer: grads_hbm.at[1 + kind, :, part(2 * peer + h, half)],
            rows_ref.at[kind, part(seq, HD), mine],
        )

    back_attended = back(0, lambda peer: grads_hbm.at[0, :, part(peer, nodes)], attended_ref.at[part(seq, HD), :])
    swap = remote(
        weight_hbm.at[:, :, part(1 - core, ROWS[0])], theirs_ref, core_sems, 0, other
    )
    swap.start()
    sent.append(swap)

    sums = (sum_send, sum_recv)
    make = lambda *args: Sum(*args, along, place_of, core)
    both = make(0, ("z", "x"), pl.ds(0, 2 * width), isum_ref, sums, (tot_a, out_a, quarters_a, parts_a, None))
    last = make(1, ("x", "z"), pl.ds(2 * width, width), isum_ref, sums, (tot_b, out_b, quarters_b, parts_b, None))
    left = make(2, ("x", "z"), pl.ds(0, half), osum_ref, sums, (tot_c, out_c, quarters_c, parts_c, levels_c))
    right = make(3, ("z", "x"), pl.ds(half, half), osum_ref, sums, (tot_d, out_d, quarters_d, parts_d, levels_d))

    loads[4].wait()
    swap.wait_recv()
    merged_ref[:, part(1 - core, HD), :] = theirs_ref[...]
    last.scatter_first(merged_ref[2].T)
    both.scatter_first(jnp.concatenate([merged_ref[0].T, merged_ref[1].T], 1))
    back_q = back_rows(0, 0)
    last.scatter_second()
    both.scatter_second()

    for load in loads[:4] + loads[5:]:
        load.wait()
    for copy in back_attended:
        copy.wait_recv()
    total_ref[...] = dot(attended_ref[...], g_ref[...])
    half_ref[0] = total_ref[part(1 - core, ROWS[0]), :].astype(BF16)
    merge = remote(half_ref.at[0], half_ref.at[1], core_sems, 1, other)
    merge.start()
    sent.append(merge)

    spread = []
    for job, kinds in ((last, (2,)), (both, (0, 1))):
        value = job.scattered()
        for k, kind in enumerate(kinds):
            columns = pl.ds(pl.multiple_of(kind * width + y * 2 * HD, 2 * HD), 2 * HD)
            here = job.region(2, columns)
            here[...] = value[:, k * 2 * HD : (k + 1) * 2 * HD]
            for offset in (2, 1, 3):
                spread.append(remote(here, here, (spread_send, spread_recv), (kind, offset - 1), along("y", offset)))
                spread[-1].start()
    sent.extend(spread)
    back_q += back_rows(0, 1)
    back_k = back_rows(1, 0)

    layer_ref[...] = (x_ref[...].astype(F32) + dot(attended_ref[...], wo_ref[...], TN)).astype(BF16)

    merge.wait_recv()
    merged = total_ref[part(core, ROWS[0]), :] + half_ref[1].astype(F32)
    left.scatter_first(merged[:, :half])
    right.scatter_first(merged[:, half:])
    for copy in spread:
        copy.wait_recv()
    last.gather(0)
    both.gather(0)
    left.scatter_second()
    right.scatter_second()
    left.exchange("y", y)
    right.exchange("y", y)
    back_k += back_rows(1, 1)
    back_v = back_rows(2, 0) + back_rows(2, 1)
    last.arrive()
    last.gather(1)
    both.arrive()
    both.gather(1)
    for copy in back_q:
        copy.wait_recv()
    total_ref[...] = dot(wi_ref[:, :width], rows_ref[0])
    left.exchanged()
    left.gather(0)
    right.exchanged()
    right.gather(0)
    for copy in back_k:
        copy.wait_recv()
    total_ref[...] += dot(wi_ref[:, width : 2 * width], rows_ref[1])
    left.arrive()
    left.gather(1)
    right.arrive()
    right.gather(1)
    last.arrive()
    both.arrive()

    def share(whole, index):
        mine = whole.at[part(core, ROWS[0]), :]
        copy = remote(mine, mine, core_sems, index, other)
        copy.start()
        sent.append(copy)
        return copy

    share_i = share(isum_ref, 2)
    for copy in back_v:
        copy.wait_recv()
    turned = (total_ref[...] + dot(wi_ref[:, 2 * width :], rows_ref[2])).T
    gradf_ref[...] = (g_ref[...].astype(F32) + turned).astype(BF16)
    left.arrive()
    right.arrive()
    share_o = share(osum_ref, 3)
    share_i.wait_recv()
    share_o.wait_recv()
    for job in (both, last, left, right):
        sent.extend(job.sent)
    for copy in sent:
        copy.wait_send()


def finish(grads, weight, x, g, wi, wo):
    nodes, width = x.shape
    vm = pl.BlockSpec(memory_space=pltpu.VMEM)
    anywhere = pl.BlockSpec(memory_space=pl.ANY)
    rows = jax.ShapeDtypeStruct((nodes, width), BF16)
    columns = (4 * HD, 2 * HD, width // 2, width // 2)
    dma = pltpu.SemaphoreType.DMA
    return pl.pallas_call(
        finish_kernel,
        out_shape=(
            rows,
            rows,
            jax.ShapeDtypeStruct((width, width), BF16),
            jax.ShapeDtypeStruct((width, 3 * width), BF16),
        ),
        in_specs=[anywhere] * 6,
        out_specs=(vm,) * 4,
        scratch_shapes=[
            pltpu.VMEM(x.shape, BF16),
            pltpu.VMEM(g.shape, BF16),
            pltpu.VMEM(wi.shape, BF16),
            pltpu.VMEM(wo.shape, BF16),
            pltpu.VMEM((width, nodes), BF16),
            pltpu.VMEM((3, width, nodes), BF16),
            pltpu.VMEM((3, 2 * HD, ROWS[0]), F32),
            pltpu.VMEM((3, HD, ROWS[0]), F32),
            pltpu.VMEM((2, ROWS[0], width), BF16),
            pltpu.VMEM((width, nodes), F32),
        ]
        + [pltpu.VMEM((ROWS[0], n), F32) for n in columns]
        + [pltpu.VMEM((ROWS[0] + ROWS[1], n), BF16) for n in columns]
        + [pltpu.VMEM((SIDE - 1, ROWS[1], n), BF16) for n in columns]
        + [pltpu.VMEM((SIDE - 1, ROWS[2], n), BF16) for n in columns]
        + [pltpu.VMEM((SIDE, ROWS[2], n), BF16) for n in columns[2:]]
        + [dma((7, H - 1))] * 2
        + [dma((4,))] * 2
        + [dma((4, 5, SIDE - 1))] * 2
        + [dma((3, SIDE - 1))] * 2
        + [dma((7,))],
        compiler_params=pltpu.CompilerParams(collective_id=1, has_side_effects=True, vmem_limit_bytes=VMEM_BYTES),
        name="finish",
    )(grads.reshape(4, HD, -1), weight.reshape(3, HD, -1), x, g, wi, wo)


def emit_kernel(factor, layer_ref, gradf_ref, osum_ref, isum_ref, layer_out, gradf_out, osum_out, isum_out):
    layer_out[...] = layer_ref[...]
    gradf_out[...] = gradf_ref[...]
    osum_out[...] = osum_ref[...].astype(F32) * factor
    isum_out[...] = isum_ref[...].astype(F32) * factor


def emit(layer, gradf, osum, isum, factor):
    arrays = (layer, gradf, osum, isum)
    kinds = (BF16, BF16, F32, F32)
    specs = [pl.BlockSpec((B, a.shape[1]), lambda i: (i, 0)) for a in arrays]
    return pl.pallas_call(
        partial(emit_kernel, factor),
        grid=(layer.shape[0] // B,),
        out_shape=tuple(jax.ShapeDtypeStruct(a.shape, kind) for a, kind in zip(arrays, kinds)),
        in_specs=specs,
        out_specs=tuple(specs),
        compiler_params=pltpu.CompilerParams(vmem_limit_bytes=VMEM_BYTES),
        name="emit",
    )(*arrays)


def shards(features, input_weight, output_weight, key_blocks, key_count, cotangent):
    x, g = features[0], cotangent[0]
    kv, kvt, qgt, order, everything = project(x, g, input_weight, output_weight, key_count[0])
    grads, weight = attention(order, key_blocks[0, 0], key_count[0, 0], kv, kvt, qgt, everything)
    results = finish(grads, weight, x, g, input_weight, output_weight)
    factor = 1.0 / (lax.axis_size("dp") * lax.axis_size("seq") * x.shape[0]) ** 0.5
    layer_out, grad_features, output_total, input_total = emit(*results, factor)
    return (layer_out[None], grad_features[None], input_total, output_total)


def solution(mesh):
    in_specs = (
        P("dp", "seq", None),
        P(),
        P(),
        P("dp", "seq", None, None),
        P("dp", "seq", None),
        P("dp", "seq", None),
    )
    out_specs = (P("dp", "seq", None), P("dp", "seq", None), P(), P())
    return jax.shard_map(shards, mesh=mesh, in_specs=in_specs, out_specs=out_specs, check_vma=False)
```

```python
from functools import partial

import jax
import jax.numpy as jnp
from jax import lax
from jax.experimental import pallas as pl
from jax.experimental.pallas import tpu as pltpu
from jax.sharding import PartitionSpec as P

H = 8
HD = 64
B = 128
KMAX = 8
NEGATIVE = -1e30
SCALE = HD**-0.5
MESH = pl.DeviceIdType.MESH
BF16 = jnp.bfloat16
F32 = jnp.float32
NN = (((1,), (0,)), ((), ()))
NT = (((1,), (1,)), ((), ()))
TN = (((0,), (0,)), ((), ()))
SIDE = 4
VMEM_BYTES = 60 << 20


def dot(a, b, dims=NN):
    return lax.dot_general(a, b, dims, preferred_element_type=F32)


def part(index, size):
    return pl.ds(pl.multiple_of(index * size, size), size)


def seq_peers(seq):
    y, core = seq // 2, seq % 2
    peers = []
    for dy in (2, 1, 3):
        for flip in (0, 1):
            peers.append(((y + dy) % SIDE) * 2 + (core + flip) % 2)
    peers.append(y * 2 + (core + 1) % 2)
    return peers


def greet(devices):
    barrier = pltpu.get_barrier_semaphore()
    for device in devices:
        pl.semaphore_signal(barrier, inc=1, device_id=device, device_id_type=MESH)
    pl.semaphore_wait(barrier, len(devices))


def remote(source, target, sems, index, device):
    return pltpu.make_async_remote_copy(
        src_ref=source,
        dst_ref=target,
        send_sem=sems[0].at[index],
        recv_sem=sems[1].at[index],
        device_id=device,
        device_id_type=MESH,
    )


def falling_order(counts):
    size = counts.shape[1]
    row = jnp.broadcast_to(counts.astype(F32), (size, size))
    here = lax.broadcasted_iota(jnp.int32, (size, size), 0)
    there = lax.broadcasted_iota(jnp.int32, (size, size), 1)
    column = jnp.sum(jnp.where(here == there, row, 0.0), 1, keepdims=True)
    ahead = (row > column) | ((row == column) & (there < here))
    rank = jnp.sum(jnp.where(ahead, 1.0, 0.0), 1, keepdims=True)
    found = jnp.where(rank == there.astype(F32), here.astype(F32), 0.0)
    return jnp.sum(found, 0, keepdims=True).astype(jnp.int32)


def project_kernel(
    x_hbm, g_hbm, wi_hbm, wo_hbm, count_ref,
    order_ref, all_hbm, kv_hbm, kvt_hbm, qt_hbm, gt_hbm,
    x_ref, kv_ref, kvt_ref, qt_ref, g_ref, wi_ref, wo_ref, grad_ref, send_sem, recv_sem, load_sem, store_sem,
):
    dp, seq = lax.axis_index("dp"), lax.axis_index("seq")
    y, core = seq // 2, seq % 2
    nodes, width = g_ref.shape
    half = nodes // 2
    sems = (send_sem, recv_sem)
    other = (dp, y * 2 + (core + 1) % 2)

    def at(dy, flip=0):
        return ((y + dy) % SIDE) * 2 + (core + flip) % 2

    peers = seq_peers(seq)
    loads = [
        pltpu.make_async_copy(source, target, load_sem.at[k])
        for k, (source, target) in enumerate(
            ((x_hbm, x_ref.at[seq]), (wi_hbm, wi_ref), (g_hbm, g_ref), (wo_hbm, wo_ref))
        )
    ]
    for load in loads:
        load.start()
    greet([(dp, peer) for peer in peers])
    up, down = (dp, at(1)), (dp, at(3))

    def rows(h):
        return pl.ds(h * half, half)

    def pass_on(source, h, index, device):
        piece = x_ref.at[source, rows(h)]
        return remote(piece, piece, sems, index, device)

    def own(h, index, device):
        return remote(x_hbm.at[rows(h)], x_ref.at[seq, rows(h)], sems, index, device)

    sent = [own(0, 0, up), own(1, 3, down), own(1, 1, up), own(0, 4, down), own(0, 6, other), own(1, 7, other)]
    for copy in sent:
        copy.start()

    loads[0].wait()
    loads[1].wait()
    chosen = []
    for kind in (1, 2, 0):
        block = wi_ref[:, pl.ds(pl.multiple_of(kind * width + y * 2 * HD, 2 * HD), 2 * HD)]
        chosen.append(jnp.where(core == 0, block[:, :HD], block[:, HD:]))
    chosen[2] = chosen[2] * jnp.asarray(SCALE, BF16)
    weights = jnp.concatenate(chosen + [jnp.zeros_like(chosen[0])], 1)
    stores = []

    def store(source, target):
        stores.append(pltpu.make_async_copy(source, target, store_sem.at[len(stores)]))
        stores[-1].start()

    def project_half(source, h):
        here = part(2 * source + h, half)
        product = dot(x_ref[source, rows(h), :], weights)
        kv = product[:, : 2 * HD].astype(BF16)
        kv_ref[here, :] = kv
        kvt_ref[:, here] = kv.T
        qt_ref[:, here] = product[:, 2 * HD :].T[:HD].astype(BF16)
        store(x_ref.at[source, rows(h)], all_hbm.at[here, :])
        store(kv_ref.at[here, :], kv_hbm.at[here, :])
        store(kvt_ref.at[:, here], kvt_hbm.at[:, here])
        store(qt_ref.at[:, here], qt_hbm.at[:, here])

    project_half(seq, 0)
    project_half(seq, 1)
    loads[2].wait()
    loads[3].wait()
    grad_ref[...] = dot(wo_ref[...], g_ref[...], NT).astype(BF16)
    store(grad_ref.at[part(seq, HD), :], gt_hbm.at[:, part(seq, nodes)])
    order_ref[...] = falling_order(count_ref[...])
    low, high, far = at(3), at(1), at(2)
    forwards = {0: pass_on(low, 0, 2, up), 3: pass_on(high, 1, 5, down)}
    shares = {0: (low, 0, 8), 3: (high, 1, 9), 1: (low, 1, 10), 4: (high, 0, 11), 2: (far, 0, 12), 5: (far, 1, 13)}
    ring = {index: own(0, index, up) for index in (0, 1, 2, 3, 4, 5)}
    near = {index: own(0, index, other) for index in range(6, 14)}

    def arrive(index):
        ring[index].wait_recv()
        source, h, share = shares[index]
        for copy in [forwards[index]] if index in forwards else []:
            copy.start()
            sent.append(copy)
        sent.append(pass_on(source, h, share, other))
        sent[-1].start()

    def project_arrived(index):
        project_half(*shares[index][:2])

    def arrive_near(share, source, h):
        near[share].wait_recv()
        project_half(source, h)

    arrive_near(6, at(0, 1), 0)
    arrive_near(7, at(0, 1), 1)
    arrive(0)
    arrive(3)
    given = []
    for place, peer in enumerate(peers):
        given.append(
            remote(grad_ref.at[part(peer, HD), :], gt_hbm.at[:, part(seq, nodes)], sems, 14 + place, (dp, peer))
        )
        given[-1].start()
    project_arrived(0)
    project_arrived(3)
    arrive_near(8, at(3, 1), 0)
    arrive_near(9, at(1, 1), 1)
    arrive(1)
    arrive(4)
    project_arrived(1)
    project_arrived(4)
    arrive_near(10, at(3, 1), 1)
    arrive_near(11, at(1, 1), 0)
    arrive(2)
    arrive(5)
    project_arrived(2)
    project_arrived(5)
    arrive_near(12, at(2, 1), 0)
    arrive_near(13, at(2, 1), 1)
    for copy in given:
        copy.wait_recv()
    for copy in sent + given:
        copy.wait_send()
    for copy in stores:
        copy.wait()


def project(x, g, wi, wo, counts):
    nodes, width = x.shape
    span = nodes * H
    vm = pl.BlockSpec(memory_space=pltpu.VMEM)
    anywhere = pl.BlockSpec(memory_space=pl.ANY)
    dma = pltpu.SemaphoreType.DMA
    return pl.pallas_call(
        project_kernel,
        out_shape=(
            jax.ShapeDtypeStruct(counts.shape, jnp.int32),
            jax.ShapeDtypeStruct((span, width), BF16),
            jax.ShapeDtypeStruct((span, 2 * HD), BF16),
            jax.ShapeDtypeStruct((2 * HD, span), BF16),
            jax.ShapeDtypeStruct((HD, span), BF16),
            jax.ShapeDtypeStruct((HD, span), BF16),
        ),
        in_specs=[anywhere] * 4 + [vm],
        out_specs=(vm,) + (anywhere,) * 5,
        scratch_shapes=[
            pltpu.VMEM((H, nodes, width), BF16),
            pltpu.VMEM((span, 2 * HD), BF16),
            pltpu.VMEM((2 * HD, span), BF16),
            pltpu.VMEM((HD, span), BF16),
            pltpu.VMEM(g.shape, BF16),
            pltpu.VMEM(wi.shape, BF16),
            pltpu.VMEM(wo.shape, BF16),
            pltpu.VMEM((width, nodes), BF16),
            dma((21,)),
            dma((21,)),
            dma((4,)),
            dma((8 * H + 1,)),
        ],
        compiler_params=pltpu.CompilerParams(collective_id=0, has_side_effects=True, vmem_limit_bytes=VMEM_BYTES),
        name="project",
    )(x, g, wi, wo, counts)


def attention_kernel(
    group, order_ref, blocks_ref, counts_ref, kv_ref, kvt_ref, qt_ref, gt_ref, all_hbm, grads_ref, weight_ref,
    total_ref, all_ref, load_sem,
):
    block_count = kvt_ref.shape[1] // B
    load = pltpu.make_async_copy(all_hbm, all_ref, load_sem)
    load.start()
    total_ref[...] = jnp.zeros_like(total_ref)
    zero = jnp.zeros((HD, B), BF16)

    def query_blocks(ids, live):
        heres = [pl.ds(pl.multiple_of(i * B, B), B) for i in ids]
        spots = [[pl.ds(pl.multiple_of(blocks_ref[j, i] * B, B), B) for j in range(live)] for i in ids]
        aparts, products = [], []
        for here, chosen in zip(heres, spots):
            apart = jnp.concatenate(
                [jnp.concatenate([qt_ref[:, here], zero], 1), jnp.concatenate([zero, gt_ref[:, here]], 1)], 0
            )
            aparts.append(apart)
            products.append(dot(jnp.concatenate([kv_ref[spot, :] for spot in chosen], 0), apart))
        pairs = []
        for i, product in zip(ids, products):
            count = counts_ref[i]
            scores = [product[:B, :B]]
            for j in range(1, live):
                scores.append(product[j * B : (j + 1) * B, :B] + jnp.where(j < count, 0.0, NEGATIVE))
            scores = jnp.concatenate(scores, 0)
            grad_probs = product[:, B:]
            raised = jnp.exp(scores - jnp.max(scores, 0, keepdims=True))
            inverse = 1.0 / jnp.sum(raised, 0, keepdims=True)
            row_delta = jnp.sum(raised * grad_probs, 0, keepdims=True) * inverse
            probs = raised * inverse
            grad_scores = (probs * (grad_probs - row_delta)).astype(BF16)
            pairs.append(jnp.concatenate([grad_scores, probs.astype(BF16)], 1))
        outs, terms = [], []
        for apart, chosen, pair in zip(aparts, spots, pairs):
            outs.append(dot(jnp.concatenate([kvt_ref[:, spot] for spot in chosen], 1), pair))
            terms.append(dot(apart, pair, NT))
        for here, out in zip(heres, outs):
            grads_ref[0:HD, here] = out[HD:, B:].astype(BF16)
            grads_ref[HD : 2 * HD, here] = (out[:HD, :B] * SCALE).astype(BF16)
        for chosen, term in zip(spots, terms):
            for j, spot in enumerate(chosen):
                total_ref[:, spot] += term[:, j * B : (j + 1) * B]

    def step(index, carry):
        ids = [order_ref[0, index * group + t] for t in range(group)]
        most = counts_ref[ids[0]]
        for live in range(1, KMAX + 1):
            pl.when(most == live)(partial(query_blocks, ids, live))
        return carry

    lax.fori_loop(0, block_count // group, step, 0)
    grads_ref[2 * HD :, :] = total_ref[...].astype(BF16)
    load.wait()
    weight_ref[...] = dot(grads_ref[HD:, :], all_ref[...])


def attention(order, blocks, counts, kv, kvt, qt, gt, everything):
    span, width = everything.shape
    vm = pl.BlockSpec(memory_space=pltpu.VMEM)
    sm = pl.BlockSpec(memory_space=pltpu.SMEM)
    return pl.pallas_call(
        partial(attention_kernel, 4),
        out_shape=(jax.ShapeDtypeStruct((4 * HD, span), BF16), jax.ShapeDtypeStruct((3 * HD, width), F32)),
        in_specs=[sm, sm, sm, vm, vm, vm, vm, pl.BlockSpec(memory_space=pl.ANY)],
        out_specs=(vm, vm),
        scratch_shapes=[
            pltpu.VMEM((2 * HD, span), F32),
            pltpu.VMEM(everything.shape, BF16),
            pltpu.SemaphoreType.DMA,
        ],
        compiler_params=pltpu.CompilerParams(vmem_limit_bytes=VMEM_BYTES),
        name="attention",
    )(order, blocks, counts, kv, kvt, qt, gt, everything)


ROWS = (256, 64, 16)


class Sum:
    def __init__(self, number, axes, columns, whole, sems, scratch, along, place_of, core):
        self.number, self.axes, self.columns, self.whole, self.sems = number, axes, columns, whole, sems
        self.total, self.out, self.quarters, self.parts, self.levels = scratch
        self.along = along
        self.place = [place_of[axis] for axis in axes]
        self.core = core
        self.waiting, self.sent = [], []

    def send(self, phase, axis, source, target):
        self.waiting = []
        for offset in (2, 1, 3):
            copy = remote(
                source(offset), target(offset), self.sems, (self.number, phase, offset - 1), self.along(axis, offset)
            )
            copy.start()
            self.waiting.append(copy)
        self.sent += self.waiting

    def arrive(self):
        for copy in self.waiting:
            copy.wait_recv()

    def scatter_first(self, value):
        self.total[...] = value
        self.out[0 : ROWS[0], :] = value.astype(BF16)
        spot = lambda offset: part((self.place[0] + offset) % SIDE, ROWS[1])
        self.send(
            0, self.axes[0], lambda o: self.out.at[spot(o), :], lambda o: self.quarters.at[o - 1]
        )

    def scatter_second(self):
        self.arrive()
        value = self.total[part(self.place[0], ROWS[1]), :] + self.quarters[0].astype(F32)
        value += self.quarters[1].astype(F32) + self.quarters[2].astype(F32)
        self.total[0 : ROWS[1], :] = value
        self.out[ROWS[0] :, :] = value.astype(BF16)
        spot = lambda offset: part(ROWS[0] // ROWS[2] + (self.place[1] + offset) % SIDE, ROWS[2])
        self.send(1, self.axes[1], lambda o: self.out.at[spot(o), :], lambda o: self.parts.at[o - 1])

    def scattered(self):
        self.arrive()
        value = self.total[part(self.place[1], ROWS[2]), :] + self.parts[0].astype(F32)
        return (value + (self.parts[1].astype(F32) + self.parts[2].astype(F32))).astype(BF16)

    def exchange(self, axis, place):
        self.levels[place] = self.scattered()
        here = self.levels.at[place]
        self.send(2, axis, lambda o: here, lambda o: here)

    def exchanged(self):
        self.arrive()
        value = [self.levels[k].astype(F32) for k in range(SIDE)]
        self.region(2)[...] = ((value[0] + value[1]) + (value[2] + value[3])).astype(BF16)

    def region(self, level, columns=None):
        first = self.core * ROWS[0]
        if level >= 1:
            first = first + self.place[0] * ROWS[1]
        if level >= 2:
            first = first + self.place[1] * ROWS[2]
        rows = pl.ds(pl.multiple_of(first, ROWS[2]), ROWS[level])
        return self.whole.at[rows, self.columns if columns is None else columns]

    def gather(self, step):
        here = self.region(2 - step)
        self.send(3 + step, self.axes[1 - step], lambda o: here, lambda o: here)


def finish_kernel(
    grads_hbm, weight_hbm, x_hbm, g_hbm, wi_hbm, wo_hbm,
    layer_ref, gradf_ref, osum_ref, isum_ref,
    x_ref, g_ref, wi_ref, wo_ref, attended_ref, rows_ref, merged_ref, theirs_ref, half_ref, total_ref,
    tot_a, tot_b, tot_c, tot_d, out_a, out_b, out_c, out_d, quarters_a, quarters_b, quarters_c, quarters_d,
    parts_a, parts_b, parts_c, parts_d, levels_c, levels_d,
    seq_send, seq_recv, core_send, core_recv, sum_send, sum_recv, spread_send, spread_recv, load_sem,
):
    dp, seq = lax.axis_index("dp"), lax.axis_index("seq")
    z, x, y, core = dp // SIDE, dp % SIDE, seq // 2, seq % 2
    place_of = {"x": x, "y": y, "z": z}
    nodes, width = x_ref.shape
    half = nodes // 2
    other = (dp, y * 2 + (core + 1) % 2)
    seq_sems, core_sems = (seq_send, seq_recv), (core_send, core_recv)

    def along(axis, offset):
        if axis == "y":
            return (dp, ((y + offset) % SIDE) * 2 + core)
        if axis == "x":
            return (z * SIDE + (x + offset) % SIDE, seq)
        return (((z + offset) % SIDE) * SIDE + x, seq)

    loads = [
        pltpu.make_async_copy(source, target, load_sem.at[k])
        for k, (source, target) in enumerate(
            (
                (x_hbm, x_ref),
                (g_hbm, g_ref),
                (wi_hbm, wi_ref),
                (wo_hbm, wo_ref),
                (weight_hbm.at[:, :, part(core, ROWS[0])], merged_ref.at[:, part(core, HD), :]),
                (grads_hbm.at[0, :, part(seq, nodes)], attended_ref.at[part(seq, HD), :]),
                (grads_hbm.at[pl.ds(1, 3), :, part(seq, nodes)], rows_ref.at[:, part(seq, HD), :]),
            )
        )
    ]
    for load in loads:
        load.start()
    peers = seq_peers(seq)
    greet([(dp, peer) for peer in peers] + [along(axis, offset) for axis in ("x", "z") for offset in (1, 2, 3)])

    sent = []

    def back(piece, source, target):
        copies = []
        for place, peer in enumerate(peers):
            copies.append(remote(source(peer), target, seq_sems, (piece, place), (dp, peer)))
            copies[-1].start()
        sent.extend(copies)
        return copies

    def back_rows(kind, h):
        mine = pl.ds(h * half, half)
        return back(
            1 + 2 * kind + h,
            lambda peer: grads_hbm.at[1 + kind, :, part(2 * peer + h, half)],
            rows_ref.at[kind, part(seq, HD), mine],
        )

    back_attended = back(0, lambda peer: grads_hbm.at[0, :, part(peer, nodes)], attended_ref.at[part(seq, HD), :])
    swap = remote(
        weight_hbm.at[:, :, part(1 - core, ROWS[0])], theirs_ref, core_sems, 0, other
    )
    swap.start()
    sent.append(swap)

    sums = (sum_send, sum_recv)
    make = lambda *args: Sum(*args, along, place_of, core)
    both = make(0, ("z", "x"), pl.ds(0, 2 * width), isum_ref, sums, (tot_a, out_a, quarters_a, parts_a, None))
    last = make(1, ("x", "z"), pl.ds(2 * width, width), isum_ref, sums, (tot_b, out_b, quarters_b, parts_b, None))
    left = make(2, ("x", "z"), pl.ds(0, half), osum_ref, sums, (tot_c, out_c, quarters_c, parts_c, levels_c))
    right = make(3, ("z", "x"), pl.ds(half, half), osum_ref, sums, (tot_d, out_d, quarters_d, parts_d, levels_d))

    loads[4].wait()
    swap.wait_recv()
    merged_ref[:, part(1 - core, HD), :] = theirs_ref[...]
    last.scatter_first(merged_ref[2].T)
    both.scatter_first(jnp.concatenate([merged_ref[0].T, merged_ref[1].T], 1))
    back_q = back_rows(0, 0)
    last.scatter_second()
    both.scatter_second()

    for load in loads[:4] + loads[5:]:
        load.wait()
    for copy in back_attended:
        copy.wait_recv()
    total_ref[...] = dot(attended_ref[...], g_ref[...])
    half_ref[0] = total_ref[part(1 - core, ROWS[0]), :].astype(BF16)
    merge = remote(half_ref.at[0], half_ref.at[1], core_sems, 1, other)
    merge.start()
    sent.append(merge)

    spread = []
    for job, kinds in ((last, (2,)), (both, (0, 1))):
        value = job.scattered()
        for k, kind in enumerate(kinds):
            columns = pl.ds(pl.multiple_of(kind * width + y * 2 * HD, 2 * HD), 2 * HD)
            here = job.region(2, columns)
            here[...] = value[:, k * 2 * HD : (k + 1) * 2 * HD]
            for offset in (2, 1, 3):
                spread.append(remote(here, here, (spread_send, spread_recv), (kind, offset - 1), along("y", offset)))
                spread[-1].start()
    sent.extend(spread)
    back_q += back_rows(0, 1)
    back_k = back_rows(1, 0)

    layer_ref[...] = (x_ref[...].astype(F32) + dot(attended_ref[...], wo_ref[...], TN)).astype(BF16)

    merge.wait_recv()
    merged = total_ref[part(core, ROWS[0]), :] + half_ref[1].astype(F32)
    left.scatter_first(merged[:, :half])
    right.scatter_first(merged[:, half:])
    for copy in spread:
        copy.wait_recv()
    last.gather(0)
    both.gather(0)
    left.scatter_second()
    right.scatter_second()
    left.exchange("y", y)
    right.exchange("y", y)
    back_k += back_rows(1, 1)
    back_v = back_rows(2, 0) + back_rows(2, 1)
    last.arrive()
    last.gather(1)
    both.arrive()
    both.gather(1)
    for copy in back_q:
        copy.wait_recv()
    total_ref[...] = dot(wi_ref[:, :width], rows_ref[0])
    left.exchanged()
    left.gather(0)
    right.exchanged()
    right.gather(0)
    for copy in back_k:
        copy.wait_recv()
    total_ref[...] += dot(wi_ref[:, width : 2 * width], rows_ref[1])
    left.arrive()
    left.gather(1)
    right.arrive()
    right.gather(1)
    last.arrive()
    both.arrive()

    def share(whole, index):
        mine = whole.at[part(core, ROWS[0]), :]
        copy = remote(mine, mine, core_sems, index, other)
        copy.start()
        sent.append(copy)
        return copy

    share_i = share(isum_ref, 2)
    for copy in back_v:
        copy.wait_recv()
    turned = (total_ref[...] + dot(wi_ref[:, 2 * width :], rows_ref[2])).T
    gradf_ref[...] = (g_ref[...].astype(F32) + turned).astype(BF16)
    left.arrive()
    right.arrive()
    share_o = share(osum_ref, 3)
    share_i.wait_recv()
    share_o.wait_recv()
    for job in (both, last, left, right):
        sent.extend(job.sent)
    for copy in sent:
        copy.wait_send()


def finish(grads, weight, x, g, wi, wo):
    nodes, width = x.shape
    vm = pl.BlockSpec(memory_space=pltpu.VMEM)
    anywhere = pl.BlockSpec(memory_space=pl.ANY)
    rows = jax.ShapeDtypeStruct((nodes, width), BF16)
    columns = (4 * HD, 2 * HD, width // 2, width // 2)
    dma = pltpu.SemaphoreType.DMA
    return pl.pallas_call(
        finish_kernel,
        out_shape=(
            rows,
            rows,
            jax.ShapeDtypeStruct((width, width), BF16),
            jax.ShapeDtypeStruct((width, 3 * width), BF16),
        ),
        in_specs=[anywhere] * 6,
        out_specs=(vm,) * 4,
        scratch_shapes=[
            pltpu.VMEM(x.shape, BF16),
            pltpu.VMEM(g.shape, BF16),
            pltpu.VMEM(wi.shape, BF16),
            pltpu.VMEM(wo.shape, BF16),
            pltpu.VMEM((width, nodes), BF16),
            pltpu.VMEM((3, width, nodes), BF16),
            pltpu.VMEM((3, 2 * HD, ROWS[0]), F32),
            pltpu.VMEM((3, HD, ROWS[0]), F32),
            pltpu.VMEM((2, ROWS[0], width), BF16),
            pltpu.VMEM((width, nodes), F32),
        ]
        + [pltpu.VMEM((ROWS[0], n), F32) for n in columns]
        + [pltpu.VMEM((ROWS[0] + ROWS[1], n), BF16) for n in columns]
        + [pltpu.VMEM((SIDE - 1, ROWS[1], n), BF16) for n in columns]
        + [pltpu.VMEM((SIDE - 1, ROWS[2], n), BF16) for n in columns]
        + [pltpu.VMEM((SIDE, ROWS[2], n), BF16) for n in columns[2:]]
        + [dma((7, H - 1))] * 2
        + [dma((4,))] * 2
        + [dma((4, 5, SIDE - 1))] * 2
        + [dma((3, SIDE - 1))] * 2
        + [dma((7,))],
        compiler_params=pltpu.CompilerParams(collective_id=1, has_side_effects=True, vmem_limit_bytes=VMEM_BYTES),
        name="finish",
    )(grads.reshape(4, HD, -1), weight.reshape(3, HD, -1), x, g, wi, wo)


def emit_kernel(factor, layer_ref, gradf_ref, osum_ref, isum_ref, layer_out, gradf_out, osum_out, isum_out):
    layer_out[...] = layer_ref[...]
    gradf_out[...] = gradf_ref[...]
    osum_out[...] = osum_ref[...].astype(F32) * factor
    isum_out[...] = isum_ref[...].astype(F32) * factor


def emit(layer, gradf, osum, isum, factor):
    arrays = (layer, gradf, osum, isum)
    kinds = (BF16, BF16, F32, F32)
    rows = layer.shape[0] // 2
    specs = [pl.BlockSpec((rows, a.shape[1]), lambda i: (i, 0)) for a in arrays]
    return pl.pallas_call(
        partial(emit_kernel, factor),
        grid=(2,),
        out_shape=tuple(jax.ShapeDtypeStruct(a.shape, kind) for a, kind in zip(arrays, kinds)),
        in_specs=specs,
        out_specs=tuple(specs),
        compiler_params=pltpu.CompilerParams(vmem_limit_bytes=VMEM_BYTES),
        name="emit",
    )(*arrays)


def shards(features, input_weight, output_weight, key_blocks, key_count, cotangent):
    x, g = features[0], cotangent[0]
    order, everything, kv, kvt, qt, gt = project(x, g, input_weight, output_weight, key_count[0])
    grads, weight = attention(order, key_blocks[0, 0].T, key_count[0, 0], kv, kvt, qt, gt, everything)
    results = finish(grads, weight, x, g, input_weight, output_weight)
    factor = 1.0 / (lax.axis_size("dp") * lax.axis_size("seq") * x.shape[0]) ** 0.5
    layer_out, grad_features, output_total, input_total = emit(*results, factor)
    return (layer_out[None], grad_features[None], input_total, output_total)


def solution(mesh):
    in_specs = (
        P("dp", "seq", None),
        P(),
        P(),
        P("dp", "seq", None, None),
        P("dp", "seq", None),
        P("dp", "seq", None),
    )
    out_specs = (P("dp", "seq", None), P("dp", "seq", None), P(), P())
    return jax.shard_map(shards, mesh=mesh, in_specs=in_specs, out_specs=out_specs, check_vma=False)
```

```python
from functools import partial

import jax
import jax.numpy as jnp
from jax import lax
from jax.experimental import pallas as pl
from jax.experimental.pallas import tpu as pltpu
from jax.sharding import PartitionSpec as P

H = 8
HD = 64
B = 128
KMAX = 8
NEGATIVE = -1e30
SCALE = HD**-0.5
MESH = pl.DeviceIdType.MESH
BF16 = jnp.bfloat16
F32 = jnp.float32
NN = (((1,), (0,)), ((), ()))
NT = (((1,), (1,)), ((), ()))
TN = (((0,), (0,)), ((), ()))
SIDE = 4
VMEM_BYTES = 60 << 20


def dot(a, b, dims=NN):
    return lax.dot_general(a, b, dims, preferred_element_type=F32)


def part(index, size):
    return pl.ds(pl.multiple_of(index * size, size), size)


def seq_peers(seq):
    y, core = seq // 2, seq % 2
    peers = []
    for dy in (2, 1, 3):
        for flip in (0, 1):
            peers.append(((y + dy) % SIDE) * 2 + (core + flip) % 2)
    peers.append(y * 2 + (core + 1) % 2)
    return peers


def greet(devices):
    barrier = pltpu.get_barrier_semaphore()
    for device in devices:
        pl.semaphore_signal(barrier, inc=1, device_id=device, device_id_type=MESH)
    pl.semaphore_wait(barrier, len(devices))


def remote(source, target, sems, index, device):
    return pltpu.make_async_remote_copy(
        src_ref=source,
        dst_ref=target,
        send_sem=sems[0].at[index],
        recv_sem=sems[1].at[index],
        device_id=device,
        device_id_type=MESH,
    )


def falling_order(counts):
    size = counts.shape[1]
    row = jnp.broadcast_to(counts.astype(F32), (size, size))
    here = lax.broadcasted_iota(jnp.int32, (size, size), 0)
    there = lax.broadcasted_iota(jnp.int32, (size, size), 1)
    column = jnp.sum(jnp.where(here == there, row, 0.0), 1, keepdims=True)
    ahead = (row > column) | ((row == column) & (there < here))
    rank = jnp.sum(jnp.where(ahead, 1.0, 0.0), 1, keepdims=True)
    found = jnp.where(rank == there.astype(F32), here.astype(F32), 0.0)
    return jnp.sum(found, 0, keepdims=True).astype(jnp.int32)


def project_kernel(
    x_hbm, g_hbm, wi_hbm, wo_hbm, count_ref,
    order_ref, all_hbm, kv_hbm, kvt_hbm, qt_hbm, gt_hbm,
    x_ref, kv_ref, kvt_ref, qt_ref, g_ref, wi_ref, wo_ref, grad_ref, send_sem, recv_sem, load_sem, store_sem,
):
    dp, seq = lax.axis_index("dp"), lax.axis_index("seq")
    y, core = seq // 2, seq % 2
    nodes, width = g_ref.shape
    half = nodes // 2
    sems = (send_sem, recv_sem)
    other = (dp, y * 2 + (core + 1) % 2)

    def at(dy, flip=0):
        return ((y + dy) % SIDE) * 2 + (core + flip) % 2

    peers = seq_peers(seq)
    loads = [
        pltpu.make_async_copy(source, target, load_sem.at[k])
        for k, (source, target) in enumerate(
            ((x_hbm, x_ref.at[seq]), (wi_hbm, wi_ref), (g_hbm, g_ref), (wo_hbm, wo_ref))
        )
    ]
    for load in loads:
        load.start()
    greet([(dp, peer) for peer in peers])
    up, down = (dp, at(1)), (dp, at(3))

    def rows(h):
        return pl.ds(h * half, half)

    def pass_on(source, h, index, device):
        piece = x_ref.at[source, rows(h)]
        return remote(piece, piece, sems, index, device)

    def own(h, index, device):
        return remote(x_hbm.at[rows(h)], x_ref.at[seq, rows(h)], sems, index, device)

    sent = [own(0, 0, up), own(1, 3, down), own(1, 1, up), own(0, 4, down), own(0, 6, other), own(1, 7, other)]
    for copy in sent:
        copy.start()

    loads[0].wait()
    loads[1].wait()
    chosen = []
    for kind in (1, 2, 0):
        block = wi_ref[:, pl.ds(pl.multiple_of(kind * width + y * 2 * HD, 2 * HD), 2 * HD)]
        chosen.append(jnp.where(core == 0, block[:, :HD], block[:, HD:]))
    chosen[2] = chosen[2] * jnp.asarray(SCALE, BF16)
    weights = jnp.concatenate(chosen + [jnp.zeros_like(chosen[0])], 1)
    stores = []

    def store(source, target):
        stores.append(pltpu.make_async_copy(source, target, store_sem.at[len(stores)]))
        stores[-1].start()

    def project_half(source, h):
        here = part(2 * source + h, half)
        product = dot(x_ref[source, rows(h), :], weights)
        kv = product[:, : 2 * HD].astype(BF16)
        kv_ref[here, :] = kv
        kvt_ref[:, here] = kv.T
        qt_ref[:, here] = product[:, 2 * HD :].T[:HD].astype(BF16)
        store(x_ref.at[source, rows(h)], all_hbm.at[here, :])
        store(kv_ref.at[here, :], kv_hbm.at[here, :])
        store(kvt_ref.at[:, here], kvt_hbm.at[:, here])
        store(qt_ref.at[:, here], qt_hbm.at[:, here])

    project_half(seq, 0)
    project_half(seq, 1)
    loads[2].wait()
    loads[3].wait()
    grad_ref[...] = dot(wo_ref[...], g_ref[...], NT).astype(BF16)
    store(grad_ref.at[part(seq, HD), :], gt_hbm.at[:, part(seq, nodes)])
    order_ref[...] = falling_order(count_ref[...])
    low, high, far = at(3), at(1), at(2)
    forwards = {0: pass_on(low, 0, 2, up), 3: pass_on(high, 1, 5, down)}
    shares = {0: (low, 0, 8), 3: (high, 1, 9), 1: (low, 1, 10), 4: (high, 0, 11), 2: (far, 0, 12), 5: (far, 1, 13)}
    ring = {index: own(0, index, up) for index in (0, 1, 2, 3, 4, 5)}
    near = {index: own(0, index, other) for index in range(6, 14)}

    def arrive(index):
        ring[index].wait_recv()
        source, h, share = shares[index]
        for copy in [forwards[index]] if index in forwards else []:
            copy.start()
            sent.append(copy)
        sent.append(pass_on(source, h, share, other))
        sent[-1].start()

    def project_arrived(index):
        project_half(*shares[index][:2])

    def arrive_near(share, source, h):
        near[share].wait_recv()
        project_half(source, h)

    arrive_near(6, at(0, 1), 0)
    arrive_near(7, at(0, 1), 1)
    arrive(0)
    arrive(3)
    given = []
    for place, peer in enumerate(peers):
        given.append(
            remote(grad_ref.at[part(peer, HD), :], gt_hbm.at[:, part(seq, nodes)], sems, 14 + place, (dp, peer))
        )
        given[-1].start()
    project_arrived(0)
    project_arrived(3)
    arrive_near(8, at(3, 1), 0)
    arrive_near(9, at(1, 1), 1)
    arrive(1)
    arrive(4)
    project_arrived(1)
    project_arrived(4)
    arrive_near(10, at(3, 1), 1)
    arrive_near(11, at(1, 1), 0)
    arrive(2)
    arrive(5)
    project_arrived(2)
    project_arrived(5)
    arrive_near(12, at(2, 1), 0)
    arrive_near(13, at(2, 1), 1)
    for copy in sent:
        copy.wait_send()
    for copy in stores:
        copy.wait()
    for copy in given:
        copy.wait_send()
    for copy in given:
        copy.wait_recv()


def project(x, g, wi, wo, counts):
    nodes, width = x.shape
    span = nodes * H
    vm = pl.BlockSpec(memory_space=pltpu.VMEM)
    anywhere = pl.BlockSpec(memory_space=pl.ANY)
    dma = pltpu.SemaphoreType.DMA
    return pl.pallas_call(
        project_kernel,
        out_shape=(
            jax.ShapeDtypeStruct(counts.shape, jnp.int32),
            jax.ShapeDtypeStruct((span, width), BF16),
            jax.ShapeDtypeStruct((span, 2 * HD), BF16),
            jax.ShapeDtypeStruct((2 * HD, span), BF16),
            jax.ShapeDtypeStruct((HD, span), BF16),
            jax.ShapeDtypeStruct((HD, span), BF16),
        ),
        in_specs=[anywhere] * 4 + [vm],
        out_specs=(vm,) + (anywhere,) * 5,
        scratch_shapes=[
            pltpu.VMEM((H, nodes, width), BF16),
            pltpu.VMEM((span, 2 * HD), BF16),
            pltpu.VMEM((2 * HD, span), BF16),
            pltpu.VMEM((HD, span), BF16),
            pltpu.VMEM(g.shape, BF16),
            pltpu.VMEM(wi.shape, BF16),
            pltpu.VMEM(wo.shape, BF16),
            pltpu.VMEM((width, nodes), BF16),
            dma((21,)),
            dma((21,)),
            dma((4,)),
            dma((8 * H + 1,)),
        ],
        compiler_params=pltpu.CompilerParams(collective_id=0, has_side_effects=True, vmem_limit_bytes=VMEM_BYTES),
        name="project",
    )(x, g, wi, wo, counts)


def attention_kernel(
    group, order_ref, blocks_ref, counts_ref, kv_ref, kvt_ref, qt_ref, gt_ref, all_hbm, grads_ref, weight_ref,
    total_ref, all_ref, load_sem,
):
    block_count = kvt_ref.shape[1] // B
    load = pltpu.make_async_copy(all_hbm, all_ref, load_sem)
    load.start()
    total_ref[...] = jnp.zeros_like(total_ref)
    zero = jnp.zeros((HD, B), BF16)

    def query_blocks(ids, live):
        heres = [pl.ds(pl.multiple_of(i * B, B), B) for i in ids]
        spots = [[pl.ds(pl.multiple_of(blocks_ref[j, i] * B, B), B) for j in range(live)] for i in ids]
        aparts, products = [], []
        for here, chosen in zip(heres, spots):
            apart = jnp.concatenate(
                [jnp.concatenate([qt_ref[:, here], zero], 1), jnp.concatenate([zero, gt_ref[:, here]], 1)], 0
            )
            aparts.append(apart)
            products.append(dot(jnp.concatenate([kv_ref[spot, :] for spot in chosen], 0), apart))
        pairs = []
        for i, product in zip(ids, products):
            count = counts_ref[i]
            scores = [product[:B, :B]]
            for j in range(1, live):
                scores.append(product[j * B : (j + 1) * B, :B] + jnp.where(j < count, 0.0, NEGATIVE))
            scores = jnp.concatenate(scores, 0)
            grad_probs = product[:, B:]
            raised = jnp.exp(scores - jnp.max(scores, 0, keepdims=True))
            inverse = 1.0 / jnp.sum(raised, 0, keepdims=True)
            row_delta = jnp.sum(raised * grad_probs, 0, keepdims=True) * inverse
            probs = raised * inverse
            grad_scores = (probs * (grad_probs - row_delta)).astype(BF16)
            pairs.append(jnp.concatenate([grad_scores, probs.astype(BF16)], 1))
        outs, terms = [], []
        for apart, chosen, pair in zip(aparts, spots, pairs):
            outs.append(dot(jnp.concatenate([kvt_ref[:, spot] for spot in chosen], 1), pair))
            terms.append(dot(apart, pair, NT))
        for here, out in zip(heres, outs):
            grads_ref[0:HD, here] = out[HD:, B:].astype(BF16)
            grads_ref[HD : 2 * HD, here] = (out[:HD, :B] * SCALE).astype(BF16)
        for chosen, term in zip(spots, terms):
            for j, spot in enumerate(chosen):
                total_ref[:, spot] += term[:, j * B : (j + 1) * B]

    def step(index, carry):
        ids = [order_ref[0, index * group + t] for t in range(group)]
        most = counts_ref[ids[0]]
        for live in range(1, KMAX + 1):
            pl.when(most == live)(partial(query_blocks, ids, live))
        return carry

    lax.fori_loop(0, block_count // group, step, 0)
    grads_ref[2 * HD :, :] = total_ref[...].astype(BF16)
    load.wait()
    weight_ref[...] = dot(grads_ref[HD:, :], all_ref[...])


def attention(order, blocks, counts, kv, kvt, qt, gt, everything):
    span, width = everything.shape
    vm = pl.BlockSpec(memory_space=pltpu.VMEM)
    sm = pl.BlockSpec(memory_space=pltpu.SMEM)
    return pl.pallas_call(
        partial(attention_kernel, 4),
        out_shape=(jax.ShapeDtypeStruct((4 * HD, span), BF16), jax.ShapeDtypeStruct((3 * HD, width), F32)),
        in_specs=[sm, sm, sm, vm, vm, vm, vm, pl.BlockSpec(memory_space=pl.ANY)],
        out_specs=(vm, vm),
        scratch_shapes=[
            pltpu.VMEM((2 * HD, span), F32),
            pltpu.VMEM(everything.shape, BF16),
            pltpu.SemaphoreType.DMA,
        ],
        compiler_params=pltpu.CompilerParams(vmem_limit_bytes=VMEM_BYTES),
        name="attention",
    )(order, blocks, counts, kv, kvt, qt, gt, everything)


ROWS = (256, 64, 16)


class Sum:
    def __init__(self, number, axes, columns, whole, sems, scratch, along, place_of, core):
        self.number, self.axes, self.columns, self.whole, self.sems = number, axes, columns, whole, sems
        self.total, self.out, self.quarters, self.parts, self.levels = scratch
        self.along = along
        self.place = [place_of[axis] for axis in axes]
        self.core = core
        self.waiting, self.sent = {}, []

    def send(self, phase, axis, source, target):
        copies = {}
        for offset in (2, 1, 3):
            copies[offset] = remote(
                source(offset), target(offset), self.sems, (self.number, phase, offset - 1), self.along(axis, offset)
            )
            copies[offset].start()
        self.waiting[phase] = copies
        self.sent += copies.values()

    def arrive(self, *phases):
        for phase in phases:
            for copy in self.waiting[phase].values():
                copy.wait_recv()

    def scatter_first(self, value):
        self.total[...] = value
        self.out[0 : ROWS[0], :] = value.astype(BF16)
        spot = lambda offset: part((self.place[0] + offset) % SIDE, ROWS[1])
        self.send(0, self.axes[0], lambda o: self.out.at[spot(o), :], lambda o: self.quarters.at[o - 1])

    def scatter_second(self):
        self.arrive(0)
        value = self.total[part(self.place[0], ROWS[1]), :] + self.quarters[0].astype(F32)
        value += self.quarters[1].astype(F32) + self.quarters[2].astype(F32)
        self.total[0 : ROWS[1], :] = value
        self.out[ROWS[0] :, :] = value.astype(BF16)
        spot = lambda offset: part(ROWS[0] // ROWS[2] + (self.place[1] + offset) % SIDE, ROWS[2])
        self.send(1, self.axes[1], lambda o: self.out.at[spot(o), :], lambda o: self.parts.at[o - 1])

    def scattered(self):
        self.arrive(1)
        value = self.total[part(self.place[1], ROWS[2]), :] + self.parts[0].astype(F32)
        return (value + (self.parts[1].astype(F32) + self.parts[2].astype(F32))).astype(BF16)

    def exchange(self, axis, place):
        self.levels[place] = self.scattered()
        here = self.levels.at[place]
        self.send(2, axis, lambda o: here, lambda o: here)

    def exchanged(self):
        self.arrive(2)
        value = [self.levels[k].astype(F32) for k in range(SIDE)]
        self.region()[...] = ((value[0] + value[1]) + (value[2] + value[3])).astype(BF16)

    def region(self, second=None, columns=None):
        second = self.place[1] if second is None else second
        first = self.core * ROWS[0] + self.place[0] * ROWS[1] + second * ROWS[2]
        rows = pl.ds(pl.multiple_of(first, ROWS[2]), ROWS[2])
        return self.whole.at[rows, self.columns if columns is None else columns]

    def gather(self):
        here = self.region()
        self.send(3, self.axes[1], lambda o: here, lambda o: here)
        self.send(4, self.axes[0], lambda o: here, lambda o: here)

    def gather_on(self):
        for offset, copy in self.waiting[3].items():
            copy.wait_recv()
            here = self.region((self.place[1] + SIDE - offset) % SIDE)
            self.send(4 + offset, self.axes[0], lambda o: here, lambda o: here)

    def gathered(self):
        self.arrive(4, 5, 6, 7)


def finish_kernel(
    grads_hbm, weight_hbm, x_hbm, g_hbm, wi_hbm, wo_hbm,
    layer_hbm, gradf_hbm, osum_hbm, isum_hbm,
    layer_ref, gradf_ref, osum_ref, isum_ref,
    x_ref, g_ref, wi_ref, wo_ref, attended_ref, rows_ref, merged_ref, theirs_ref, half_ref, total_ref,
    tot_a, tot_b, tot_c, tot_d, out_a, out_b, out_c, out_d, quarters_a, quarters_b, quarters_c, quarters_d,
    parts_a, parts_b, parts_c, parts_d, levels_c, levels_d,
    seq_send, seq_recv, core_send, core_recv, sum_send, sum_recv, spread_send, spread_recv, load_sem, store_sem,
):
    dp, seq = lax.axis_index("dp"), lax.axis_index("seq")
    z, x, y, core = dp // SIDE, dp % SIDE, seq // 2, seq % 2
    place_of = {"x": x, "y": y, "z": z}
    nodes, width = x_ref.shape
    half = nodes // 2
    other = (dp, y * 2 + (core + 1) % 2)
    seq_sems, core_sems = (seq_send, seq_recv), (core_send, core_recv)

    def along(axis, offset):
        if axis == "y":
            return (dp, ((y + offset) % SIDE) * 2 + core)
        if axis == "x":
            return (z * SIDE + (x + offset) % SIDE, seq)
        return (((z + offset) % SIDE) * SIDE + x, seq)

    loads = [
        pltpu.make_async_copy(source, target, load_sem.at[k])
        for k, (source, target) in enumerate(
            (
                (weight_hbm.at[:, :, part(core, ROWS[0])], merged_ref.at[:, part(core, HD), :]),
                (grads_hbm.at[0, :, part(seq, nodes)], attended_ref.at[part(seq, HD), :]),
                (g_hbm, g_ref),
                (x_hbm, x_ref),
                (wo_hbm, wo_ref),
                (wi_hbm, wi_ref),
                (grads_hbm.at[pl.ds(1, 3), :, part(seq, nodes)], rows_ref.at[:, part(seq, HD), :]),
            )
        )
    ]
    for load in loads:
        load.start()
    peers = seq_peers(seq)
    greet([(dp, peer) for peer in peers] + [along(axis, offset) for axis in ("x", "z") for offset in (1, 2, 3)])

    sent, stores = [], []

    def store(source, target):
        stores.append(pltpu.make_async_copy(source, target, store_sem.at[len(stores)]))
        stores[-1].start()

    def back(piece, source, target):
        copies = []
        for place, peer in enumerate(peers):
            copies.append(remote(source(peer), target, seq_sems, (piece, place), (dp, peer)))
            copies[-1].start()
        sent.extend(copies)
        return copies

    def back_rows(kind, h):
        mine = pl.ds(h * half, half)
        return back(
            1 + 2 * kind + h,
            lambda peer: grads_hbm.at[1 + kind, :, part(2 * peer + h, half)],
            rows_ref.at[kind, part(seq, HD), mine],
        )

    swap = remote(weight_hbm.at[:, :, part(1 - core, ROWS[0])], theirs_ref, core_sems, 0, other)
    swap.start()
    sent.append(swap)
    back_attended = back(0, lambda peer: grads_hbm.at[0, :, part(peer, nodes)], attended_ref.at[part(seq, HD), :])

    sums = (sum_send, sum_recv)
    make = lambda *args: Sum(*args, along, place_of, core)
    both = make(0, ("z", "x"), pl.ds(0, 2 * width), isum_ref, sums, (tot_a, out_a, quarters_a, parts_a, None))
    last = make(1, ("x", "z"), pl.ds(2 * width, width), isum_ref, sums, (tot_b, out_b, quarters_b, parts_b, None))
    left = make(2, ("x", "z"), pl.ds(0, half), osum_ref, sums, (tot_c, out_c, quarters_c, parts_c, levels_c))
    right = make(3, ("z", "x"), pl.ds(half, half), osum_ref, sums, (tot_d, out_d, quarters_d, parts_d, levels_d))

    loads[0].wait()
    swap.wait_recv()
    merged_ref[:, part(1 - core, HD), :] = theirs_ref[...]
    both.scatter_first(jnp.concatenate([merged_ref[0].T, merged_ref[1].T], 1))
    last.scatter_first(merged_ref[2].T)
    back_q = back_rows(0, 0)
    for load in loads[1:]:
        load.wait()
    both.scatter_second()
    last.scatter_second()

    for copy in back_attended:
        copy.wait_recv()
    total_ref[...] = dot(attended_ref[...], g_ref[...])
    half_ref[0] = total_ref[part(1 - core, ROWS[0]), :].astype(BF16)
    merge = remote(half_ref.at[0], half_ref.at[1], core_sems, 1, other)
    merge.start()
    sent.append(merge)

    spread = []
    for job, kinds in ((both, (0, 1)), (last, (2,))):
        value = job.scattered()
        for k, kind in enumerate(kinds):
            columns = pl.ds(pl.multiple_of(kind * width + y * 2 * HD, 2 * HD), 2 * HD)
            here = job.region(columns=columns)
            here[...] = value[:, k * 2 * HD : (k + 1) * 2 * HD]
            for offset in (2, 1, 3):
                spread.append(remote(here, here, (spread_send, spread_recv), (kind, offset - 1), along("y", offset)))
                spread[-1].start()
    sent.extend(spread)
    back_q += back_rows(0, 1)
    back_k = back_rows(1, 0)
    merge.wait_recv()
    merged = total_ref[part(core, ROWS[0]), :] + half_ref[1].astype(F32)
    left.scatter_first(merged[:, :half])
    right.scatter_first(merged[:, half:])
    back_k += back_rows(1, 1)

    layer_ref[...] = (x_ref[...].astype(F32) + dot(attended_ref[...], wo_ref[...], TN)).astype(BF16)
    store(layer_ref, layer_hbm)
    for copy in spread:
        copy.wait_recv()
    both.gather()
    last.gather()
    left.scatter_second()
    right.scatter_second()
    both.gather_on()
    last.gather_on()
    left.exchange("y", y)
    right.exchange("y", y)
    back_v = back_rows(2, 0) + back_rows(2, 1)
    for copy in back_q:
        copy.wait_recv()
    total_ref[...] = dot(wi_ref[:, :width], rows_ref[0])
    left.exchanged()
    right.exchanged()
    left.gather()
    right.gather()
    both.gathered()
    last.gathered()

    def share(source, target, index):
        mine = part(core, ROWS[0])
        copy = remote(source.at[mine, :], target.at[mine, :], core_sems, index, other)
        copy.start()
        store(source.at[mine, :], target.at[mine, :])
        sent.append(copy)
        return copy

    share_i = share(isum_ref, isum_hbm, 2)
    left.gather_on()
    right.gather_on()
    for copy in back_k:
        copy.wait_recv()
    total_ref[...] += dot(wi_ref[:, width : 2 * width], rows_ref[1])
    late = {id(copy) for copy in back_v}
    settled = [copy for copy in sent if id(copy) not in late]
    for job in (both, last, left, right):
        settled.extend(job.sent)
    for copy in settled + back_v:
        copy.wait_send()
    for copy in back_v:
        copy.wait_recv()
    turned = (total_ref[...] + dot(wi_ref[:, 2 * width :], rows_ref[2])).T
    gradf_ref[...] = (g_ref[...].astype(F32) + turned).astype(BF16)
    store(gradf_ref, gradf_hbm)
    left.gathered()
    right.gathered()
    share_o = share(osum_ref, osum_hbm, 3)
    share_o.wait_send()
    for copy in stores:
        copy.wait()
    share_i.wait_recv()
    share_o.wait_recv()


def finish(grads, weight, x, g, wi, wo):
    nodes, width = x.shape
    anywhere = pl.BlockSpec(memory_space=pl.ANY)
    columns = (4 * HD, 2 * HD, width // 2, width // 2)
    dma = pltpu.SemaphoreType.DMA
    results = [(nodes, width), (nodes, width), (width, width), (width, 3 * width)]
    return pl.pallas_call(
        finish_kernel,
        out_shape=tuple(jax.ShapeDtypeStruct(shape, BF16) for shape in results),
        in_specs=[anywhere] * 6,
        out_specs=(anywhere,) * 4,
        scratch_shapes=[pltpu.VMEM(shape, BF16) for shape in results]
        + [
            pltpu.VMEM(x.shape, BF16),
            pltpu.VMEM(g.shape, BF16),
            pltpu.VMEM(wi.shape, BF16),
            pltpu.VMEM(wo.shape, BF16),
            pltpu.VMEM((width, nodes), BF16),
            pltpu.VMEM((3, width, nodes), BF16),
            pltpu.VMEM((3, 2 * HD, ROWS[0]), F32),
            pltpu.VMEM((3, HD, ROWS[0]), F32),
            pltpu.VMEM((2, ROWS[0], width), BF16),
            pltpu.VMEM((width, nodes), F32),
        ]
        + [pltpu.VMEM((ROWS[0], n), F32) for n in columns]
        + [pltpu.VMEM((ROWS[0] + ROWS[1], n), BF16) for n in columns]
        + [pltpu.VMEM((SIDE - 1, ROWS[1], n), BF16) for n in columns]
        + [pltpu.VMEM((SIDE - 1, ROWS[2], n), BF16) for n in columns]
        + [pltpu.VMEM((SIDE, ROWS[2], n), BF16) for n in columns[2:]]
        + [dma((7, H - 1))] * 2
        + [dma((4,))] * 2
        + [dma((4, 8, SIDE - 1))] * 2
        + [dma((3, SIDE - 1))] * 2
        + [dma((7,)), dma((4,))],
        compiler_params=pltpu.CompilerParams(collective_id=1, has_side_effects=True, vmem_limit_bytes=VMEM_BYTES),
        name="finish",
    )(grads.reshape(4, HD, -1), weight.reshape(3, HD, -1), x, g, wi, wo)


def emit_kernel(factor, layer_ref, gradf_ref, osum_ref, isum_ref, layer_out, gradf_out, osum_out, isum_out):
    layer_out[...] = layer_ref[...]
    gradf_out[...] = gradf_ref[...]
    osum_out[...] = osum_ref[...].astype(F32) * factor
    isum_out[...] = isum_ref[...].astype(F32) * factor


def emit(layer, gradf, osum, isum, factor):
    arrays = (layer, gradf, osum, isum)
    kinds = (BF16, BF16, F32, F32)
    rows = layer.shape[0] // 2
    specs = [pl.BlockSpec((rows, a.shape[1]), lambda i: (i, 0)) for a in arrays]
    return pl.pallas_call(
        partial(emit_kernel, factor),
        grid=(2,),
        out_shape=tuple(jax.ShapeDtypeStruct(a.shape, kind) for a, kind in zip(arrays, kinds)),
        in_specs=specs,
        out_specs=tuple(specs),
        compiler_params=pltpu.CompilerParams(vmem_limit_bytes=VMEM_BYTES),
        name="emit",
    )(*arrays)


def shards(features, input_weight, output_weight, key_blocks, key_count, cotangent):
    x, g = features[0], cotangent[0]
    order, everything, kv, kvt, qt, gt = project(x, g, input_weight, output_weight, key_count[0])
    grads, weight = attention(order, key_blocks[0, 0].T, key_count[0, 0], kv, kvt, qt, gt, everything)
    results = finish(grads, weight, x, g, input_weight, output_weight)
    factor = 1.0 / (lax.axis_size("dp") * lax.axis_size("seq") * x.shape[0]) ** 0.5
    layer_out, grad_features, output_total, input_total = emit(*results, factor)
    return (layer_out[None], grad_features[None], input_total, output_total)


def solution(mesh):
    in_specs = (
        P("dp", "seq", None),
        P(),
        P(),
        P("dp", "seq", None, None),
        P("dp", "seq", None),
        P("dp", "seq", None),
    )
    out_specs = (P("dp", "seq", None), P("dp", "seq", None), P(), P())
    return jax.shard_map(shards, mesh=mesh, in_specs=in_specs, out_specs=out_specs, check_vma=False)
```

```python
from functools import partial

import jax
import jax.numpy as jnp
from jax import lax
from jax.experimental import pallas as pl
from jax.experimental.pallas import tpu as pltpu
from jax.sharding import PartitionSpec as P

H = 8
HD = 64
B = 128
KMAX = 8
NEGATIVE = -1e30
SCALE = HD**-0.5
MESH = pl.DeviceIdType.MESH
BF16 = jnp.bfloat16
F32 = jnp.float32
NN = (((1,), (0,)), ((), ()))
NT = (((1,), (1,)), ((), ()))
TN = (((0,), (0,)), ((), ()))
SIDE = 4
VMEM_BYTES = 60 << 20
CALM = 1600.0


def dot(a, b, dims=NN):
    return lax.dot_general(a, b, dims, preferred_element_type=F32)


def part(index, size):
    return pl.ds(pl.multiple_of(index * size, size), size)


def seq_peers(seq):
    y, core = seq // 2, seq % 2
    peers = []
    for dy in (2, 1, 3):
        for flip in (0, 1):
            peers.append(((y + dy) % SIDE) * 2 + (core + flip) % 2)
    peers.append(y * 2 + (core + 1) % 2)
    return peers


def greet(devices):
    barrier = pltpu.get_barrier_semaphore()
    for device in devices:
        pl.semaphore_signal(barrier, inc=1, device_id=device, device_id_type=MESH)
    pl.semaphore_wait(barrier, len(devices))


def remote(source, target, sems, index, device):
    return pltpu.make_async_remote_copy(
        src_ref=source,
        dst_ref=target,
        send_sem=sems[0].at[index],
        recv_sem=sems[1].at[index],
        device_id=device,
        device_id_type=MESH,
    )


def falling_order(counts):
    size = counts.shape[1]
    row = jnp.broadcast_to(counts.astype(F32), (size, size))
    here = lax.broadcasted_iota(jnp.int32, (size, size), 0)
    there = lax.broadcasted_iota(jnp.int32, (size, size), 1)
    column = jnp.sum(jnp.where(here == there, row, 0.0), 1, keepdims=True)
    ahead = (row > column) | ((row == column) & (there < here))
    rank = jnp.sum(jnp.where(ahead, 1.0, 0.0), 1, keepdims=True)
    found = jnp.where(rank == there.astype(F32), here.astype(F32), 0.0)
    return jnp.sum(found, 0, keepdims=True).astype(jnp.int32)


def project_kernel(
    x_hbm, g_hbm, wi_hbm, wo_hbm, count_ref,
    order_ref, reach_ref, all_hbm, kv_hbm, kvt_hbm, qt_hbm, gt_hbm,
    x_ref, kv_ref, kvt_ref, qt_ref, g_ref, wi_ref, wo_ref, grad_ref, send_sem, recv_sem, load_sem, store_sem,
):
    dp, seq = lax.axis_index("dp"), lax.axis_index("seq")
    y, core = seq // 2, seq % 2
    nodes, width = g_ref.shape
    half = nodes // 2
    sems = (send_sem, recv_sem)
    other = (dp, y * 2 + (core + 1) % 2)

    def at(dy, flip=0):
        return ((y + dy) % SIDE) * 2 + (core + flip) % 2

    peers = seq_peers(seq)
    loads = [
        pltpu.make_async_copy(source, target, load_sem.at[k])
        for k, (source, target) in enumerate(
            ((x_hbm, x_ref.at[seq]), (wi_hbm, wi_ref), (g_hbm, g_ref), (wo_hbm, wo_ref))
        )
    ]
    for load in loads:
        load.start()
    greet([(dp, peer) for peer in peers])
    up, down = (dp, at(1)), (dp, at(3))

    def rows(h):
        return pl.ds(h * half, half)

    def pass_on(source, h, index, device):
        piece = x_ref.at[source, rows(h)]
        return remote(piece, piece, sems, index, device)

    def own(h, index, device):
        return remote(x_hbm.at[rows(h)], x_ref.at[seq, rows(h)], sems, index, device)

    sent = [own(0, 0, up), own(1, 3, down), own(1, 1, up), own(0, 4, down), own(0, 6, other), own(1, 7, other)]
    for copy in sent:
        copy.start()

    loads[0].wait()
    loads[1].wait()
    chosen = []
    for kind in (1, 2, 0):
        block = wi_ref[:, pl.ds(pl.multiple_of(kind * width + y * 2 * HD, 2 * HD), 2 * HD)]
        chosen.append(jnp.where(core == 0, block[:, :HD], block[:, HD:]))
    chosen[2] = chosen[2] * jnp.asarray(SCALE, BF16)
    weights = jnp.concatenate(chosen + [jnp.zeros_like(chosen[0])], 1)
    stores, largest = [], [None, None]

    def store(source, target):
        stores.append(pltpu.make_async_copy(source, target, store_sem.at[len(stores)]))
        stores[-1].start()

    def project_half(source, h):
        here = part(2 * source + h, half)
        product = dot(x_ref[source, rows(h), :], weights)
        kv = product[:, : 2 * HD].astype(BF16)
        kvt, qt = kv.T, product[:, 2 * HD :].T[:HD].astype(BF16)
        kv_ref[here, :] = kv
        kvt_ref[:, here] = kvt
        qt_ref[:, here] = qt
        for k, rows_of in enumerate((kvt[:HD], qt)):
            norms = jnp.sum(jnp.square(rows_of.astype(F32)), 0, keepdims=True)
            largest[k] = norms if largest[k] is None else jnp.maximum(largest[k], norms)
        store(x_ref.at[source, rows(h)], all_hbm.at[here, :])
        store(kv_ref.at[here, :], kv_hbm.at[here, :])
        store(kvt_ref.at[:, here], kvt_hbm.at[:, here])
        store(qt_ref.at[:, here], qt_hbm.at[:, here])

    project_half(seq, 0)
    project_half(seq, 1)
    loads[2].wait()
    loads[3].wait()
    grad_ref[...] = dot(wo_ref[...], g_ref[...], NT).astype(BF16)
    store(grad_ref.at[part(seq, HD), :], gt_hbm.at[:, part(seq, nodes)])
    order_ref[...] = falling_order(count_ref[...])
    low, high, far = at(3), at(1), at(2)
    forwards = {0: pass_on(low, 0, 2, up), 3: pass_on(high, 1, 5, down)}
    shares = {0: (low, 0, 8), 3: (high, 1, 9), 1: (low, 1, 10), 4: (high, 0, 11), 2: (far, 0, 12), 5: (far, 1, 13)}
    ring = {index: own(0, index, up) for index in (0, 1, 2, 3, 4, 5)}
    near = {index: own(0, index, other) for index in range(6, 14)}

    def arrive(index):
        ring[index].wait_recv()
        source, h, share = shares[index]
        for copy in [forwards[index]] if index in forwards else []:
            copy.start()
            sent.append(copy)
        sent.append(pass_on(source, h, share, other))
        sent[-1].start()

    def project_arrived(index):
        project_half(*shares[index][:2])

    def arrive_near(share, source, h):
        near[share].wait_recv()
        project_half(source, h)

    arrive_near(6, at(0, 1), 0)
    arrive_near(7, at(0, 1), 1)
    arrive(0)
    arrive(3)
    given = []
    for place, peer in enumerate(peers):
        given.append(
            remote(grad_ref.at[part(peer, HD), :], gt_hbm.at[:, part(seq, nodes)], sems, 14 + place, (dp, peer))
        )
        given[-1].start()
    project_arrived(0)
    project_arrived(3)
    arrive_near(8, at(3, 1), 0)
    arrive_near(9, at(1, 1), 1)
    arrive(1)
    arrive(4)
    project_arrived(1)
    project_arrived(4)
    arrive_near(10, at(3, 1), 1)
    arrive_near(11, at(1, 1), 0)
    arrive(2)
    arrive(5)
    project_arrived(2)
    project_arrived(5)
    arrive_near(12, at(2, 1), 0)
    arrive_near(13, at(2, 1), 1)
    reach = jnp.max(largest[0], 1, keepdims=True) * jnp.max(largest[1], 1, keepdims=True)
    reach_ref[...] = jnp.broadcast_to(reach, reach_ref.shape)
    for copy in sent:
        copy.wait_send()
    for copy in stores:
        copy.wait()
    for copy in given:
        copy.wait_send()
    for copy in given:
        copy.wait_recv()


def project(x, g, wi, wo, counts):
    nodes, width = x.shape
    span = nodes * H
    vm = pl.BlockSpec(memory_space=pltpu.VMEM)
    anywhere = pl.BlockSpec(memory_space=pl.ANY)
    dma = pltpu.SemaphoreType.DMA
    return pl.pallas_call(
        project_kernel,
        out_shape=(
            jax.ShapeDtypeStruct(counts.shape, jnp.int32),
            jax.ShapeDtypeStruct((1, B), F32),
            jax.ShapeDtypeStruct((span, width), BF16),
            jax.ShapeDtypeStruct((span, 2 * HD), BF16),
            jax.ShapeDtypeStruct((2 * HD, span), BF16),
            jax.ShapeDtypeStruct((HD, span), BF16),
            jax.ShapeDtypeStruct((HD, span), BF16),
        ),
        in_specs=[anywhere] * 4 + [vm],
        out_specs=(vm, vm) + (anywhere,) * 5,
        scratch_shapes=[
            pltpu.VMEM((H, nodes, width), BF16),
            pltpu.VMEM((span, 2 * HD), BF16),
            pltpu.VMEM((2 * HD, span), BF16),
            pltpu.VMEM((HD, span), BF16),
            pltpu.VMEM(g.shape, BF16),
            pltpu.VMEM(wi.shape, BF16),
            pltpu.VMEM(wo.shape, BF16),
            pltpu.VMEM((width, nodes), BF16),
            dma((21,)),
            dma((21,)),
            dma((4,)),
            dma((8 * H + 1,)),
        ],
        compiler_params=pltpu.CompilerParams(collective_id=0, has_side_effects=True, vmem_limit_bytes=VMEM_BYTES),
        name="project",
    )(x, g, wi, wo, counts)


def attention_kernel(
    group, order_ref, reach_ref, blocks_ref, counts_ref, kv_ref, kvt_ref, qt_ref, gt_ref, all_hbm, grads_ref, weight_ref,
    total_ref, all_ref, load_sem,
):
    block_count = kvt_ref.shape[1] // B
    load = pltpu.make_async_copy(all_hbm, all_ref, load_sem)
    load.start()
    total_ref[...] = jnp.zeros_like(total_ref)
    zero = jnp.zeros((HD, B), BF16)

    def query_blocks(ids, live, shifted):
        heres = [pl.ds(pl.multiple_of(i * B, B), B) for i in ids]
        spots = [[pl.ds(pl.multiple_of(blocks_ref[j, i] * B, B), B) for j in range(live)] for i in ids]
        aparts, products = [], []
        for here, chosen in zip(heres, spots):
            apart = jnp.concatenate(
                [jnp.concatenate([qt_ref[:, here], zero], 1), jnp.concatenate([zero, gt_ref[:, here]], 1)], 0
            )
            aparts.append(apart)
            products.append(dot(jnp.concatenate([kv_ref[spot, :] for spot in chosen], 0), apart))
        pairs = []
        for i, product in zip(ids, products):
            count = counts_ref[i]
            scores = [product[:B, :B]]
            for j in range(1, live):
                scores.append(product[j * B : (j + 1) * B, :B] + jnp.where(j < count, 0.0, NEGATIVE))
            scores = jnp.concatenate(scores, 0)
            grad_probs = product[:, B:]
            if shifted:
                scores = scores - jnp.max(scores, 0, keepdims=True)
            raised = jnp.exp(scores)
            inverse = 1.0 / jnp.sum(raised, 0, keepdims=True)
            row_delta = jnp.sum(raised * grad_probs, 0, keepdims=True) * inverse
            probs = raised * inverse
            grad_scores = (probs * (grad_probs - row_delta)).astype(BF16)
            pairs.append(jnp.concatenate([grad_scores, probs.astype(BF16)], 1))
        outs, terms = [], []
        for apart, chosen, pair in zip(aparts, spots, pairs):
            outs.append(dot(jnp.concatenate([kvt_ref[:, spot] for spot in chosen], 1), pair))
            terms.append(dot(apart, pair, NT))
        for here, out in zip(heres, outs):
            grads_ref[0:HD, here] = out[HD:, B:].astype(BF16)
            grads_ref[HD : 2 * HD, here] = (out[:HD, :B] * SCALE).astype(BF16)
        for chosen, term in zip(spots, terms):
            for j, spot in enumerate(chosen):
                total_ref[:, spot] += term[:, j * B : (j + 1) * B]

    def step(index, carry):
        ids = [order_ref[0, index * group + t] for t in range(group)]
        most = counts_ref[ids[0]]
        for live in range(1, KMAX + 1):
            pl.when(most == live)(partial(query_blocks, ids, live, False))
        return carry

    def step_shifted(index, carry):
        query_blocks([index], KMAX, True)
        return carry

    calm = reach_ref[0, 0] <= CALM

    @pl.when(calm)
    def _():
        lax.fori_loop(0, block_count // group, step, 0)

    @pl.when(jnp.logical_not(calm))
    def _():
        lax.fori_loop(0, block_count, step_shifted, 0)

    grads_ref[2 * HD :, :] = total_ref[...].astype(BF16)
    load.wait()
    weight_ref[...] = dot(grads_ref[HD:, :], all_ref[...])


def attention(order, reach, blocks, counts, kv, kvt, qt, gt, everything):
    span, width = everything.shape
    vm = pl.BlockSpec(memory_space=pltpu.VMEM)
    sm = pl.BlockSpec(memory_space=pltpu.SMEM)
    return pl.pallas_call(
        partial(attention_kernel, 4),
        out_shape=(jax.ShapeDtypeStruct((4 * HD, span), BF16), jax.ShapeDtypeStruct((3 * HD, width), F32)),
        in_specs=[sm, sm, sm, sm, vm, vm, vm, vm, pl.BlockSpec(memory_space=pl.ANY)],
        out_specs=(vm, vm),
        scratch_shapes=[
            pltpu.VMEM((2 * HD, span), F32),
            pltpu.VMEM(everything.shape, BF16),
            pltpu.SemaphoreType.DMA,
        ],
        compiler_params=pltpu.CompilerParams(vmem_limit_bytes=VMEM_BYTES),
        name="attention",
    )(order, reach, blocks, counts, kv, kvt, qt, gt, everything)


ROWS = (256, 64, 16)


class Sum:
    def __init__(self, number, axes, columns, whole, sems, scratch, along, place_of, core):
        self.number, self.axes, self.columns, self.whole, self.sems = number, axes, columns, whole, sems
        self.total, self.out, self.quarters, self.parts, self.levels = scratch
        self.along = along
        self.place = [place_of[axis] for axis in axes]
        self.core = core
        self.waiting, self.sent = {}, []

    def send(self, phase, axis, source, target):
        copies = {}
        for offset in (2, 1, 3):
            copies[offset] = remote(
                source(offset), target(offset), self.sems, (self.number, phase, offset - 1), self.along(axis, offset)
            )
            copies[offset].start()
        self.waiting[phase] = copies
        self.sent += copies.values()

    def arrive(self, *phases):
        for phase in phases:
            for copy in self.waiting[phase].values():
                copy.wait_recv()

    def scatter_first(self, value):
        self.total[...] = value
        self.out[0 : ROWS[0], :] = value.astype(BF16)
        spot = lambda offset: part((self.place[0] + offset) % SIDE, ROWS[1])
        self.send(0, self.axes[0], lambda o: self.out.at[spot(o), :], lambda o: self.quarters.at[o - 1])

    def scatter_second(self):
        self.arrive(0)
        value = self.total[part(self.place[0], ROWS[1]), :] + self.quarters[0].astype(F32)
        value += self.quarters[1].astype(F32) + self.quarters[2].astype(F32)
        self.total[0 : ROWS[1], :] = value
        self.out[ROWS[0] :, :] = value.astype(BF16)
        spot = lambda offset: part(ROWS[0] // ROWS[2] + (self.place[1] + offset) % SIDE, ROWS[2])
        self.send(1, self.axes[1], lambda o: self.out.at[spot(o), :], lambda o: self.parts.at[o - 1])

    def scattered(self):
        self.arrive(1)
        value = self.total[part(self.place[1], ROWS[2]), :] + self.parts[0].astype(F32)
        return (value + (self.parts[1].astype(F32) + self.parts[2].astype(F32))).astype(BF16)

    def exchange(self, axis, place):
        self.levels[place] = self.scattered()
        here = self.levels.at[place]
        self.send(2, axis, lambda o: here, lambda o: here)

    def exchanged(self):
        self.arrive(2)
        value = [self.levels[k].astype(F32) for k in range(SIDE)]
        self.region()[...] = ((value[0] + value[1]) + (value[2] + value[3])).astype(BF16)

    def region(self, second=None, columns=None):
        second = self.place[1] if second is None else second
        first = self.core * ROWS[0] + self.place[0] * ROWS[1] + second * ROWS[2]
        rows = pl.ds(pl.multiple_of(first, ROWS[2]), ROWS[2])
        return self.whole.at[rows, self.columns if columns is None else columns]

    def gather(self):
        here = self.region()
        self.send(3, self.axes[1], lambda o: here, lambda o: here)
        self.send(4, self.axes[0], lambda o: here, lambda o: here)

    def gather_on(self):
        for offset, copy in self.waiting[3].items():
            copy.wait_recv()
            here = self.region((self.place[1] + SIDE - offset) % SIDE)
            self.send(4 + offset, self.axes[0], lambda o: here, lambda o: here)

    def gathered(self):
        self.arrive(4, 5, 6, 7)


def finish_kernel(
    grads_hbm, weight_hbm, x_hbm, g_hbm, wi_hbm, wo_hbm,
    layer_hbm, gradf_hbm, osum_hbm, isum_hbm,
    layer_ref, gradf_ref, osum_ref, isum_ref,
    x_ref, g_ref, wi_ref, wo_ref, attended_ref, rows_ref, merged_ref, theirs_ref, half_ref, total_ref,
    tot_a, tot_b, tot_c, tot_d, out_a, out_b, out_c, out_d, quarters_a, quarters_b, quarters_c, quarters_d,
    parts_a, parts_b, parts_c, parts_d, levels_c, levels_d,
    seq_send, seq_recv, core_send, core_recv, sum_send, sum_recv, spread_send, spread_recv, load_sem, store_sem,
):
    dp, seq = lax.axis_index("dp"), lax.axis_index("seq")
    z, x, y, core = dp // SIDE, dp % SIDE, seq // 2, seq % 2
    place_of = {"x": x, "y": y, "z": z}
    nodes, width = x_ref.shape
    half = nodes // 2
    other = (dp, y * 2 + (core + 1) % 2)
    seq_sems, core_sems = (seq_send, seq_recv), (core_send, core_recv)

    def along(axis, offset):
        if axis == "y":
            return (dp, ((y + offset) % SIDE) * 2 + core)
        if axis == "x":
            return (z * SIDE + (x + offset) % SIDE, seq)
        return (((z + offset) % SIDE) * SIDE + x, seq)

    loads = [
        pltpu.make_async_copy(source, target, load_sem.at[k])
        for k, (source, target) in enumerate(
            (
                (weight_hbm.at[:, :, part(core, ROWS[0])], merged_ref.at[:, part(core, HD), :]),
                (grads_hbm.at[0, :, part(seq, nodes)], attended_ref.at[part(seq, HD), :]),
                (g_hbm, g_ref),
                (x_hbm, x_ref),
                (wo_hbm, wo_ref),
                (wi_hbm, wi_ref),
                (grads_hbm.at[pl.ds(1, 3), :, part(seq, nodes)], rows_ref.at[:, part(seq, HD), :]),
            )
        )
    ]
    for load in loads:
        load.start()
    peers = seq_peers(seq)
    greet([(dp, peer) for peer in peers] + [along(axis, offset) for axis in ("x", "z") for offset in (1, 2, 3)])

    sent, stores = [], []

    def store(source, target):
        stores.append(pltpu.make_async_copy(source, target, store_sem.at[len(stores)]))
        stores[-1].start()

    def back(piece, source, target):
        copies = []
        for place, peer in enumerate(peers):
            copies.append(remote(source(peer), target, seq_sems, (piece, place), (dp, peer)))
            copies[-1].start()
        sent.extend(copies)
        return copies

    def back_rows(kind, h):
        mine = pl.ds(h * half, half)
        return back(
            1 + 2 * kind + h,
            lambda peer: grads_hbm.at[1 + kind, :, part(2 * peer + h, half)],
            rows_ref.at[kind, part(seq, HD), mine],
        )

    swap = remote(weight_hbm.at[:, :, part(1 - core, ROWS[0])], theirs_ref, core_sems, 0, other)
    swap.start()
    sent.append(swap)
    back_attended = back(0, lambda peer: grads_hbm.at[0, :, part(peer, nodes)], attended_ref.at[part(seq, HD), :])

    sums = (sum_send, sum_recv)
    make = lambda *args: Sum(*args, along, place_of, core)
    both = make(0, ("z", "x"), pl.ds(0, 2 * width), isum_ref, sums, (tot_a, out_a, quarters_a, parts_a, None))
    last = make(1, ("x", "z"), pl.ds(2 * width, width), isum_ref, sums, (tot_b, out_b, quarters_b, parts_b, None))
    left = make(2, ("x", "z"), pl.ds(0, half), osum_ref, sums, (tot_c, out_c, quarters_c, parts_c, levels_c))
    right = make(3, ("z", "x"), pl.ds(half, half), osum_ref, sums, (tot_d, out_d, quarters_d, parts_d, levels_d))

    loads[0].wait()
    swap.wait_recv()
    merged_ref[:, part(1 - core, HD), :] = theirs_ref[...]
    both.scatter_first(jnp.concatenate([merged_ref[0].T, merged_ref[1].T], 1))
    last.scatter_first(merged_ref[2].T)
    back_q = back_rows(0, 0)
    for load in loads[1:]:
        load.wait()
    both.scatter_second()
    last.scatter_second()

    for copy in back_attended:
        copy.wait_recv()
    total_ref[...] = dot(attended_ref[...], g_ref[...])
    half_ref[0] = total_ref[part(1 - core, ROWS[0]), :].astype(BF16)
    merge = remote(half_ref.at[0], half_ref.at[1], core_sems, 1, other)
    merge.start()
    sent.append(merge)

    spread = []
    for job, kinds in ((both, (0, 1)), (last, (2,))):
        value = job.scattered()
        for k, kind in enumerate(kinds):
            columns = pl.ds(pl.multiple_of(kind * width + y * 2 * HD, 2 * HD), 2 * HD)
            here = job.region(columns=columns)
            here[...] = value[:, k * 2 * HD : (k + 1) * 2 * HD]
            for offset in (2, 1, 3):
                spread.append(remote(here, here, (spread_send, spread_recv), (kind, offset - 1), along("y", offset)))
                spread[-1].start()
    sent.extend(spread)
    back_q += back_rows(0, 1)
    back_k = back_rows(1, 0)
    merge.wait_recv()
    merged = total_ref[part(core, ROWS[0]), :] + half_ref[1].astype(F32)
    left.scatter_first(merged[:, :half])
    right.scatter_first(merged[:, half:])
    back_k += back_rows(1, 1)

    left.scatter_second()
    right.scatter_second()
    for copy in spread:
        copy.wait_recv()
    both.gather()
    last.gather()
    left.exchange("y", y)
    right.exchange("y", y)
    back_v = back_rows(2, 0) + back_rows(2, 1)
    both.gather_on()
    last.gather_on()
    layer_ref[...] = (x_ref[...].astype(F32) + dot(attended_ref[...], wo_ref[...], TN)).astype(BF16)
    store(layer_ref, layer_hbm)
    for copy in back_q:
        copy.wait_recv()
    total_ref[...] = dot(wi_ref[:, :width], rows_ref[0])
    left.exchanged()
    right.exchanged()
    left.gather()
    right.gather()
    both.gathered()
    last.gathered()

    def share(source, target, index):
        mine = part(core, ROWS[0])
        copy = remote(source.at[mine, :], target.at[mine, :], core_sems, index, other)
        copy.start()
        store(source.at[mine, :], target.at[mine, :])
        sent.append(copy)
        return copy

    share_i = share(isum_ref, isum_hbm, 2)
    left.gather_on()
    right.gather_on()
    for copy in back_k:
        copy.wait_recv()
    total_ref[...] += dot(wi_ref[:, width : 2 * width], rows_ref[1])
    late = {id(copy) for copy in back_v}
    settled = [copy for copy in sent if id(copy) not in late]
    for job in (both, last, left, right):
        settled.extend(job.sent)
    for copy in settled + back_v:
        copy.wait_send()
    for copy in back_v:
        copy.wait_recv()
    turned = (total_ref[...] + dot(wi_ref[:, 2 * width :], rows_ref[2])).T
    gradf_ref[...] = (g_ref[...].astype(F32) + turned).astype(BF16)
    store(gradf_ref, gradf_hbm)
    left.gathered()
    right.gathered()
    share_o = share(osum_ref, osum_hbm, 3)
    share_o.wait_send()
    for copy in stores:
        copy.wait()
    share_i.wait_recv()
    share_o.wait_recv()


def finish(grads, weight, x, g, wi, wo):
    nodes, width = x.shape
    anywhere = pl.BlockSpec(memory_space=pl.ANY)
    columns = (4 * HD, 2 * HD, width // 2, width // 2)
    dma = pltpu.SemaphoreType.DMA
    results = [(nodes, width), (nodes, width), (width, width), (width, 3 * width)]
    return pl.pallas_call(
        finish_kernel,
        out_shape=tuple(jax.ShapeDtypeStruct(shape, BF16) for shape in results),
        in_specs=[anywhere] * 6,
        out_specs=(anywhere,) * 4,
        scratch_shapes=[pltpu.VMEM(shape, BF16) for shape in results]
        + [
            pltpu.VMEM(x.shape, BF16),
            pltpu.VMEM(g.shape, BF16),
            pltpu.VMEM(wi.shape, BF16),
            pltpu.VMEM(wo.shape, BF16),
            pltpu.VMEM((width, nodes), BF16),
            pltpu.VMEM((3, width, nodes), BF16),
            pltpu.VMEM((3, 2 * HD, ROWS[0]), F32),
            pltpu.VMEM((3, HD, ROWS[0]), F32),
            pltpu.VMEM((2, ROWS[0], width), BF16),
            pltpu.VMEM((width, nodes), F32),
        ]
        + [pltpu.VMEM((ROWS[0], n), F32) for n in columns]
        + [pltpu.VMEM((ROWS[0] + ROWS[1], n), BF16) for n in columns]
        + [pltpu.VMEM((SIDE - 1, ROWS[1], n), BF16) for n in columns]
        + [pltpu.VMEM((SIDE - 1, ROWS[2], n), BF16) for n in columns]
        + [pltpu.VMEM((SIDE, ROWS[2], n), BF16) for n in columns[2:]]
        + [dma((7, H - 1))] * 2
        + [dma((4,))] * 2
        + [dma((4, 8, SIDE - 1))] * 2
        + [dma((3, SIDE - 1))] * 2
        + [dma((7,)), dma((4,))],
        compiler_params=pltpu.CompilerParams(collective_id=1, has_side_effects=True, vmem_limit_bytes=VMEM_BYTES),
        name="finish",
    )(grads.reshape(4, HD, -1), weight.reshape(3, HD, -1), x, g, wi, wo)


def emit_kernel(factor, layer_ref, gradf_ref, osum_ref, isum_ref, layer_out, gradf_out, osum_out, isum_out):
    layer_out[...] = layer_ref[...]
    gradf_out[...] = gradf_ref[...]
    osum_out[...] = osum_ref[...].astype(F32) * factor
    isum_out[...] = isum_ref[...].astype(F32) * factor


def emit(layer, gradf, osum, isum, factor):
    arrays = (layer, gradf, osum, isum)
    kinds = (BF16, BF16, F32, F32)
    rows = layer.shape[0] // 2
    specs = [pl.BlockSpec((rows, a.shape[1]), lambda i: (i, 0)) for a in arrays]
    return pl.pallas_call(
        partial(emit_kernel, factor),
        grid=(2,),
        out_shape=tuple(jax.ShapeDtypeStruct(a.shape, kind) for a, kind in zip(arrays, kinds)),
        in_specs=specs,
        out_specs=tuple(specs),
        compiler_params=pltpu.CompilerParams(vmem_limit_bytes=VMEM_BYTES),
        name="emit",
    )(*arrays)


def shards(features, input_weight, output_weight, key_blocks, key_count, cotangent):
    x, g = features[0], cotangent[0]
    order, reach, everything, kv, kvt, qt, gt = project(x, g, input_weight, output_weight, key_count[0])
    grads, weight = attention(order, reach, key_blocks[0, 0].T, key_count[0, 0], kv, kvt, qt, gt, everything)
    results = finish(grads, weight, x, g, input_weight, output_weight)
    factor = 1.0 / (lax.axis_size("dp") * lax.axis_size("seq") * x.shape[0]) ** 0.5
    layer_out, grad_features, output_total, input_total = emit(*results, factor)
    return (layer_out[None], grad_features[None], input_total, output_total)


def solution(mesh):
    in_specs = (
        P("dp", "seq", None),
        P(),
        P(),
        P("dp", "seq", None, None),
        P("dp", "seq", None),
        P("dp", "seq", None),
    )
    out_specs = (P("dp", "seq", None), P("dp", "seq", None), P(), P())
    return jax.shard_map(shards, mesh=mesh, in_specs=in_specs, out_specs=out_specs, check_vma=False)
```

```python
from functools import partial

import jax
import jax.numpy as jnp
from jax import lax
from jax.experimental import pallas as pl
from jax.experimental.pallas import tpu as pltpu
from jax.sharding import PartitionSpec as P

H = 8
HD = 64
B = 128
KMAX = 8
NEGATIVE = -1e30
SCALE = HD**-0.5
MESH = pl.DeviceIdType.MESH
BF16 = jnp.bfloat16
F32 = jnp.float32
NN = (((1,), (0,)), ((), ()))
NT = (((1,), (1,)), ((), ()))
TN = (((0,), (0,)), ((), ()))
SIDE = 4
VMEM_BYTES = 60 << 20
CALM = 1600.0


def dot(a, b, dims=NN):
    return lax.dot_general(a, b, dims, preferred_element_type=F32)


def part(index, size):
    return pl.ds(pl.multiple_of(index * size, size), size)


def seq_peers(seq):
    y, core = seq // 2, seq % 2
    peers = []
    for dy in (2, 1, 3):
        for flip in (0, 1):
            peers.append(((y + dy) % SIDE) * 2 + (core + flip) % 2)
    peers.append(y * 2 + (core + 1) % 2)
    return peers


def greet(devices):
    barrier = pltpu.get_barrier_semaphore()
    for device in devices:
        pl.semaphore_signal(barrier, inc=1, device_id=device, device_id_type=MESH)
    pl.semaphore_wait(barrier, len(devices))


def remote(source, target, sems, index, device):
    return pltpu.make_async_remote_copy(
        src_ref=source,
        dst_ref=target,
        send_sem=sems[0].at[index],
        recv_sem=sems[1].at[index],
        device_id=device,
        device_id_type=MESH,
    )


def falling_order(counts):
    size = counts.shape[1]
    row = jnp.broadcast_to(counts.astype(F32), (size, size))
    here = lax.broadcasted_iota(jnp.int32, (size, size), 0)
    there = lax.broadcasted_iota(jnp.int32, (size, size), 1)
    column = jnp.sum(jnp.where(here == there, row, 0.0), 1, keepdims=True)
    ahead = (row > column) | ((row == column) & (there < here))
    rank = jnp.sum(jnp.where(ahead, 1.0, 0.0), 1, keepdims=True)
    found = jnp.where(rank == there.astype(F32), here.astype(F32), 0.0)
    return jnp.sum(found, 0, keepdims=True).astype(jnp.int32)


def project_kernel(
    x_hbm, g_hbm, wi_hbm, wo_hbm, count_ref,
    order_ref, reach_ref, all_hbm, kv_hbm, kvt_hbm, qt_hbm, gt_hbm,
    x_ref, kv_ref, kvt_ref, qt_ref, g_ref, wi_ref, wo_ref, grad_ref, send_sem, recv_sem, load_sem, store_sem,
):
    dp, seq = lax.axis_index("dp"), lax.axis_index("seq")
    y, core = seq // 2, seq % 2
    nodes, width = g_ref.shape
    half = nodes // 2
    sems = (send_sem, recv_sem)
    other = (dp, y * 2 + (core + 1) % 2)

    def at(dy, flip=0):
        return ((y + dy) % SIDE) * 2 + (core + flip) % 2

    peers = seq_peers(seq)
    loads = [
        pltpu.make_async_copy(source, target, load_sem.at[k])
        for k, (source, target) in enumerate(
            ((x_hbm, x_ref.at[seq]), (wi_hbm, wi_ref), (g_hbm, g_ref), (wo_hbm, wo_ref))
        )
    ]
    for load in loads:
        load.start()
    greet([(dp, peer) for peer in peers])
    up, down = (dp, at(1)), (dp, at(3))

    def rows(h):
        return pl.ds(h * half, half)

    def pass_on(source, h, index, device):
        piece = x_ref.at[source, rows(h)]
        return remote(piece, piece, sems, index, device)

    def own(h, index, device):
        return remote(x_hbm.at[rows(h)], x_ref.at[seq, rows(h)], sems, index, device)

    sent = [own(0, 0, up), own(1, 3, down), own(1, 1, up), own(0, 4, down), own(0, 6, other), own(1, 7, other)]
    for copy in sent:
        copy.start()

    loads[0].wait()
    loads[1].wait()
    chosen = []
    for kind in (1, 2, 0):
        block = wi_ref[:, pl.ds(pl.multiple_of(kind * width + y * 2 * HD, 2 * HD), 2 * HD)]
        chosen.append(jnp.where(core == 0, block[:, :HD], block[:, HD:]))
    chosen[2] = chosen[2] * jnp.asarray(SCALE, BF16)
    weights = jnp.concatenate(chosen + [jnp.zeros_like(chosen[0])], 1)
    stores, largest = [], [None, None]

    def store(source, target):
        stores.append(pltpu.make_async_copy(source, target, store_sem.at[len(stores)]))
        stores[-1].start()

    def project_half(source, h):
        here = part(2 * source + h, half)
        product = dot(x_ref[source, rows(h), :], weights)
        kv = product[:, : 2 * HD].astype(BF16)
        kvt, qt = kv.T, product[:, 2 * HD :].T[:HD].astype(BF16)
        kv_ref[here, :] = kv
        kvt_ref[:, here] = kvt
        qt_ref[:, here] = qt
        for k, rows_of in enumerate((kvt[:HD], qt)):
            norms = jnp.sum(jnp.square(rows_of.astype(F32)), 0, keepdims=True)
            largest[k] = norms if largest[k] is None else jnp.maximum(largest[k], norms)
        store(x_ref.at[source, rows(h)], all_hbm.at[here, :])
        store(kv_ref.at[here, :], kv_hbm.at[here, :])
        store(kvt_ref.at[:, here], kvt_hbm.at[:, here])
        store(qt_ref.at[:, here], qt_hbm.at[:, here])

    project_half(seq, 0)
    project_half(seq, 1)
    loads[2].wait()
    loads[3].wait()
    grad_ref[...] = dot(wo_ref[...], g_ref[...], NT).astype(BF16)
    store(grad_ref.at[part(seq, HD), :], gt_hbm.at[:, part(seq, nodes)])
    order_ref[...] = falling_order(count_ref[...])
    low, high, far = at(3), at(1), at(2)
    forwards = {0: pass_on(low, 0, 2, up), 3: pass_on(high, 1, 5, down)}
    shares = {0: (low, 0, 8), 3: (high, 1, 9), 1: (low, 1, 10), 4: (high, 0, 11), 2: (far, 0, 12), 5: (far, 1, 13)}
    ring = {index: own(0, index, up) for index in (0, 1, 2, 3, 4, 5)}
    near = {index: own(0, index, other) for index in range(6, 14)}

    def arrive(index):
        ring[index].wait_recv()
        source, h, share = shares[index]
        for copy in [forwards[index]] if index in forwards else []:
            copy.start()
            sent.append(copy)
        sent.append(pass_on(source, h, share, other))
        sent[-1].start()

    def project_arrived(index):
        project_half(*shares[index][:2])

    def arrive_near(share, source, h):
        near[share].wait_recv()
        project_half(source, h)

    arrive_near(6, at(0, 1), 0)
    arrive_near(7, at(0, 1), 1)
    arrive(0)
    arrive(3)
    given = []
    for place, peer in enumerate(peers):
        given.append(
            remote(grad_ref.at[part(peer, HD), :], gt_hbm.at[:, part(seq, nodes)], sems, 14 + place, (dp, peer))
        )
        given[-1].start()
    project_arrived(0)
    project_arrived(3)
    arrive_near(8, at(3, 1), 0)
    arrive_near(9, at(1, 1), 1)
    arrive(1)
    arrive(4)
    project_arrived(1)
    project_arrived(4)
    arrive_near(10, at(3, 1), 1)
    arrive_near(11, at(1, 1), 0)
    arrive(2)
    arrive(5)
    project_arrived(2)
    project_arrived(5)
    arrive_near(12, at(2, 1), 0)
    arrive_near(13, at(2, 1), 1)
    reach = jnp.max(largest[0], 1, keepdims=True) * jnp.max(largest[1], 1, keepdims=True)
    reach_ref[...] = jnp.broadcast_to(reach, reach_ref.shape)
    for copy in sent:
        copy.wait_send()
    for copy in stores:
        copy.wait()
    for copy in given:
        copy.wait_send()
    for copy in given:
        copy.wait_recv()


def project(x, g, wi, wo, counts):
    nodes, width = x.shape
    span = nodes * H
    vm = pl.BlockSpec(memory_space=pltpu.VMEM)
    anywhere = pl.BlockSpec(memory_space=pl.ANY)
    dma = pltpu.SemaphoreType.DMA
    return pl.pallas_call(
        project_kernel,
        out_shape=(
            jax.ShapeDtypeStruct(counts.shape, jnp.int32),
            jax.ShapeDtypeStruct((1, B), F32),
            jax.ShapeDtypeStruct((span, width), BF16),
            jax.ShapeDtypeStruct((span, 2 * HD), BF16),
            jax.ShapeDtypeStruct((2 * HD, span), BF16),
            jax.ShapeDtypeStruct((HD, span), BF16),
            jax.ShapeDtypeStruct((HD, span), BF16),
        ),
        in_specs=[anywhere] * 4 + [vm],
        out_specs=(vm, vm) + (anywhere,) * 5,
        scratch_shapes=[
            pltpu.VMEM((H, nodes, width), BF16),
            pltpu.VMEM((span, 2 * HD), BF16),
            pltpu.VMEM((2 * HD, span), BF16),
            pltpu.VMEM((HD, span), BF16),
            pltpu.VMEM(g.shape, BF16),
            pltpu.VMEM(wi.shape, BF16),
            pltpu.VMEM(wo.shape, BF16),
            pltpu.VMEM((width, nodes), BF16),
            dma((21,)),
            dma((21,)),
            dma((4,)),
            dma((8 * H + 1,)),
        ],
        compiler_params=pltpu.CompilerParams(collective_id=0, has_side_effects=True, vmem_limit_bytes=VMEM_BYTES),
        name="project",
    )(x, g, wi, wo, counts)


def attention_kernel(
    group, order_ref, reach_ref, blocks_ref, counts_ref, kv_hbm, kvt_hbm, qt_hbm, gt_hbm, all_hbm, grads_hbm, weight_hbm,
    kv_ref, kvt_ref, qt_ref, gt_ref, all_ref, grads_ref, weight_ref, total_ref, load_sem, store_sem,
):
    block_count = kvt_ref.shape[1] // B
    loads = [
        pltpu.make_async_copy(source, target, load_sem.at[k])
        for k, (source, target) in enumerate(
            ((kv_hbm, kv_ref), (qt_hbm, qt_ref), (gt_hbm, gt_ref), (kvt_hbm, kvt_ref), (all_hbm, all_ref))
        )
    ]
    for load in loads:
        load.start()
    total_ref[...] = jnp.zeros_like(total_ref)
    for load in loads[:4]:
        load.wait()
    zero = jnp.zeros((HD, B), BF16)

    def query_blocks(ids, live, shifted):
        heres = [pl.ds(pl.multiple_of(i * B, B), B) for i in ids]
        spots = [[pl.ds(pl.multiple_of(blocks_ref[j, i] * B, B), B) for j in range(live)] for i in ids]
        aparts, products = [], []
        for here, chosen in zip(heres, spots):
            apart = jnp.concatenate(
                [jnp.concatenate([qt_ref[:, here], zero], 1), jnp.concatenate([zero, gt_ref[:, here]], 1)], 0
            )
            aparts.append(apart)
            products.append(dot(jnp.concatenate([kv_ref[spot, :] for spot in chosen], 0), apart))
        pairs = []
        for i, product in zip(ids, products):
            count = counts_ref[i]
            scores = [product[:B, :B]]
            for j in range(1, live):
                scores.append(product[j * B : (j + 1) * B, :B] + jnp.where(j < count, 0.0, NEGATIVE))
            scores = jnp.concatenate(scores, 0)
            grad_probs = product[:, B:]
            if shifted:
                scores = scores - jnp.max(scores, 0, keepdims=True)
            raised = jnp.exp(scores)
            inverse = 1.0 / jnp.sum(raised, 0, keepdims=True)
            row_delta = jnp.sum(raised * grad_probs, 0, keepdims=True) * inverse
            probs = raised * inverse
            grad_scores = (probs * (grad_probs - row_delta)).astype(BF16)
            pairs.append(jnp.concatenate([grad_scores, probs.astype(BF16)], 1))
        outs, terms = [], []
        for apart, chosen, pair in zip(aparts, spots, pairs):
            outs.append(dot(jnp.concatenate([kvt_ref[:, spot] for spot in chosen], 1), pair))
            terms.append(dot(apart, pair, NT))
        for here, out in zip(heres, outs):
            grads_ref[0:HD, here] = out[HD:, B:].astype(BF16)
            grads_ref[HD : 2 * HD, here] = (out[:HD, :B] * SCALE).astype(BF16)
        for chosen, term in zip(spots, terms):
            for j, spot in enumerate(chosen):
                total_ref[:, spot] += term[:, j * B : (j + 1) * B]

    def step(index, carry):
        ids = [order_ref[0, index * group + t] for t in range(group)]
        most = counts_ref[ids[0]]
        for live in range(1, KMAX + 1):
            pl.when(most == live)(partial(query_blocks, ids, live, False))
        return carry

    def step_shifted(index, carry):
        query_blocks([index], KMAX, True)
        return carry

    calm = reach_ref[0, 0] <= CALM

    @pl.when(calm)
    def _():
        lax.fori_loop(0, block_count // group, step, 0)

    @pl.when(jnp.logical_not(calm))
    def _():
        lax.fori_loop(0, block_count, step_shifted, 0)

    stores = [
        pltpu.make_async_copy(source, target, store_sem.at[k])
        for k, (source, target) in enumerate(
            (
                (grads_ref.at[pl.ds(0, 2 * HD), :], grads_hbm.at[pl.ds(0, 2 * HD), :]),
                (grads_ref.at[pl.ds(2 * HD, 2 * HD), :], grads_hbm.at[pl.ds(2 * HD, 2 * HD), :]),
                (weight_ref, weight_hbm),
            )
        )
    ]
    stores[0].start()
    grads_ref[2 * HD :, :] = total_ref[...].astype(BF16)
    stores[1].start()
    loads[4].wait()
    weight_ref[...] = dot(grads_ref[HD:, :], all_ref[...])
    stores[2].start()
    for store in stores:
        store.wait()


def attention(order, reach, blocks, counts, *arrays):
    span, width = arrays[-1].shape
    sm = pl.BlockSpec(memory_space=pltpu.SMEM)
    anywhere = pl.BlockSpec(memory_space=pl.ANY)
    results = (jax.ShapeDtypeStruct((4 * HD, span), BF16), jax.ShapeDtypeStruct((3 * HD, width), F32))
    return pl.pallas_call(
        partial(attention_kernel, 4),
        out_shape=results,
        in_specs=[sm] * 4 + [anywhere] * len(arrays),
        out_specs=(anywhere,) * 2,
        scratch_shapes=[pltpu.VMEM(a.shape, a.dtype) for a in arrays + results]
        + [
            pltpu.VMEM((2 * HD, span), F32),
            pltpu.SemaphoreType.DMA((len(arrays),)),
            pltpu.SemaphoreType.DMA((3,)),
        ],
        compiler_params=pltpu.CompilerParams(vmem_limit_bytes=VMEM_BYTES),
        name="attention",
    )(order, reach, blocks, counts, *arrays)


ROWS = (256, 64, 16)


class Sum:
    def __init__(self, number, axes, columns, whole, sems, scratch, along, place_of, core):
        self.number, self.axes, self.columns, self.whole, self.sems = number, axes, columns, whole, sems
        self.total, self.out, self.quarters, self.parts, self.levels = scratch
        self.along = along
        self.place = [place_of[axis] for axis in axes]
        self.core = core
        self.waiting, self.sent = {}, []

    def send(self, phase, axis, source, target):
        copies = {}
        for offset in (2, 1, 3):
            copies[offset] = remote(
                source(offset), target(offset), self.sems, (self.number, phase, offset - 1), self.along(axis, offset)
            )
            copies[offset].start()
        self.waiting[phase] = copies
        self.sent += copies.values()

    def arrive(self, *phases):
        for phase in phases:
            for copy in self.waiting[phase].values():
                copy.wait_recv()

    def scatter_first(self, value):
        self.total[...] = value
        self.out[0 : ROWS[0], :] = value.astype(BF16)
        spot = lambda offset: part((self.place[0] + offset) % SIDE, ROWS[1])
        self.send(0, self.axes[0], lambda o: self.out.at[spot(o), :], lambda o: self.quarters.at[o - 1])

    def scatter_second(self):
        self.arrive(0)
        value = self.total[part(self.place[0], ROWS[1]), :] + self.quarters[0].astype(F32)
        value += self.quarters[1].astype(F32) + self.quarters[2].astype(F32)
        self.total[0 : ROWS[1], :] = value
        self.out[ROWS[0] :, :] = value.astype(BF16)
        spot = lambda offset: part(ROWS[0] // ROWS[2] + (self.place[1] + offset) % SIDE, ROWS[2])
        self.send(1, self.axes[1], lambda o: self.out.at[spot(o), :], lambda o: self.parts.at[o - 1])

    def scattered(self):
        self.arrive(1)
        value = self.total[part(self.place[1], ROWS[2]), :] + self.parts[0].astype(F32)
        return (value + (self.parts[1].astype(F32) + self.parts[2].astype(F32))).astype(BF16)

    def exchange(self, axis, place):
        self.levels[place] = self.scattered()
        here = self.levels.at[place]
        self.send(2, axis, lambda o: here, lambda o: here)

    def exchanged(self):
        self.arrive(2)
        value = [self.levels[k].astype(F32) for k in range(SIDE)]
        self.region()[...] = ((value[0] + value[1]) + (value[2] + value[3])).astype(BF16)

    def region(self, second=None, columns=None):
        second = self.place[1] if second is None else second
        first = self.core * ROWS[0] + self.place[0] * ROWS[1] + second * ROWS[2]
        rows = pl.ds(pl.multiple_of(first, ROWS[2]), ROWS[2])
        return self.whole.at[rows, self.columns if columns is None else columns]

    def gather(self):
        here = self.region()
        self.send(3, self.axes[1], lambda o: here, lambda o: here)
        self.send(4, self.axes[0], lambda o: here, lambda o: here)

    def gather_on(self):
        for offset, copy in self.waiting[3].items():
            copy.wait_recv()
            here = self.region((self.place[1] + SIDE - offset) % SIDE)
            self.send(4 + offset, self.axes[0], lambda o: here, lambda o: here)

    def gathered(self):
        self.arrive(4, 5, 6, 7)


def finish_kernel(
    grads_hbm, weight_hbm, x_hbm, g_hbm, wi_hbm, wo_hbm,
    layer_hbm, gradf_hbm, osum_hbm, isum_hbm,
    layer_ref, gradf_ref, osum_ref, isum_ref,
    x_ref, g_ref, wi_ref, wo_ref, attended_ref, rows_ref, merged_ref, theirs_ref, half_ref, total_ref,
    tot_a, tot_b, tot_c, tot_d, out_a, out_b, out_c, out_d, quarters_a, quarters_b, quarters_c, quarters_d,
    parts_a, parts_b, parts_c, parts_d, levels_c, levels_d,
    seq_send, seq_recv, core_send, core_recv, sum_send, sum_recv, spread_send, spread_recv, load_sem, store_sem,
):
    dp, seq = lax.axis_index("dp"), lax.axis_index("seq")
    z, x, y, core = dp // SIDE, dp % SIDE, seq // 2, seq % 2
    place_of = {"x": x, "y": y, "z": z}
    nodes, width = x_ref.shape
    half = nodes // 2
    other = (dp, y * 2 + (core + 1) % 2)
    seq_sems, core_sems = (seq_send, seq_recv), (core_send, core_recv)

    def along(axis, offset):
        if axis == "y":
            return (dp, ((y + offset) % SIDE) * 2 + core)
        if axis == "x":
            return (z * SIDE + (x + offset) % SIDE, seq)
        return (((z + offset) % SIDE) * SIDE + x, seq)

    loads = [
        pltpu.make_async_copy(source, target, load_sem.at[k])
        for k, (source, target) in enumerate(
            (
                (weight_hbm.at[:, :, part(core, ROWS[0])], merged_ref.at[:, part(core, HD), :]),
                (grads_hbm.at[0, :, part(seq, nodes)], attended_ref.at[part(seq, HD), :]),
                (g_hbm, g_ref),
                (x_hbm, x_ref),
                (wo_hbm, wo_ref),
                (wi_hbm, wi_ref),
                (grads_hbm.at[pl.ds(1, 3), :, part(seq, nodes)], rows_ref.at[:, part(seq, HD), :]),
            )
        )
    ]
    for load in loads:
        load.start()
    peers = seq_peers(seq)
    greet([(dp, peer) for peer in peers] + [along(axis, offset) for axis in ("x", "z") for offset in (1, 2, 3)])

    sent, stores = [], []

    def store(source, target):
        stores.append(pltpu.make_async_copy(source, target, store_sem.at[len(stores)]))
        stores[-1].start()

    def back(piece, source, target):
        copies = []
        for place, peer in enumerate(peers):
            copies.append(remote(source(peer), target, seq_sems, (piece, place), (dp, peer)))
            copies[-1].start()
        sent.extend(copies)
        return copies

    def back_rows(kind, h):
        mine = pl.ds(h * half, half)
        return back(
            1 + 2 * kind + h,
            lambda peer: grads_hbm.at[1 + kind, :, part(2 * peer + h, half)],
            rows_ref.at[kind, part(seq, HD), mine],
        )

    swap = remote(weight_hbm.at[:, :, part(1 - core, ROWS[0])], theirs_ref, core_sems, 0, other)
    swap.start()
    sent.append(swap)
    back_attended = back(0, lambda peer: grads_hbm.at[0, :, part(peer, nodes)], attended_ref.at[part(seq, HD), :])

    sums = (sum_send, sum_recv)
    make = lambda *args: Sum(*args, along, place_of, core)
    both = make(0, ("z", "x"), pl.ds(0, 2 * width), isum_ref, sums, (tot_a, out_a, quarters_a, parts_a, None))
    last = make(1, ("x", "z"), pl.ds(2 * width, width), isum_ref, sums, (tot_b, out_b, quarters_b, parts_b, None))
    left = make(2, ("x", "z"), pl.ds(0, half), osum_ref, sums, (tot_c, out_c, quarters_c, parts_c, levels_c))
    right = make(3, ("z", "x"), pl.ds(half, half), osum_ref, sums, (tot_d, out_d, quarters_d, parts_d, levels_d))

    loads[0].wait()
    swap.wait_recv()
    merged_ref[:, part(1 - core, HD), :] = theirs_ref[...]
    both.scatter_first(jnp.concatenate([merged_ref[0].T, merged_ref[1].T], 1))
    last.scatter_first(merged_ref[2].T)
    back_q = back_rows(0, 0) + back_rows(0, 1)
    for load in loads[1:]:
        load.wait()
    both.scatter_second()
    last.scatter_second()

    for copy in back_attended:
        copy.wait_recv()
    half_ref[0] = dot(attended_ref[part(1 - core, ROWS[0]), :], g_ref[...]).astype(BF16)
    merge = remote(half_ref.at[0], half_ref.at[1], core_sems, 1, other)
    merge.start()
    sent.append(merge)
    total_ref[0 : ROWS[0], :] = dot(attended_ref[part(core, ROWS[0]), :], g_ref[...])

    merge.wait_recv()
    merged = total_ref[0 : ROWS[0], :] + half_ref[1].astype(F32)
    left.scatter_first(merged[:, :half])
    right.scatter_first(merged[:, half:])

    spread = []
    for job, kinds in ((both, (0, 1)), (last, (2,))):
        value = job.scattered()
        for k, kind in enumerate(kinds):
            columns = pl.ds(pl.multiple_of(kind * width + y * 2 * HD, 2 * HD), 2 * HD)
            here = job.region(columns=columns)
            here[...] = value[:, k * 2 * HD : (k + 1) * 2 * HD]
            for offset in (2, 1, 3):
                spread.append(remote(here, here, (spread_send, spread_recv), (kind, offset - 1), along("y", offset)))
                spread[-1].start()
    sent.extend(spread)
    back_k = back_rows(1, 0) + back_rows(1, 1)
    left.scatter_second()
    right.scatter_second()
    for copy in spread:
        copy.wait_recv()
    both.gather()
    last.gather()
    left.exchange("y", y)
    right.exchange("y", y)
    back_v = back_rows(2, 0) + back_rows(2, 1)
    both.gather_on()
    last.gather_on()
    layer_ref[...] = (x_ref[...].astype(F32) + dot(attended_ref[...], wo_ref[...], TN)).astype(BF16)
    store(layer_ref, layer_hbm)
    for copy in back_q:
        copy.wait_recv()
    total_ref[...] = dot(wi_ref[:, :width], rows_ref[0])
    left.exchanged()
    right.exchanged()
    left.gather()
    right.gather()
    both.gathered()
    last.gathered()

    def share(source, target, index):
        mine = part(core, ROWS[0])
        copy = remote(source.at[mine, :], target.at[mine, :], core_sems, index, other)
        copy.start()
        store(source.at[mine, :], target.at[mine, :])
        sent.append(copy)
        return copy

    share_i = share(isum_ref, isum_hbm, 2)
    left.gather_on()
    right.gather_on()
    for copy in back_k:
        copy.wait_recv()
    total_ref[...] += dot(wi_ref[:, width : 2 * width], rows_ref[1])
    late = {id(copy) for copy in back_v}
    settled = [copy for copy in sent if id(copy) not in late]
    for job in (both, last, left, right):
        settled.extend(job.sent)
    for copy in settled + back_v:
        copy.wait_send()
    for copy in back_v:
        copy.wait_recv()
    turned = (total_ref[...] + dot(wi_ref[:, 2 * width :], rows_ref[2])).T
    gradf_ref[...] = (g_ref[...].astype(F32) + turned).astype(BF16)
    store(gradf_ref, gradf_hbm)
    left.gathered()
    right.gathered()
    share_o = share(osum_ref, osum_hbm, 3)
    share_o.wait_send()
    for copy in stores:
        copy.wait()
    share_i.wait_recv()
    share_o.wait_recv()


def finish(grads, weight, x, g, wi, wo):
    nodes, width = x.shape
    anywhere = pl.BlockSpec(memory_space=pl.ANY)
    columns = (4 * HD, 2 * HD, width // 2, width // 2)
    dma = pltpu.SemaphoreType.DMA
    results = [(nodes, width), (nodes, width), (width, width), (width, 3 * width)]
    return pl.pallas_call(
        finish_kernel,
        out_shape=tuple(jax.ShapeDtypeStruct(shape, BF16) for shape in results),
        in_specs=[anywhere] * 6,
        out_specs=(anywhere,) * 4,
        scratch_shapes=[pltpu.VMEM(shape, BF16) for shape in results]
        + [
            pltpu.VMEM(x.shape, BF16),
            pltpu.VMEM(g.shape, BF16),
            pltpu.VMEM(wi.shape, BF16),
            pltpu.VMEM(wo.shape, BF16),
            pltpu.VMEM((width, nodes), BF16),
            pltpu.VMEM((3, width, nodes), BF16),
            pltpu.VMEM((3, 2 * HD, ROWS[0]), F32),
            pltpu.VMEM((3, HD, ROWS[0]), F32),
            pltpu.VMEM((2, ROWS[0], width), BF16),
            pltpu.VMEM((width, nodes), F32),
        ]
        + [pltpu.VMEM((ROWS[0], n), F32) for n in columns]
        + [pltpu.VMEM((ROWS[0] + ROWS[1], n), BF16) for n in columns]
        + [pltpu.VMEM((SIDE - 1, ROWS[1], n), BF16) for n in columns]
        + [pltpu.VMEM((SIDE - 1, ROWS[2], n), BF16) for n in columns]
        + [pltpu.VMEM((SIDE, ROWS[2], n), BF16) for n in columns[2:]]
        + [dma((7, H - 1))] * 2
        + [dma((4,))] * 2
        + [dma((4, 8, SIDE - 1))] * 2
        + [dma((3, SIDE - 1))] * 2
        + [dma((7,)), dma((4,))],
        compiler_params=pltpu.CompilerParams(collective_id=1, has_side_effects=True, vmem_limit_bytes=VMEM_BYTES),
        name="finish",
    )(grads.reshape(4, HD, -1), weight.reshape(3, HD, -1), x, g, wi, wo)


def emit_kernel(factor, layer_ref, gradf_ref, osum_ref, isum_ref, layer_out, gradf_out, osum_out, isum_out):
    layer_out[...] = layer_ref[...]
    gradf_out[...] = gradf_ref[...]
    osum_out[...] = osum_ref[...].astype(F32) * factor
    isum_out[...] = isum_ref[...].astype(F32) * factor


def emit(layer, gradf, osum, isum, factor):
    arrays = (layer, gradf, osum, isum)
    kinds = (BF16, BF16, F32, F32)
    rows = layer.shape[0] // 2
    specs = [pl.BlockSpec((rows, a.shape[1]), lambda i: (i, 0)) for a in arrays]
    return pl.pallas_call(
        partial(emit_kernel, factor),
        grid=(2,),
        out_shape=tuple(jax.ShapeDtypeStruct(a.shape, kind) for a, kind in zip(arrays, kinds)),
        in_specs=specs,
        out_specs=tuple(specs),
        compiler_params=pltpu.CompilerParams(vmem_limit_bytes=VMEM_BYTES),
        name="emit",
    )(*arrays)


def shards(features, input_weight, output_weight, key_blocks, key_count, cotangent):
    x, g = features[0], cotangent[0]
    order, reach, everything, kv, kvt, qt, gt = project(x, g, input_weight, output_weight, key_count[0])
    grads, weight = attention(order, reach, key_blocks[0, 0].T, key_count[0, 0], kv, kvt, qt, gt, everything)
    results = finish(grads, weight, x, g, input_weight, output_weight)
    factor = 1.0 / (lax.axis_size("dp") * lax.axis_size("seq") * x.shape[0]) ** 0.5
    layer_out, grad_features, output_total, input_total = emit(*results, factor)
    return (layer_out[None], grad_features[None], input_total, output_total)


def solution(mesh):
    in_specs = (
        P("dp", "seq", None),
        P(),
        P(),
        P("dp", "seq", None, None),
        P("dp", "seq", None),
        P("dp", "seq", None),
    )
    out_specs = (P("dp", "seq", None), P("dp", "seq", None), P(), P())
    return jax.shard_map(shards, mesh=mesh, in_specs=in_specs, out_specs=out_specs, check_vma=False)
```

```python
from functools import partial

import jax
import jax.numpy as jnp
from jax import lax
from jax.experimental import pallas as pl
from jax.experimental.pallas import tpu as pltpu
from jax.sharding import PartitionSpec as P

H = 8
HD = 64
B = 128
KMAX = 8
NEGATIVE = -1e30
SCALE = HD**-0.5
MESH = pl.DeviceIdType.MESH
BF16 = jnp.bfloat16
F32 = jnp.float32
NN = (((1,), (0,)), ((), ()))
NT = (((1,), (1,)), ((), ()))
TN = (((0,), (0,)), ((), ()))
SIDE = 4
VMEM_BYTES = 60 << 20
CALM = 1600.0


def dot(a, b, dims=NN):
    return lax.dot_general(a, b, dims, preferred_element_type=F32)


def part(index, size):
    return pl.ds(pl.multiple_of(index * size, size), size)


def seq_peers(seq):
    y, core = seq // 2, seq % 2
    peers = []
    for dy in (2, 1, 3):
        for flip in (0, 1):
            peers.append(((y + dy) % SIDE) * 2 + (core + flip) % 2)
    peers.append(y * 2 + (core + 1) % 2)
    return peers


def greet(devices):
    barrier = pltpu.get_barrier_semaphore()
    for device in devices:
        pl.semaphore_signal(barrier, inc=1, device_id=device, device_id_type=MESH)
    return partial(pl.semaphore_wait, barrier, len(devices))


def remote(source, target, sems, index, device):
    return pltpu.make_async_remote_copy(
        src_ref=source,
        dst_ref=target,
        send_sem=sems[0].at[index],
        recv_sem=sems[1].at[index],
        device_id=device,
        device_id_type=MESH,
    )


def falling_order(counts):
    size = counts.shape[1]
    row = jnp.broadcast_to(counts.astype(F32), (size, size))
    here = lax.broadcasted_iota(jnp.int32, (size, size), 0)
    there = lax.broadcasted_iota(jnp.int32, (size, size), 1)
    column = jnp.sum(jnp.where(here == there, row, 0.0), 1, keepdims=True)
    ahead = (row > column) | ((row == column) & (there < here))
    rank = jnp.sum(jnp.where(ahead, 1.0, 0.0), 1, keepdims=True)
    found = jnp.where(rank == there.astype(F32), here.astype(F32), 0.0)
    return jnp.sum(found, 0, keepdims=True).astype(jnp.int32)


def project_kernel(
    x_hbm, g_hbm, wi_hbm, wo_hbm, count_ref,
    order_ref, reach_ref, all_hbm, kv_hbm, kvt_hbm, qt_hbm, gt_hbm,
    x_ref, kv_ref, kvt_ref, qt_ref, g_ref, wi_ref, wo_ref, grad_ref, send_sem, recv_sem, load_sem, store_sem,
):
    dp, seq = lax.axis_index("dp"), lax.axis_index("seq")
    y, core = seq // 2, seq % 2
    nodes, width = g_ref.shape
    half = nodes // 2
    sems = (send_sem, recv_sem)
    other = (dp, y * 2 + (core + 1) % 2)

    def at(dy, flip=0):
        return ((y + dy) % SIDE) * 2 + (core + flip) % 2

    peers = seq_peers(seq)
    met = greet([(dp, peer) for peer in peers])
    loads = [
        pltpu.make_async_copy(source, target, load_sem.at[k])
        for k, (source, target) in enumerate(
            ((x_hbm, x_ref.at[seq]), (wi_hbm, wi_ref), (g_hbm, g_ref), (wo_hbm, wo_ref))
        )
    ]
    for load in loads:
        load.start()
    met()
    up, down = (dp, at(1)), (dp, at(3))

    def rows(h):
        return pl.ds(h * half, half)

    def pass_on(source, h, index, device):
        piece = x_ref.at[source, rows(h)]
        return remote(piece, piece, sems, index, device)

    def own(h, index, device):
        return remote(x_hbm.at[rows(h)], x_ref.at[seq, rows(h)], sems, index, device)

    sent = [own(0, 0, up), own(1, 3, down), own(1, 1, up), own(0, 4, down), own(0, 6, other), own(1, 7, other)]
    for copy in sent:
        copy.start()

    loads[0].wait()
    loads[1].wait()
    chosen = []
    for kind in (1, 2, 0):
        block = wi_ref[:, pl.ds(pl.multiple_of(kind * width + y * 2 * HD, 2 * HD), 2 * HD)]
        chosen.append(jnp.where(core == 0, block[:, :HD], block[:, HD:]))
    chosen[2] = chosen[2] * jnp.asarray(SCALE, BF16)
    weights = jnp.concatenate(chosen + [jnp.zeros_like(chosen[0])], 1)
    stores, largest = [], [None, None]

    def store(source, target):
        stores.append(pltpu.make_async_copy(source, target, store_sem.at[len(stores)]))
        stores[-1].start()

    def project_half(source, h):
        here = part(2 * source + h, half)
        product = dot(x_ref[source, rows(h), :], weights)
        kv = product[:, : 2 * HD].astype(BF16)
        kvt, qt = kv.T, product[:, 2 * HD :].T[:HD].astype(BF16)
        kv_ref[here, :] = kv
        kvt_ref[:, here] = kvt
        qt_ref[:, here] = qt
        for k, rows_of in enumerate((kvt[:HD], qt)):
            norms = jnp.sum(jnp.square(rows_of.astype(F32)), 0, keepdims=True)
            largest[k] = norms if largest[k] is None else jnp.maximum(largest[k], norms)
        store(x_ref.at[source, rows(h)], all_hbm.at[here, :])
        store(kv_ref.at[here, :], kv_hbm.at[here, :])
        store(kvt_ref.at[:, here], kvt_hbm.at[:, here])
        store(qt_ref.at[:, here], qt_hbm.at[:, here])

    project_half(seq, 0)
    project_half(seq, 1)
    loads[2].wait()
    loads[3].wait()
    grad_ref[...] = dot(wo_ref[...], g_ref[...], NT).astype(BF16)
    store(grad_ref.at[part(seq, HD), :], gt_hbm.at[:, part(seq, nodes)])
    order_ref[...] = falling_order(count_ref[...])
    low, high, far = at(3), at(1), at(2)
    forwards = {0: pass_on(low, 0, 2, up), 3: pass_on(high, 1, 5, down)}
    shares = {0: (low, 0, 8), 3: (high, 1, 9), 1: (low, 1, 10), 4: (high, 0, 11), 2: (far, 0, 12), 5: (far, 1, 13)}
    ring = {index: own(0, index, up) for index in (0, 1, 2, 3, 4, 5)}
    near = {index: own(0, index, other) for index in range(6, 14)}

    def arrive(index):
        ring[index].wait_recv()
        source, h, share = shares[index]
        for copy in [forwards[index]] if index in forwards else []:
            copy.start()
            sent.append(copy)
        sent.append(pass_on(source, h, share, other))
        sent[-1].start()

    def project_arrived(index):
        project_half(*shares[index][:2])

    def arrive_near(share, source, h):
        near[share].wait_recv()
        project_half(source, h)

    arrive_near(6, at(0, 1), 0)
    arrive_near(7, at(0, 1), 1)
    arrive(0)
    arrive(3)
    given = []
    for place, peer in enumerate(peers):
        given.append(
            remote(grad_ref.at[part(peer, HD), :], gt_hbm.at[:, part(seq, nodes)], sems, 14 + place, (dp, peer))
        )
        given[-1].start()
    project_arrived(0)
    project_arrived(3)
    arrive_near(8, at(3, 1), 0)
    arrive_near(9, at(1, 1), 1)
    arrive(1)
    arrive(4)
    project_arrived(1)
    project_arrived(4)
    arrive_near(10, at(3, 1), 1)
    arrive_near(11, at(1, 1), 0)
    arrive(2)
    arrive(5)
    project_arrived(2)
    project_arrived(5)
    arrive_near(12, at(2, 1), 0)
    arrive_near(13, at(2, 1), 1)
    reach = jnp.max(largest[0], 1, keepdims=True) * jnp.max(largest[1], 1, keepdims=True)
    reach_ref[...] = jnp.broadcast_to(reach, reach_ref.shape)
    for copy in sent:
        copy.wait_send()
    for copy in stores:
        copy.wait()
    for copy in given:
        copy.wait_send()
    for copy in given:
        copy.wait_recv()


def project(x, g, wi, wo, counts):
    nodes, width = x.shape
    span = nodes * H
    vm = pl.BlockSpec(memory_space=pltpu.VMEM)
    anywhere = pl.BlockSpec(memory_space=pl.ANY)
    dma = pltpu.SemaphoreType.DMA
    return pl.pallas_call(
        project_kernel,
        out_shape=(
            jax.ShapeDtypeStruct(counts.shape, jnp.int32),
            jax.ShapeDtypeStruct((1, B), F32),
            jax.ShapeDtypeStruct((span, width), BF16),
            jax.ShapeDtypeStruct((span, 2 * HD), BF16),
            jax.ShapeDtypeStruct((2 * HD, span), BF16),
            jax.ShapeDtypeStruct((HD, span), BF16),
            jax.ShapeDtypeStruct((HD, span), BF16),
        ),
        in_specs=[anywhere] * 4 + [vm],
        out_specs=(vm, vm) + (anywhere,) * 5,
        scratch_shapes=[
            pltpu.VMEM((H, nodes, width), BF16),
            pltpu.VMEM((span, 2 * HD), BF16),
            pltpu.VMEM((2 * HD, span), BF16),
            pltpu.VMEM((HD, span), BF16),
            pltpu.VMEM(g.shape, BF16),
            pltpu.VMEM(wi.shape, BF16),
            pltpu.VMEM(wo.shape, BF16),
            pltpu.VMEM((width, nodes), BF16),
            dma((21,)),
            dma((21,)),
            dma((4,)),
            dma((8 * H + 1,)),
        ],
        compiler_params=pltpu.CompilerParams(collective_id=0, has_side_effects=True, vmem_limit_bytes=VMEM_BYTES),
        name="project",
    )(x, g, wi, wo, counts)


def attention_kernel(
    group, order_ref, reach_ref, blocks_ref, counts_ref, kv_hbm, kvt_hbm, qt_hbm, gt_hbm, all_hbm, grads_hbm, weight_hbm,
    kv_ref, kvt_ref, qt_ref, gt_ref, all_ref, grads_ref, weight_ref, total_ref, load_sem, store_sem,
):
    block_count = kvt_ref.shape[1] // B
    loads = [
        pltpu.make_async_copy(source, target, load_sem.at[k])
        for k, (source, target) in enumerate(
            ((kv_hbm, kv_ref), (qt_hbm, qt_ref), (gt_hbm, gt_ref), (kvt_hbm, kvt_ref), (all_hbm, all_ref))
        )
    ]
    for load in loads[:4]:
        load.start()
    total_ref[...] = jnp.zeros_like(total_ref)
    for load in loads[:4]:
        load.wait()
    loads[4].start()
    zero = jnp.zeros((HD, B), BF16)

    def query_blocks(ids, live, shifted):
        heres = [pl.ds(pl.multiple_of(i * B, B), B) for i in ids]
        spots = [[pl.ds(pl.multiple_of(blocks_ref[j, i] * B, B), B) for j in range(live)] for i in ids]
        aparts, products = [], []
        for here, chosen in zip(heres, spots):
            apart = jnp.concatenate(
                [jnp.concatenate([qt_ref[:, here], zero], 1), jnp.concatenate([zero, gt_ref[:, here]], 1)], 0
            )
            aparts.append(apart)
            products.append(dot(jnp.concatenate([kv_ref[spot, :] for spot in chosen], 0), apart))
        pairs = []
        for i, product in zip(ids, products):
            count = counts_ref[i]
            scores = [product[:B, :B]]
            for j in range(1, live):
                scores.append(product[j * B : (j + 1) * B, :B] + jnp.where(j < count, 0.0, NEGATIVE))
            scores = jnp.concatenate(scores, 0)
            grad_probs = product[:, B:]
            if shifted:
                scores = scores - jnp.max(scores, 0, keepdims=True)
            raised = jnp.exp(scores)
            inverse = 1.0 / jnp.sum(raised, 0, keepdims=True)
            row_delta = jnp.sum(raised * grad_probs, 0, keepdims=True) * inverse
            probs = raised * inverse
            grad_scores = (probs * (grad_probs - row_delta)).astype(BF16)
            pairs.append(jnp.concatenate([grad_scores, probs.astype(BF16)], 1))
        outs, terms = [], []
        for apart, chosen, pair in zip(aparts, spots, pairs):
            outs.append(dot(jnp.concatenate([kvt_ref[:, spot] for spot in chosen], 1), pair))
            terms.append(dot(apart, pair, NT))
        for here, out in zip(heres, outs):
            grads_ref[0:HD, here] = out[HD:, B:].astype(BF16)
            grads_ref[HD : 2 * HD, here] = (out[:HD, :B] * SCALE).astype(BF16)
        for chosen, term in zip(spots, terms):
            for j, spot in enumerate(chosen):
                total_ref[:, spot] += term[:, j * B : (j + 1) * B]

    def step(index, carry):
        ids = [order_ref[0, index * group + t] for t in range(group)]
        most = counts_ref[ids[0]]
        for live in range(1, KMAX + 1):
            pl.when(most == live)(partial(query_blocks, ids, live, False))
        return carry

    def step_shifted(index, carry):
        query_blocks([index], KMAX, True)
        return carry

    calm = reach_ref[0, 0] <= CALM

    @pl.when(calm)
    def _():
        lax.fori_loop(0, block_count // group, step, 0)

    @pl.when(jnp.logical_not(calm))
    def _():
        lax.fori_loop(0, block_count, step_shifted, 0)

    stores = [
        pltpu.make_async_copy(source, target, store_sem.at[k])
        for k, (source, target) in enumerate(
            (
                (grads_ref.at[pl.ds(0, 2 * HD), :], grads_hbm.at[pl.ds(0, 2 * HD), :]),
                (grads_ref.at[pl.ds(2 * HD, 2 * HD), :], grads_hbm.at[pl.ds(2 * HD, 2 * HD), :]),
                (weight_ref, weight_hbm),
            )
        )
    ]
    stores[0].start()
    grads_ref[2 * HD :, :] = total_ref[...].astype(BF16)
    stores[1].start()
    loads[4].wait()
    weight_ref[...] = dot(grads_ref[HD:, :], all_ref[...])
    stores[2].start()
    for store in stores:
        store.wait()


def attention(order, reach, blocks, counts, *arrays):
    span, width = arrays[-1].shape
    sm = pl.BlockSpec(memory_space=pltpu.SMEM)
    anywhere = pl.BlockSpec(memory_space=pl.ANY)
    results = (jax.ShapeDtypeStruct((4 * HD, span), BF16), jax.ShapeDtypeStruct((3 * HD, width), F32))
    return pl.pallas_call(
        partial(attention_kernel, 4),
        out_shape=results,
        in_specs=[sm] * 4 + [anywhere] * len(arrays),
        out_specs=(anywhere,) * 2,
        scratch_shapes=[pltpu.VMEM(a.shape, a.dtype) for a in arrays + results]
        + [
            pltpu.VMEM((2 * HD, span), F32),
            pltpu.SemaphoreType.DMA((len(arrays),)),
            pltpu.SemaphoreType.DMA((3,)),
        ],
        compiler_params=pltpu.CompilerParams(vmem_limit_bytes=VMEM_BYTES),
        name="attention",
    )(order, reach, blocks, counts, *arrays)


ROWS = (256, 64, 16)


class Sum:
    def __init__(self, number, axes, columns, whole, sems, scratch, along, place_of, core):
        self.number, self.axes, self.columns, self.whole, self.sems = number, axes, columns, whole, sems
        self.total, self.out, self.quarters, self.parts, self.levels = scratch
        self.along = along
        self.place = [place_of[axis] for axis in axes]
        self.core = core
        self.waiting, self.sent = {}, []

    def send(self, phase, axis, source, target):
        copies = {}
        for offset in (2, 1, 3):
            copies[offset] = remote(
                source(offset), target(offset), self.sems, (self.number, phase, offset - 1), self.along(axis, offset)
            )
            copies[offset].start()
        self.waiting[phase] = copies
        self.sent += copies.values()

    def arrive(self, *phases):
        for phase in phases:
            for copy in self.waiting[phase].values():
                copy.wait_recv()

    def scatter_first(self, value):
        self.total[...] = value
        self.out[0 : ROWS[0], :] = value.astype(BF16)
        spot = lambda offset: part((self.place[0] + offset) % SIDE, ROWS[1])
        self.send(0, self.axes[0], lambda o: self.out.at[spot(o), :], lambda o: self.quarters.at[o - 1])

    def scatter_second(self):
        self.arrive(0)
        value = self.total[part(self.place[0], ROWS[1]), :] + self.quarters[0].astype(F32)
        value += self.quarters[1].astype(F32) + self.quarters[2].astype(F32)
        self.total[0 : ROWS[1], :] = value
        self.out[ROWS[0] :, :] = value.astype(BF16)
        spot = lambda offset: part(ROWS[0] // ROWS[2] + (self.place[1] + offset) % SIDE, ROWS[2])
        self.send(1, self.axes[1], lambda o: self.out.at[spot(o), :], lambda o: self.parts.at[o - 1])

    def scattered(self):
        self.arrive(1)
        value = self.total[part(self.place[1], ROWS[2]), :] + self.parts[0].astype(F32)
        return (value + (self.parts[1].astype(F32) + self.parts[2].astype(F32))).astype(BF16)

    def exchange(self, axis, place):
        self.levels[place] = self.scattered()
        here = self.levels.at[place]
        self.send(2, axis, lambda o: here, lambda o: here)

    def exchanged(self):
        self.arrive(2)
        value = [self.levels[k].astype(F32) for k in range(SIDE)]
        self.region()[...] = ((value[0] + value[1]) + (value[2] + value[3])).astype(BF16)

    def region(self, second=None, columns=None):
        second = self.place[1] if second is None else second
        first = self.core * ROWS[0] + self.place[0] * ROWS[1] + second * ROWS[2]
        rows = pl.ds(pl.multiple_of(first, ROWS[2]), ROWS[2])
        return self.whole.at[rows, self.columns if columns is None else columns]

    def gather(self):
        here = self.region()
        self.send(3, self.axes[1], lambda o: here, lambda o: here)
        self.send(4, self.axes[0], lambda o: here, lambda o: here)

    def gather_on(self):
        for offset, copy in self.waiting[3].items():
            copy.wait_recv()
            here = self.region((self.place[1] + SIDE - offset) % SIDE)
            self.send(4 + offset, self.axes[0], lambda o: here, lambda o: here)

    def gathered(self):
        self.arrive(4, 5, 6, 7)


def finish_kernel(
    grads_hbm, weight_hbm, x_hbm, g_hbm, wi_hbm, wo_hbm,
    layer_hbm, gradf_hbm, osum_hbm, isum_hbm,
    layer_ref, gradf_ref, osum_ref, isum_ref,
    x_ref, g_ref, wi_ref, wo_ref, attended_ref, rows_ref, merged_ref, theirs_ref, half_ref, total_ref,
    tot_a, tot_b, tot_c, tot_d, out_a, out_b, out_c, out_d, quarters_a, quarters_b, quarters_c, quarters_d,
    parts_a, parts_b, parts_c, parts_d, levels_c, levels_d,
    seq_send, seq_recv, core_send, core_recv, sum_send, sum_recv, spread_send, spread_recv, load_sem, store_sem,
):
    dp, seq = lax.axis_index("dp"), lax.axis_index("seq")
    z, x, y, core = dp // SIDE, dp % SIDE, seq // 2, seq % 2
    place_of = {"x": x, "y": y, "z": z}
    nodes, width = x_ref.shape
    half = nodes // 2
    other = (dp, y * 2 + (core + 1) % 2)
    seq_sems, core_sems = (seq_send, seq_recv), (core_send, core_recv)

    def along(axis, offset):
        if axis == "y":
            return (dp, ((y + offset) % SIDE) * 2 + core)
        if axis == "x":
            return (z * SIDE + (x + offset) % SIDE, seq)
        return (((z + offset) % SIDE) * SIDE + x, seq)

    peers = seq_peers(seq)
    met = greet([(dp, peer) for peer in peers] + [along(axis, offset) for axis in ("x", "z") for offset in (1, 2, 3)])
    loads = [
        pltpu.make_async_copy(source, target, load_sem.at[k])
        for k, (source, target) in enumerate(
            (
                (weight_hbm.at[:, :, part(core, ROWS[0])], merged_ref.at[:, part(core, HD), :]),
                (grads_hbm.at[0, :, part(seq, nodes)], attended_ref.at[part(seq, HD), :]),
                (g_hbm, g_ref),
                (x_hbm, x_ref),
                (wo_hbm, wo_ref),
                (wi_hbm, wi_ref),
                (grads_hbm.at[pl.ds(1, 3), :, part(seq, nodes)], rows_ref.at[:, part(seq, HD), :]),
            )
        )
    ]
    for load in loads:
        load.start()
    met()

    sent, stores = [], []

    def store(source, target):
        stores.append(pltpu.make_async_copy(source, target, store_sem.at[len(stores)]))
        stores[-1].start()

    def back(piece, source, target):
        copies = []
        for place, peer in enumerate(peers):
            copies.append(remote(source(peer), target, seq_sems, (piece, place), (dp, peer)))
            copies[-1].start()
        sent.extend(copies)
        return copies

    def back_rows(kind, h):
        mine = pl.ds(h * half, half)
        return back(
            1 + 2 * kind + h,
            lambda peer: grads_hbm.at[1 + kind, :, part(2 * peer + h, half)],
            rows_ref.at[kind, part(seq, HD), mine],
        )

    swap = remote(weight_hbm.at[:, :, part(1 - core, ROWS[0])], theirs_ref, core_sems, 0, other)
    swap.start()
    sent.append(swap)
    back_attended = back(0, lambda peer: grads_hbm.at[0, :, part(peer, nodes)], attended_ref.at[part(seq, HD), :])

    sums = (sum_send, sum_recv)
    make = lambda *args: Sum(*args, along, place_of, core)
    both = make(0, ("z", "x"), pl.ds(0, 2 * width), isum_ref, sums, (tot_a, out_a, quarters_a, parts_a, None))
    last = make(1, ("x", "z"), pl.ds(2 * width, width), isum_ref, sums, (tot_b, out_b, quarters_b, parts_b, None))
    left = make(2, ("x", "z"), pl.ds(0, half), osum_ref, sums, (tot_c, out_c, quarters_c, parts_c, levels_c))
    right = make(3, ("z", "x"), pl.ds(half, half), osum_ref, sums, (tot_d, out_d, quarters_d, parts_d, levels_d))

    loads[0].wait()
    swap.wait_recv()
    merged_ref[:, part(1 - core, HD), :] = theirs_ref[...]
    both.scatter_first(jnp.concatenate([merged_ref[0].T, merged_ref[1].T], 1))
    last.scatter_first(merged_ref[2].T)
    back_q = back_rows(0, 0) + back_rows(0, 1)
    for load in loads[1:]:
        load.wait()
    both.scatter_second()
    last.scatter_second()

    for copy in back_attended:
        copy.wait_recv()
    half_ref[0] = dot(attended_ref[part(1 - core, ROWS[0]), :], g_ref[...]).astype(BF16)
    merge = remote(half_ref.at[0], half_ref.at[1], core_sems, 1, other)
    merge.start()
    sent.append(merge)
    total_ref[0 : ROWS[0], :] = dot(attended_ref[part(core, ROWS[0]), :], g_ref[...])

    merge.wait_recv()
    merged = total_ref[0 : ROWS[0], :] + half_ref[1].astype(F32)
    left.scatter_first(merged[:, :half])
    right.scatter_first(merged[:, half:])

    spread = []
    for job, kinds in ((both, (0, 1)), (last, (2,))):
        value = job.scattered()
        for k, kind in enumerate(kinds):
            columns = pl.ds(pl.multiple_of(kind * width + y * 2 * HD, 2 * HD), 2 * HD)
            here = job.region(columns=columns)
            here[...] = value[:, k * 2 * HD : (k + 1) * 2 * HD]
            for offset in (2, 1, 3):
                spread.append(remote(here, here, (spread_send, spread_recv), (kind, offset - 1), along("y", offset)))
                spread[-1].start()
    sent.extend(spread)
    back_k = back_rows(1, 0) + back_rows(1, 1)
    left.scatter_second()
    right.scatter_second()
    for copy in spread:
        copy.wait_recv()
    both.gather()
    last.gather()
    left.exchange("y", y)
    right.exchange("y", y)
    back_v = back_rows(2, 0) + back_rows(2, 1)
    both.gather_on()
    last.gather_on()
    layer_ref[...] = (x_ref[...].astype(F32) + dot(attended_ref[...], wo_ref[...], TN)).astype(BF16)
    store(layer_ref, layer_hbm)
    for copy in back_q:
        copy.wait_recv()
    total_ref[...] = dot(wi_ref[:, :width], rows_ref[0])
    left.exchanged()
    right.exchanged()
    left.gather()
    right.gather()
    both.gathered()
    last.gathered()

    def share(source, target, index):
        mine = part(core, ROWS[0])
        copy = remote(source.at[mine, :], target.at[mine, :], core_sems, index, other)
        copy.start()
        store(source.at[mine, :], target.at[mine, :])
        sent.append(copy)
        return copy

    share_i = share(isum_ref, isum_hbm, 2)
    left.gather_on()
    right.gather_on()
    for copy in back_k:
        copy.wait_recv()
    total_ref[...] += dot(wi_ref[:, width : 2 * width], rows_ref[1])
    late = {id(copy) for copy in back_v}
    settled = [copy for copy in sent if id(copy) not in late]
    for job in (both, last, left, right):
        settled.extend(job.sent)
    for copy in settled + back_v:
        copy.wait_send()
    for copy in back_v:
        copy.wait_recv()
    turned = (total_ref[...] + dot(wi_ref[:, 2 * width :], rows_ref[2])).T
    gradf_ref[...] = (g_ref[...].astype(F32) + turned).astype(BF16)
    store(gradf_ref, gradf_hbm)
    left.gathered()
    right.gathered()
    share_o = share(osum_ref, osum_hbm, 3)
    share_o.wait_send()
    for copy in stores:
        copy.wait()
    share_i.wait_recv()
    share_o.wait_recv()


def finish(grads, weight, x, g, wi, wo):
    nodes, width = x.shape
    anywhere = pl.BlockSpec(memory_space=pl.ANY)
    columns = (4 * HD, 2 * HD, width // 2, width // 2)
    dma = pltpu.SemaphoreType.DMA
    results = [(nodes, width), (nodes, width), (width, width), (width, 3 * width)]
    return pl.pallas_call(
        finish_kernel,
        out_shape=tuple(jax.ShapeDtypeStruct(shape, BF16) for shape in results),
        in_specs=[anywhere] * 6,
        out_specs=(anywhere,) * 4,
        scratch_shapes=[pltpu.VMEM(shape, BF16) for shape in results]
        + [
            pltpu.VMEM(x.shape, BF16),
            pltpu.VMEM(g.shape, BF16),
            pltpu.VMEM(wi.shape, BF16),
            pltpu.VMEM(wo.shape, BF16),
            pltpu.VMEM((width, nodes), BF16),
            pltpu.VMEM((3, width, nodes), BF16),
            pltpu.VMEM((3, 2 * HD, ROWS[0]), F32),
            pltpu.VMEM((3, HD, ROWS[0]), F32),
            pltpu.VMEM((2, ROWS[0], width), BF16),
            pltpu.VMEM((width, nodes), F32),
        ]
        + [pltpu.VMEM((ROWS[0], n), F32) for n in columns]
        + [pltpu.VMEM((ROWS[0] + ROWS[1], n), BF16) for n in columns]
        + [pltpu.VMEM((SIDE - 1, ROWS[1], n), BF16) for n in columns]
        + [pltpu.VMEM((SIDE - 1, ROWS[2], n), BF16) for n in columns]
        + [pltpu.VMEM((SIDE, ROWS[2], n), BF16) for n in columns[2:]]
        + [dma((7, H - 1))] * 2
        + [dma((4,))] * 2
        + [dma((4, 8, SIDE - 1))] * 2
        + [dma((3, SIDE - 1))] * 2
        + [dma((7,)), dma((4,))],
        compiler_params=pltpu.CompilerParams(collective_id=1, has_side_effects=True, vmem_limit_bytes=VMEM_BYTES),
        name="finish",
    )(grads.reshape(4, HD, -1), weight.reshape(3, HD, -1), x, g, wi, wo)


def emit_kernel(factor, layer_ref, gradf_ref, osum_ref, isum_ref, layer_out, gradf_out, osum_out, isum_out):
    layer_out[...] = layer_ref[...]
    gradf_out[...] = gradf_ref[...]
    osum_out[...] = osum_ref[...].astype(F32) * factor
    isum_out[...] = isum_ref[...].astype(F32) * factor


def emit(layer, gradf, osum, isum, factor):
    arrays = (layer, gradf, osum, isum)
    kinds = (BF16, BF16, F32, F32)
    rows = layer.shape[0] // 2
    specs = [pl.BlockSpec((rows, a.shape[1]), lambda i: (i, 0)) for a in arrays]
    return pl.pallas_call(
        partial(emit_kernel, factor),
        grid=(2,),
        out_shape=tuple(jax.ShapeDtypeStruct(a.shape, kind) for a, kind in zip(arrays, kinds)),
        in_specs=specs,
        out_specs=tuple(specs),
        compiler_params=pltpu.CompilerParams(vmem_limit_bytes=VMEM_BYTES),
        name="emit",
    )(*arrays)


def shards(features, input_weight, output_weight, key_blocks, key_count, cotangent):
    x, g = features[0], cotangent[0]
    order, reach, everything, kv, kvt, qt, gt = project(x, g, input_weight, output_weight, key_count[0])
    grads, weight = attention(order, reach, key_blocks[0, 0].T, key_count[0, 0], kv, kvt, qt, gt, everything)
    results = finish(grads, weight, x, g, input_weight, output_weight)
    factor = 1.0 / (lax.axis_size("dp") * lax.axis_size("seq") * x.shape[0]) ** 0.5
    layer_out, grad_features, output_total, input_total = emit(*results, factor)
    return (layer_out[None], grad_features[None], input_total, output_total)


def solution(mesh):
    in_specs = (
        P("dp", "seq", None),
        P(),
        P(),
        P("dp", "seq", None, None),
        P("dp", "seq", None),
        P("dp", "seq", None),
    )
    out_specs = (P("dp", "seq", None), P("dp", "seq", None), P(), P())
    return jax.shard_map(shards, mesh=mesh, in_specs=in_specs, out_specs=out_specs, check_vma=False)
```

```python
from functools import partial

import jax
import jax.numpy as jnp
from jax import lax
from jax.experimental import pallas as pl
from jax.experimental.pallas import tpu as pltpu
from jax.sharding import PartitionSpec as P

H = 8
HD = 64
B = 128
KMAX = 8
NEGATIVE = -1e30
SCALE = HD**-0.5
MESH = pl.DeviceIdType.MESH
BF16 = jnp.bfloat16
F32 = jnp.float32
NN = (((1,), (0,)), ((), ()))
NT = (((1,), (1,)), ((), ()))
TN = (((0,), (0,)), ((), ()))
SIDE = 4
VMEM_BYTES = 60 << 20
CALM = 1600.0


def dot(a, b, dims=NN):
    return lax.dot_general(a, b, dims, preferred_element_type=F32)


def part(index, size):
    return pl.ds(pl.multiple_of(index * size, size), size)


def seq_peers(seq):
    y, core = seq // 2, seq % 2
    peers = []
    for dy in (2, 1, 3):
        for flip in (0, 1):
            peers.append(((y + dy) % SIDE) * 2 + (core + flip) % 2)
    peers.append(y * 2 + (core + 1) % 2)
    return peers


def greet(devices):
    barrier = pltpu.get_barrier_semaphore()
    for device in devices:
        pl.semaphore_signal(barrier, inc=1, device_id=device, device_id_type=MESH)
    return partial(pl.semaphore_wait, barrier, len(devices))


def remote(source, target, sems, index, device):
    return pltpu.make_async_remote_copy(
        src_ref=source,
        dst_ref=target,
        send_sem=sems[0].at[index],
        recv_sem=sems[1].at[index],
        device_id=device,
        device_id_type=MESH,
    )


def falling_order(counts):
    size = counts.shape[1]
    row = jnp.broadcast_to(counts.astype(F32), (size, size))
    here = lax.broadcasted_iota(jnp.int32, (size, size), 0)
    there = lax.broadcasted_iota(jnp.int32, (size, size), 1)
    column = jnp.sum(jnp.where(here == there, row, 0.0), 1, keepdims=True)
    ahead = (row > column) | ((row == column) & (there < here))
    rank = jnp.sum(jnp.where(ahead, 1.0, 0.0), 1, keepdims=True)
    found = jnp.where(rank == there.astype(F32), here.astype(F32), 0.0)
    return jnp.sum(found, 0, keepdims=True).astype(jnp.int32)


def project_kernel(
    x_hbm, g_hbm, wi_hbm, wo_hbm, count_ref,
    order_ref, reach_ref, all_hbm, kv_hbm, kvt_hbm, qt_hbm, gt_hbm,
    x_ref, kv_ref, kvt_ref, qt_ref, g_ref, wi_ref, wo_ref, grad_ref, send_sem, recv_sem, load_sem, store_sem,
):
    dp, seq = lax.axis_index("dp"), lax.axis_index("seq")
    y, core = seq // 2, seq % 2
    nodes, width = g_ref.shape
    half = nodes // 2
    sems = (send_sem, recv_sem)
    other = (dp, y * 2 + (core + 1) % 2)

    def at(dy, flip=0):
        return ((y + dy) % SIDE) * 2 + (core + flip) % 2

    peers = seq_peers(seq)
    met = greet([(dp, peer) for peer in peers])
    loads = [
        pltpu.make_async_copy(source, target, load_sem.at[k])
        for k, (source, target) in enumerate(
            ((x_hbm, x_ref.at[seq]), (wi_hbm, wi_ref), (g_hbm, g_ref), (wo_hbm, wo_ref))
        )
    ]
    for load in loads:
        load.start()
    met()
    up, down = (dp, at(1)), (dp, at(3))

    def rows(h):
        return pl.ds(h * half, half)

    def pass_on(source, h, index, device):
        piece = x_ref.at[source, rows(h)]
        return remote(piece, piece, sems, index, device)

    def own(h, index, device):
        return remote(x_hbm.at[rows(h)], x_ref.at[seq, rows(h)], sems, index, device)

    sent = [own(0, 0, up), own(1, 3, down), own(1, 1, up), own(0, 4, down), own(0, 6, other), own(1, 7, other)]
    for copy in sent:
        copy.start()

    loads[0].wait()
    loads[1].wait()
    chosen = []
    for kind in (1, 2, 0):
        block = wi_ref[:, pl.ds(pl.multiple_of(kind * width + y * 2 * HD, 2 * HD), 2 * HD)]
        chosen.append(jnp.where(core == 0, block[:, :HD], block[:, HD:]))
    chosen[2] = chosen[2] * jnp.asarray(SCALE, BF16)
    weights = jnp.concatenate(chosen + [jnp.zeros_like(chosen[0])], 1)
    stores, largest = [], [None, None]

    def store(source, target):
        stores.append(pltpu.make_async_copy(source, target, store_sem.at[len(stores)]))
        stores[-1].start()

    def project_half(source, h):
        here = part(2 * source + h, half)
        product = dot(x_ref[source, rows(h), :], weights)
        kv = product[:, : 2 * HD].astype(BF16)
        kvt, qt = kv.T, product[:, 2 * HD :].T[:HD].astype(BF16)
        kv_ref[here, :] = kv
        kvt_ref[:, here] = kvt
        qt_ref[:, here] = qt
        for k, rows_of in enumerate((kvt[:HD], qt)):
            norms = jnp.sum(jnp.square(rows_of.astype(F32)), 0, keepdims=True)
            largest[k] = norms if largest[k] is None else jnp.maximum(largest[k], norms)
        store(x_ref.at[source, rows(h)], all_hbm.at[here, :])
        store(kv_ref.at[here, :], kv_hbm.at[here, :])
        store(kvt_ref.at[:, here], kvt_hbm.at[:, here])
        store(qt_ref.at[:, here], qt_hbm.at[:, here])

    project_half(seq, 0)
    project_half(seq, 1)
    loads[2].wait()
    loads[3].wait()
    grad_ref[...] = dot(wo_ref[...], g_ref[...], NT).astype(BF16)
    store(grad_ref.at[part(seq, HD), :], gt_hbm.at[:, part(seq, nodes)])
    order_ref[...] = falling_order(count_ref[...])
    low, high, far = at(3), at(1), at(2)
    forwards = {0: pass_on(low, 0, 2, up), 3: pass_on(high, 1, 5, down)}
    shares = {0: (low, 0, 8), 3: (high, 1, 9), 1: (low, 1, 10), 4: (high, 0, 11), 2: (far, 0, 12), 5: (far, 1, 13)}
    ring = {index: own(0, index, up) for index in (0, 1, 2, 3, 4, 5)}
    near = {index: own(0, index, other) for index in range(6, 14)}

    def arrive(index):
        ring[index].wait_recv()
        source, h, share = shares[index]
        for copy in [forwards[index]] if index in forwards else []:
            copy.start()
            sent.append(copy)
        sent.append(pass_on(source, h, share, other))
        sent[-1].start()

    def project_arrived(index):
        project_half(*shares[index][:2])

    def arrive_near(share, source, h):
        near[share].wait_recv()
        project_half(source, h)

    arrive_near(6, at(0, 1), 0)
    arrive_near(7, at(0, 1), 1)
    arrive(0)
    arrive(3)
    given = []
    for place, peer in enumerate(peers):
        given.append(
            remote(grad_ref.at[part(peer, HD), :], gt_hbm.at[:, part(seq, nodes)], sems, 14 + place, (dp, peer))
        )
        given[-1].start()
    project_arrived(0)
    project_arrived(3)
    arrive_near(8, at(3, 1), 0)
    arrive_near(9, at(1, 1), 1)
    arrive(1)
    arrive(4)
    project_arrived(1)
    project_arrived(4)
    arrive_near(10, at(3, 1), 1)
    arrive_near(11, at(1, 1), 0)
    arrive(2)
    arrive(5)
    project_arrived(2)
    project_arrived(5)
    arrive_near(12, at(2, 1), 0)
    arrive_near(13, at(2, 1), 1)
    reach = jnp.max(largest[0], 1, keepdims=True) * jnp.max(largest[1], 1, keepdims=True)
    reach_ref[...] = jnp.broadcast_to(reach, reach_ref.shape)
    for copy in sent:
        copy.wait_send()
    for copy in stores:
        copy.wait()
    for copy in given:
        copy.wait_send()
    for copy in given:
        copy.wait_recv()


def project(x, g, wi, wo, counts):
    nodes, width = x.shape
    span = nodes * H
    vm = pl.BlockSpec(memory_space=pltpu.VMEM)
    anywhere = pl.BlockSpec(memory_space=pl.ANY)
    dma = pltpu.SemaphoreType.DMA
    return pl.pallas_call(
        project_kernel,
        out_shape=(
            jax.ShapeDtypeStruct(counts.shape, jnp.int32),
            jax.ShapeDtypeStruct((1, B), F32),
            jax.ShapeDtypeStruct((span, width), BF16),
            jax.ShapeDtypeStruct((span, 2 * HD), BF16),
            jax.ShapeDtypeStruct((2 * HD, span), BF16),
            jax.ShapeDtypeStruct((HD, span), BF16),
            jax.ShapeDtypeStruct((HD, span), BF16),
        ),
        in_specs=[anywhere] * 4 + [vm],
        out_specs=(vm, vm) + (anywhere,) * 5,
        scratch_shapes=[
            pltpu.VMEM((H, nodes, width), BF16),
            pltpu.VMEM((span, 2 * HD), BF16),
            pltpu.VMEM((2 * HD, span), BF16),
            pltpu.VMEM((HD, span), BF16),
            pltpu.VMEM(g.shape, BF16),
            pltpu.VMEM(wi.shape, BF16),
            pltpu.VMEM(wo.shape, BF16),
            pltpu.VMEM((width, nodes), BF16),
            dma((21,)),
            dma((21,)),
            dma((4,)),
            dma((8 * H + 1,)),
        ],
        compiler_params=pltpu.CompilerParams(collective_id=0, has_side_effects=True, vmem_limit_bytes=VMEM_BYTES),
        name="project",
    )(x, g, wi, wo, counts)


def attention_kernel(
    group, order_ref, reach_ref, blocks_ref, counts_ref, kv_ref, kvt_ref, qt_ref, gt_ref, all_hbm, grads_ref, weight_ref,
    total_ref, all_ref, load_sem,
):
    block_count = kvt_ref.shape[1] // B
    load = pltpu.make_async_copy(all_hbm, all_ref, load_sem)
    load.start()
    total_ref[...] = jnp.zeros_like(total_ref)
    zero = jnp.zeros((HD, B), BF16)

    def query_blocks(ids, live, shifted):
        heres = [pl.ds(pl.multiple_of(i * B, B), B) for i in ids]
        spots = [[pl.ds(pl.multiple_of(blocks_ref[j, i] * B, B), B) for j in range(live)] for i in ids]
        aparts, products = [], []
        for here, chosen in zip(heres, spots):
            apart = jnp.concatenate(
                [jnp.concatenate([qt_ref[:, here], zero], 1), jnp.concatenate([zero, gt_ref[:, here]], 1)], 0
            )
            aparts.append(apart)
            products.append(dot(jnp.concatenate([kv_ref[spot, :] for spot in chosen], 0), apart))
        pairs = []
        for i, product in zip(ids, products):
            count = counts_ref[i]
            scores = [product[:B, :B]]
            for j in range(1, live):
                scores.append(product[j * B : (j + 1) * B, :B] + jnp.where(j < count, 0.0, NEGATIVE))
            scores = jnp.concatenate(scores, 0)
            grad_probs = product[:, B:]
            if shifted:
                scores = scores - jnp.max(scores, 0, keepdims=True)
            raised = jnp.exp(scores)
            inverse = 1.0 / jnp.sum(raised, 0, keepdims=True)
            row_delta = jnp.sum(raised * grad_probs, 0, keepdims=True) * inverse
            probs = raised * inverse
            grad_scores = (probs * (grad_probs - row_delta)).astype(BF16)
            pairs.append(jnp.concatenate([grad_scores, probs.astype(BF16)], 1))
        outs, terms = [], []
        for apart, chosen, pair in zip(aparts, spots, pairs):
            outs.append(dot(jnp.concatenate([kvt_ref[:, spot] for spot in chosen], 1), pair))
            terms.append(dot(apart, pair, NT))
        for here, out in zip(heres, outs):
            grads_ref[0:HD, here] = out[HD:, B:].astype(BF16)
            grads_ref[HD : 2 * HD, here] = (out[:HD, :B] * SCALE).astype(BF16)
        for chosen, term in zip(spots, terms):
            for j, spot in enumerate(chosen):
                total_ref[:, spot] += term[:, j * B : (j + 1) * B]

    def step(index, carry):
        ids = [order_ref[0, index * group + t] for t in range(group)]
        most = counts_ref[ids[0]]
        for live in range(1, KMAX + 1):
            pl.when(most == live)(partial(query_blocks, ids, live, False))
        return carry

    def step_shifted(index, carry):
        query_blocks([index], KMAX, True)
        return carry

    calm = reach_ref[0, 0] <= CALM

    @pl.when(calm)
    def _():
        lax.fori_loop(0, block_count // group, step, 0)

    @pl.when(jnp.logical_not(calm))
    def _():
        lax.fori_loop(0, block_count, step_shifted, 0)

    grads_ref[2 * HD :, :] = total_ref[...].astype(BF16)
    load.wait()
    weight_ref[...] = dot(grads_ref[HD:, :], all_ref[...])


def attention(order, reach, blocks, counts, kv, kvt, qt, gt, everything):
    span, width = everything.shape
    vm = pl.BlockSpec(memory_space=pltpu.VMEM)
    sm = pl.BlockSpec(memory_space=pltpu.SMEM)
    return pl.pallas_call(
        partial(attention_kernel, 4),
        out_shape=(jax.ShapeDtypeStruct((4 * HD, span), BF16), jax.ShapeDtypeStruct((3 * HD, width), F32)),
        in_specs=[sm, sm, sm, sm, vm, vm, vm, vm, pl.BlockSpec(memory_space=pl.ANY)],
        out_specs=(vm, vm),
        scratch_shapes=[
            pltpu.VMEM((2 * HD, span), F32),
            pltpu.VMEM(everything.shape, BF16),
            pltpu.SemaphoreType.DMA,
        ],
        compiler_params=pltpu.CompilerParams(vmem_limit_bytes=VMEM_BYTES),
        name="attention",
    )(order, reach, blocks, counts, kv, kvt, qt, gt, everything)


ROWS = (256, 64, 16)


class Sum:
    def __init__(self, number, axes, columns, whole, sems, scratch, along, place_of, core):
        self.number, self.axes, self.columns, self.whole, self.sems = number, axes, columns, whole, sems
        self.total, self.out, self.quarters, self.parts, self.levels = scratch
        self.along = along
        self.place = [place_of[axis] for axis in axes]
        self.core = core
        self.waiting, self.sent = {}, []

    def send(self, phase, axis, source, target):
        copies = {}
        for offset in (2, 1, 3):
            copies[offset] = remote(
                source(offset), target(offset), self.sems, (self.number, phase, offset - 1), self.along(axis, offset)
            )
            copies[offset].start()
        self.waiting[phase] = copies
        self.sent += copies.values()

    def arrive(self, *phases):
        for phase in phases:
            for copy in self.waiting[phase].values():
                copy.wait_recv()

    def scatter_first(self, value):
        self.total[...] = value
        self.out[0 : ROWS[0], :] = value.astype(BF16)
        spot = lambda offset: part((self.place[0] + offset) % SIDE, ROWS[1])
        self.send(0, self.axes[0], lambda o: self.out.at[spot(o), :], lambda o: self.quarters.at[o - 1])

    def scatter_second(self):
        self.arrive(0)
        value = self.total[part(self.place[0], ROWS[1]), :] + self.quarters[0].astype(F32)
        value += self.quarters[1].astype(F32) + self.quarters[2].astype(F32)
        self.total[0 : ROWS[1], :] = value
        self.out[ROWS[0] :, :] = value.astype(BF16)
        spot = lambda offset: part(ROWS[0] // ROWS[2] + (self.place[1] + offset) % SIDE, ROWS[2])
        self.send(1, self.axes[1], lambda o: self.out.at[spot(o), :], lambda o: self.parts.at[o - 1])

    def scattered(self):
        self.arrive(1)
        value = self.total[part(self.place[1], ROWS[2]), :] + self.parts[0].astype(F32)
        return (value + (self.parts[1].astype(F32) + self.parts[2].astype(F32))).astype(BF16)

    def exchange(self, axis, place):
        self.levels[place] = self.scattered()
        here = self.levels.at[place]
        self.send(2, axis, lambda o: here, lambda o: here)

    def exchanged(self):
        self.arrive(2)
        value = [self.levels[k].astype(F32) for k in range(SIDE)]
        self.region()[...] = ((value[0] + value[1]) + (value[2] + value[3])).astype(BF16)

    def region(self, second=None, columns=None):
        second = self.place[1] if second is None else second
        first = self.core * ROWS[0] + self.place[0] * ROWS[1] + second * ROWS[2]
        rows = pl.ds(pl.multiple_of(first, ROWS[2]), ROWS[2])
        return self.whole.at[rows, self.columns if columns is None else columns]

    def gather(self):
        here = self.region()
        self.send(3, self.axes[1], lambda o: here, lambda o: here)
        self.send(4, self.axes[0], lambda o: here, lambda o: here)

    def gather_on(self):
        for offset, copy in self.waiting[3].items():
            copy.wait_recv()
            here = self.region((self.place[1] + SIDE - offset) % SIDE)
            self.send(4 + offset, self.axes[0], lambda o: here, lambda o: here)

    def gathered(self):
        self.arrive(4, 5, 6, 7)


def finish_kernel(
    grads_hbm, weight_hbm, x_hbm, g_hbm, wi_hbm, wo_hbm,
    layer_hbm, gradf_hbm, osum_hbm, isum_hbm,
    layer_ref, gradf_ref, osum_ref, isum_ref,
    x_ref, g_ref, wi_ref, wo_ref, attended_ref, rows_ref, merged_ref, theirs_ref, half_ref, total_ref,
    tot_a, tot_b, tot_c, tot_d, out_a, out_b, out_c, out_d, quarters_a, quarters_b, quarters_c, quarters_d,
    parts_a, parts_b, parts_c, parts_d, levels_c, levels_d,
    seq_send, seq_recv, core_send, core_recv, sum_send, sum_recv, spread_send, spread_recv, load_sem, store_sem,
):
    dp, seq = lax.axis_index("dp"), lax.axis_index("seq")
    z, x, y, core = dp // SIDE, dp % SIDE, seq // 2, seq % 2
    place_of = {"x": x, "y": y, "z": z}
    nodes, width = x_ref.shape
    half = nodes // 2
    other = (dp, y * 2 + (core + 1) % 2)
    seq_sems, core_sems = (seq_send, seq_recv), (core_send, core_recv)

    def along(axis, offset):
        if axis == "y":
            return (dp, ((y + offset) % SIDE) * 2 + core)
        if axis == "x":
            return (z * SIDE + (x + offset) % SIDE, seq)
        return (((z + offset) % SIDE) * SIDE + x, seq)

    peers = seq_peers(seq)
    met = greet([(dp, peer) for peer in peers] + [along(axis, offset) for axis in ("x", "z") for offset in (1, 2, 3)])
    loads = [
        pltpu.make_async_copy(source, target, load_sem.at[k])
        for k, (source, target) in enumerate(
            (
                (weight_hbm.at[:, :, part(core, ROWS[0])], merged_ref.at[:, part(core, HD), :]),
                (grads_hbm.at[0, :, part(seq, nodes)], attended_ref.at[part(seq, HD), :]),
                (g_hbm, g_ref),
                (x_hbm, x_ref),
                (wo_hbm, wo_ref),
                (wi_hbm, wi_ref),
                (grads_hbm.at[pl.ds(1, 3), :, part(seq, nodes)], rows_ref.at[:, part(seq, HD), :]),
            )
        )
    ]
    for load in loads:
        load.start()
    met()

    sent, stores = [], []

    def store(source, target):
        stores.append(pltpu.make_async_copy(source, target, store_sem.at[len(stores)]))
        stores[-1].start()

    def back(piece, source, target):
        copies = []
        for place, peer in enumerate(peers):
            copies.append(remote(source(peer), target, seq_sems, (piece, place), (dp, peer)))
            copies[-1].start()
        sent.extend(copies)
        return copies

    def back_rows(kind, h):
        mine = pl.ds(h * half, half)
        return back(
            1 + 2 * kind + h,
            lambda peer: grads_hbm.at[1 + kind, :, part(2 * peer + h, half)],
            rows_ref.at[kind, part(seq, HD), mine],
        )

    swap = remote(weight_hbm.at[:, :, part(1 - core, ROWS[0])], theirs_ref, core_sems, 0, other)
    swap.start()
    sent.append(swap)
    back_attended = back(0, lambda peer: grads_hbm.at[0, :, part(peer, nodes)], attended_ref.at[part(seq, HD), :])

    sums = (sum_send, sum_recv)
    make = lambda *args: Sum(*args, along, place_of, core)
    both = make(0, ("z", "x"), pl.ds(0, 2 * width), isum_ref, sums, (tot_a, out_a, quarters_a, parts_a, None))
    last = make(1, ("x", "z"), pl.ds(2 * width, width), isum_ref, sums, (tot_b, out_b, quarters_b, parts_b, None))
    left = make(2, ("x", "z"), pl.ds(0, half), osum_ref, sums, (tot_c, out_c, quarters_c, parts_c, levels_c))
    right = make(3, ("z", "x"), pl.ds(half, half), osum_ref, sums, (tot_d, out_d, quarters_d, parts_d, levels_d))

    loads[0].wait()
    swap.wait_recv()
    merged_ref[:, part(1 - core, HD), :] = theirs_ref[...]
    both.scatter_first(jnp.concatenate([merged_ref[0].T, merged_ref[1].T], 1))
    last.scatter_first(merged_ref[2].T)
    back_q = back_rows(0, 0) + back_rows(0, 1)
    for load in loads[1:]:
        load.wait()
    both.scatter_second()
    last.scatter_second()

    for copy in back_attended:
        copy.wait_recv()
    half_ref[0] = dot(attended_ref[part(1 - core, ROWS[0]), :], g_ref[...]).astype(BF16)
    merge = remote(half_ref.at[0], half_ref.at[1], core_sems, 1, other)
    merge.start()
    sent.append(merge)
    total_ref[0 : ROWS[0], :] = dot(attended_ref[part(core, ROWS[0]), :], g_ref[...])

    merge.wait_recv()
    merged = total_ref[0 : ROWS[0], :] + half_ref[1].astype(F32)
    left.scatter_first(merged[:, :half])
    right.scatter_first(merged[:, half:])

    spread = []
    for job, kinds in ((both, (0, 1)), (last, (2,))):
        value = job.scattered()
        for k, kind in enumerate(kinds):
            columns = pl.ds(pl.multiple_of(kind * width + y * 2 * HD, 2 * HD), 2 * HD)
            here = job.region(columns=columns)
            here[...] = value[:, k * 2 * HD : (k + 1) * 2 * HD]
            for offset in (2, 1, 3):
                spread.append(remote(here, here, (spread_send, spread_recv), (kind, offset - 1), along("y", offset)))
                spread[-1].start()
    sent.extend(spread)
    back_k = back_rows(1, 0) + back_rows(1, 1)
    left.scatter_second()
    right.scatter_second()
    for copy in spread:
        copy.wait_recv()
    both.gather()
    last.gather()
    left.exchange("y", y)
    right.exchange("y", y)
    back_v = back_rows(2, 0) + back_rows(2, 1)
    both.gather_on()
    last.gather_on()
    layer_ref[...] = (x_ref[...].astype(F32) + dot(attended_ref[...], wo_ref[...], TN)).astype(BF16)
    store(layer_ref, layer_hbm)
    for copy in back_q:
        copy.wait_recv()
    total_ref[...] = dot(wi_ref[:, :width], rows_ref[0])
    left.exchanged()
    right.exchanged()
    left.gather()
    right.gather()
    both.gathered()
    last.gathered()

    def share(source, target, index):
        mine = part(core, ROWS[0])
        copy = remote(source.at[mine, :], target.at[mine, :], core_sems, index, other)
        copy.start()
        store(source.at[mine, :], target.at[mine, :])
        sent.append(copy)
        return copy

    share_i = share(isum_ref, isum_hbm, 2)
    left.gather_on()
    right.gather_on()
    for copy in back_k:
        copy.wait_recv()
    total_ref[...] += dot(wi_ref[:, width : 2 * width], rows_ref[1])
    late = {id(copy) for copy in back_v}
    settled = [copy for copy in sent if id(copy) not in late]
    for job in (both, last, left, right):
        settled.extend(job.sent)
    for copy in settled + back_v:
        copy.wait_send()
    for copy in back_v:
        copy.wait_recv()
    turned = (total_ref[...] + dot(wi_ref[:, 2 * width :], rows_ref[2])).T
    gradf_ref[...] = (g_ref[...].astype(F32) + turned).astype(BF16)
    store(gradf_ref, gradf_hbm)
    left.gathered()
    right.gathered()
    share_o = share(osum_ref, osum_hbm, 3)
    share_o.wait_send()
    for copy in stores:
        copy.wait()
    share_i.wait_recv()
    share_o.wait_recv()


def finish(grads, weight, x, g, wi, wo):
    nodes, width = x.shape
    anywhere = pl.BlockSpec(memory_space=pl.ANY)
    columns = (4 * HD, 2 * HD, width // 2, width // 2)
    dma = pltpu.SemaphoreType.DMA
    results = [(nodes, width), (nodes, width), (width, width), (width, 3 * width)]
    return pl.pallas_call(
        finish_kernel,
        out_shape=tuple(jax.ShapeDtypeStruct(shape, BF16) for shape in results),
        in_specs=[anywhere] * 6,
        out_specs=(anywhere,) * 4,
        scratch_shapes=[pltpu.VMEM(shape, BF16) for shape in results]
        + [
            pltpu.VMEM(x.shape, BF16),
            pltpu.VMEM(g.shape, BF16),
            pltpu.VMEM(wi.shape, BF16),
            pltpu.VMEM(wo.shape, BF16),
            pltpu.VMEM((width, nodes), BF16),
            pltpu.VMEM((3, width, nodes), BF16),
            pltpu.VMEM((3, 2 * HD, ROWS[0]), F32),
            pltpu.VMEM((3, HD, ROWS[0]), F32),
            pltpu.VMEM((2, ROWS[0], width), BF16),
            pltpu.VMEM((width, nodes), F32),
        ]
        + [pltpu.VMEM((ROWS[0], n), F32) for n in columns]
        + [pltpu.VMEM((ROWS[0] + ROWS[1], n), BF16) for n in columns]
        + [pltpu.VMEM((SIDE - 1, ROWS[1], n), BF16) for n in columns]
        + [pltpu.VMEM((SIDE - 1, ROWS[2], n), BF16) for n in columns]
        + [pltpu.VMEM((SIDE, ROWS[2], n), BF16) for n in columns[2:]]
        + [dma((7, H - 1))] * 2
        + [dma((4,))] * 2
        + [dma((4, 8, SIDE - 1))] * 2
        + [dma((3, SIDE - 1))] * 2
        + [dma((7,)), dma((4,))],
        compiler_params=pltpu.CompilerParams(collective_id=1, has_side_effects=True, vmem_limit_bytes=VMEM_BYTES),
        name="finish",
    )(grads.reshape(4, HD, -1), weight.reshape(3, HD, -1), x, g, wi, wo)


def emit_kernel(factor, layer_ref, gradf_ref, osum_ref, isum_ref, layer_out, gradf_out, osum_out, isum_out):
    layer_out[...] = layer_ref[...]
    gradf_out[...] = gradf_ref[...]
    osum_out[...] = osum_ref[...].astype(F32) * factor
    isum_out[...] = isum_ref[...].astype(F32) * factor


def emit(layer, gradf, osum, isum, factor):
    arrays = (layer, gradf, osum, isum)
    kinds = (BF16, BF16, F32, F32)
    rows = layer.shape[0] // 2
    specs = [pl.BlockSpec((rows, a.shape[1]), lambda i: (i, 0)) for a in arrays]
    return pl.pallas_call(
        partial(emit_kernel, factor),
        grid=(2,),
        out_shape=tuple(jax.ShapeDtypeStruct(a.shape, kind) for a, kind in zip(arrays, kinds)),
        in_specs=specs,
        out_specs=tuple(specs),
        compiler_params=pltpu.CompilerParams(vmem_limit_bytes=VMEM_BYTES),
        name="emit",
    )(*arrays)


def shards(features, input_weight, output_weight, key_blocks, key_count, cotangent):
    x, g = features[0], cotangent[0]
    order, reach, everything, kv, kvt, qt, gt = project(x, g, input_weight, output_weight, key_count[0])
    grads, weight = attention(order, reach, key_blocks[0, 0].T, key_count[0, 0], kv, kvt, qt, gt, everything)
    results = finish(grads, weight, x, g, input_weight, output_weight)
    factor = 1.0 / (lax.axis_size("dp") * lax.axis_size("seq") * x.shape[0]) ** 0.5
    layer_out, grad_features, output_total, input_total = emit(*results, factor)
    return (layer_out[None], grad_features[None], input_total, output_total)


def solution(mesh):
    in_specs = (
        P("dp", "seq", None),
        P(),
        P(),
        P("dp", "seq", None, None),
        P("dp", "seq", None),
        P("dp", "seq", None),
    )
    out_specs = (P("dp", "seq", None), P("dp", "seq", None), P(), P())
    return jax.shard_map(shards, mesh=mesh, in_specs=in_specs, out_specs=out_specs, check_vma=False)
```

```python
from functools import partial

import jax
import jax.numpy as jnp
from jax import lax
from jax.experimental import pallas as pl
from jax.experimental.pallas import tpu as pltpu
from jax.sharding import PartitionSpec as P

H = 8
HD = 64
B = 128
KMAX = 8
NEGATIVE = -1e30
SCALE = HD**-0.5
MESH = pl.DeviceIdType.MESH
BF16 = jnp.bfloat16
F32 = jnp.float32
NN = (((1,), (0,)), ((), ()))
NT = (((1,), (1,)), ((), ()))
TN = (((0,), (0,)), ((), ()))
SIDE = 4
VMEM_BYTES = 60 << 20
CALM = 1600.0


def dot(a, b, dims=NN):
    return lax.dot_general(a, b, dims, preferred_element_type=F32)


def part(index, size):
    return pl.ds(pl.multiple_of(index * size, size), size)


def seq_peers(seq):
    y, core = seq // 2, seq % 2
    peers = []
    for dy in (2, 1, 3):
        for flip in (0, 1):
            peers.append(((y + dy) % SIDE) * 2 + (core + flip) % 2)
    peers.append(y * 2 + (core + 1) % 2)
    return peers


def greet(devices):
    barrier = pltpu.get_barrier_semaphore()
    for device in devices:
        pl.semaphore_signal(barrier, inc=1, device_id=device, device_id_type=MESH)
    return partial(pl.semaphore_wait, barrier, len(devices))


def remote(source, target, sems, index, device):
    return pltpu.make_async_remote_copy(
        src_ref=source,
        dst_ref=target,
        send_sem=sems[0].at[index],
        recv_sem=sems[1].at[index],
        device_id=device,
        device_id_type=MESH,
    )


def falling_order(counts):
    size = counts.shape[1]
    row = jnp.broadcast_to(counts.astype(F32), (size, size))
    here = lax.broadcasted_iota(jnp.int32, (size, size), 0)
    there = lax.broadcasted_iota(jnp.int32, (size, size), 1)
    column = jnp.sum(jnp.where(here == there, row, 0.0), 1, keepdims=True)
    ahead = (row > column) | ((row == column) & (there < here))
    rank = jnp.sum(jnp.where(ahead, 1.0, 0.0), 1, keepdims=True)
    found = jnp.where(rank == there.astype(F32), here.astype(F32), 0.0)
    return jnp.sum(found, 0, keepdims=True).astype(jnp.int32)


def project_kernel(
    x_hbm, g_hbm, wi_hbm, wo_hbm, count_ref,
    order_ref, reach_ref, all_hbm, kv_hbm, kvt_hbm, qt_hbm, gt_hbm,
    x_ref, kv_ref, kvt_ref, qt_ref, g_ref, wi_ref, wo_ref, grad_ref, send_sem, recv_sem, load_sem, store_sem,
):
    dp, seq = lax.axis_index("dp"), lax.axis_index("seq")
    y, core = seq // 2, seq % 2
    nodes, width = g_ref.shape
    half = nodes // 2
    sems = (send_sem, recv_sem)
    other = (dp, y * 2 + (core + 1) % 2)

    def at(dy, flip=0):
        return ((y + dy) % SIDE) * 2 + (core + flip) % 2

    peers = seq_peers(seq)
    met = greet([(dp, peer) for peer in peers])
    loads = [
        pltpu.make_async_copy(source, target, load_sem.at[k])
        for k, (source, target) in enumerate(
            ((x_hbm, x_ref.at[seq]), (wi_hbm, wi_ref), (g_hbm, g_ref), (wo_hbm, wo_ref))
        )
    ]
    for load in loads:
        load.start()
    met()
    up, down = (dp, at(1)), (dp, at(3))

    def rows(h):
        return pl.ds(h * half, half)

    def pass_on(source, h, index, device):
        piece = x_ref.at[source, rows(h)]
        return remote(piece, piece, sems, index, device)

    def own(h, index, device):
        return remote(x_hbm.at[rows(h)], x_ref.at[seq, rows(h)], sems, index, device)

    sent = [own(0, 0, up), own(1, 3, down), own(1, 1, up), own(0, 4, down), own(0, 6, other), own(1, 7, other)]
    for copy in sent:
        copy.start()

    loads[0].wait()
    loads[1].wait()
    chosen = []
    for kind in (1, 2, 0):
        block = wi_ref[:, pl.ds(pl.multiple_of(kind * width + y * 2 * HD, 2 * HD), 2 * HD)]
        chosen.append(jnp.where(core == 0, block[:, :HD], block[:, HD:]))
    chosen[2] = chosen[2] * jnp.asarray(SCALE, BF16)
    weights = jnp.concatenate(chosen + [jnp.zeros_like(chosen[0])], 1)
    stores, largest = [], [None, None]

    def store(source, target):
        stores.append(pltpu.make_async_copy(source, target, store_sem.at[len(stores)]))
        stores[-1].start()

    def project_half(source, h):
        here = part(2 * source + h, half)
        product = dot(x_ref[source, rows(h), :], weights)
        kv = product[:, : 2 * HD].astype(BF16)
        kvt, qt = kv.T, product[:, 2 * HD :].T[:HD].astype(BF16)
        kv_ref[here, :] = kv
        kvt_ref[:, here] = kvt
        qt_ref[:, here] = qt
        for k, rows_of in enumerate((kvt[:HD], qt)):
            norms = jnp.sum(jnp.square(rows_of.astype(F32)), 0, keepdims=True)
            largest[k] = norms if largest[k] is None else jnp.maximum(largest[k], norms)
        store(x_ref.at[source, rows(h)], all_hbm.at[here, :])
        store(kv_ref.at[here, :], kv_hbm.at[here, :])
        store(kvt_ref.at[:, here], kvt_hbm.at[:, here])
        store(qt_ref.at[:, here], qt_hbm.at[:, here])

    project_half(seq, 0)
    project_half(seq, 1)
    loads[2].wait()
    loads[3].wait()
    grad_ref[...] = dot(wo_ref[...], g_ref[...], NT).astype(BF16)
    store(grad_ref.at[part(seq, HD), :], gt_hbm.at[:, part(seq, nodes)])
    order_ref[...] = falling_order(count_ref[...])
    low, high, far = at(3), at(1), at(2)
    forwards = {0: pass_on(low, 0, 2, up), 3: pass_on(high, 1, 5, down)}
    shares = {0: (low, 0, 8), 3: (high, 1, 9), 1: (low, 1, 10), 4: (high, 0, 11), 2: (far, 0, 12), 5: (far, 1, 13)}
    ring = {index: own(0, index, up) for index in (0, 1, 2, 3, 4, 5)}
    near = {index: own(0, index, other) for index in range(6, 14)}

    def arrive(index):
        ring[index].wait_recv()
        source, h, share = shares[index]
        for copy in [forwards[index]] if index in forwards else []:
            copy.start()
            sent.append(copy)
        sent.append(pass_on(source, h, share, other))
        sent[-1].start()

    def project_arrived(index):
        project_half(*shares[index][:2])

    def arrive_near(share, source, h):
        near[share].wait_recv()
        project_half(source, h)

    arrive_near(6, at(0, 1), 0)
    arrive_near(7, at(0, 1), 1)
    arrive(0)
    arrive(3)
    given = []
    for place, peer in enumerate(peers):
        given.append(
            remote(grad_ref.at[part(peer, HD), :], gt_hbm.at[:, part(seq, nodes)], sems, 14 + place, (dp, peer))
        )
        given[-1].start()
    project_arrived(0)
    project_arrived(3)
    arrive_near(8, at(3, 1), 0)
    arrive_near(9, at(1, 1), 1)
    arrive(1)
    arrive(4)
    project_arrived(1)
    project_arrived(4)
    arrive_near(10, at(3, 1), 1)
    arrive_near(11, at(1, 1), 0)
    arrive(2)
    arrive(5)
    project_arrived(2)
    project_arrived(5)
    arrive_near(12, at(2, 1), 0)
    arrive_near(13, at(2, 1), 1)
    reach = jnp.max(largest[0], 1, keepdims=True) * jnp.max(largest[1], 1, keepdims=True)
    reach_ref[...] = jnp.broadcast_to(reach, reach_ref.shape)
    for copy in sent:
        copy.wait_send()
    for copy in stores:
        copy.wait()
    for copy in given:
        copy.wait_send()
    for copy in given:
        copy.wait_recv()


def project(x, g, wi, wo, counts):
    nodes, width = x.shape
    span = nodes * H
    vm = pl.BlockSpec(memory_space=pltpu.VMEM)
    anywhere = pl.BlockSpec(memory_space=pl.ANY)
    dma = pltpu.SemaphoreType.DMA
    return pl.pallas_call(
        project_kernel,
        out_shape=(
            jax.ShapeDtypeStruct(counts.shape, jnp.int32),
            jax.ShapeDtypeStruct((1, B), F32),
            jax.ShapeDtypeStruct((span, width), BF16),
            jax.ShapeDtypeStruct((span, 2 * HD), BF16),
            jax.ShapeDtypeStruct((2 * HD, span), BF16),
            jax.ShapeDtypeStruct((HD, span), BF16),
            jax.ShapeDtypeStruct((HD, span), BF16),
        ),
        in_specs=[anywhere] * 4 + [vm],
        out_specs=(vm, vm) + (anywhere,) * 5,
        scratch_shapes=[
            pltpu.VMEM((H, nodes, width), BF16),
            pltpu.VMEM((span, 2 * HD), BF16),
            pltpu.VMEM((2 * HD, span), BF16),
            pltpu.VMEM((HD, span), BF16),
            pltpu.VMEM(g.shape, BF16),
            pltpu.VMEM(wi.shape, BF16),
            pltpu.VMEM(wo.shape, BF16),
            pltpu.VMEM((width, nodes), BF16),
            dma((21,)),
            dma((21,)),
            dma((4,)),
            dma((8 * H + 1,)),
        ],
        compiler_params=pltpu.CompilerParams(collective_id=0, has_side_effects=True, vmem_limit_bytes=VMEM_BYTES),
        name="project",
    )(x, g, wi, wo, counts)


def attention_kernel(
    group, order_ref, reach_ref, blocks_ref, counts_ref, kv_ref, kvt_ref, qt_ref, gt_ref, all_hbm, grads_ref, weight_ref,
    total_ref, all_ref, load_sem,
):
    block_count = kvt_ref.shape[1] // B
    load = pltpu.make_async_copy(all_hbm, all_ref, load_sem)
    load.start()
    total_ref[...] = jnp.zeros_like(total_ref)
    zero = jnp.zeros((HD, B), BF16)

    def query_blocks(ids, live, shifted):
        heres = [pl.ds(pl.multiple_of(i * B, B), B) for i in ids]
        spots = [[pl.ds(pl.multiple_of(blocks_ref[j, i] * B, B), B) for j in range(live)] for i in ids]
        aparts, products = [], []
        for here, chosen in zip(heres, spots):
            apart = jnp.concatenate(
                [jnp.concatenate([qt_ref[:, here], zero], 1), jnp.concatenate([zero, gt_ref[:, here]], 1)], 0
            )
            aparts.append(apart)
            products.append(dot(jnp.concatenate([kv_ref[spot, :] for spot in chosen], 0), apart))
        pairs = []
        for i, product in zip(ids, products):
            count = counts_ref[i]
            scores = [product[:B, :B]]
            for j in range(1, live):
                scores.append(product[j * B : (j + 1) * B, :B] + jnp.where(j < count, 0.0, NEGATIVE))
            scores = jnp.concatenate(scores, 0)
            grad_probs = product[:, B:]
            if shifted:
                scores = scores - jnp.max(scores, 0, keepdims=True)
            raised = jnp.exp(scores)
            inverse = 1.0 / jnp.sum(raised, 0, keepdims=True)
            row_delta = jnp.sum(raised * grad_probs, 0, keepdims=True) * inverse
            probs = raised * inverse
            grad_scores = (probs * (grad_probs - row_delta)).astype(BF16)
            pairs.append(jnp.concatenate([grad_scores, probs.astype(BF16)], 1))
        outs, terms = [], []
        for apart, chosen, pair in zip(aparts, spots, pairs):
            outs.append(dot(jnp.concatenate([kvt_ref[:, spot] for spot in chosen], 1), pair))
            terms.append(dot(apart, pair, NT))
        for here, out in zip(heres, outs):
            grads_ref[0:HD, here] = out[HD:, B:].astype(BF16)
            grads_ref[HD : 2 * HD, here] = (out[:HD, :B] * SCALE).astype(BF16)
        for chosen, term in zip(spots, terms):
            for j, spot in enumerate(chosen):
                total_ref[:, spot] += term[:, j * B : (j + 1) * B]

    def step(index, carry):
        ids = [order_ref[0, index * group + t] for t in range(group)]
        most = counts_ref[ids[0]]
        for live in range(1, KMAX + 1):
            pl.when(most == live)(partial(query_blocks, ids, live, False))
        return carry

    def step_shifted(index, carry):
        query_blocks([index], KMAX, True)
        return carry

    calm = reach_ref[0, 0] <= CALM

    @pl.when(calm)
    def _():
        lax.fori_loop(0, block_count // group, step, 0)

    @pl.when(jnp.logical_not(calm))
    def _():
        lax.fori_loop(0, block_count, step_shifted, 0)

    grads_ref[2 * HD :, :] = total_ref[...].astype(BF16)
    load.wait()
    weight_ref[...] = dot(grads_ref[HD:, :], all_ref[...])


def attention(order, reach, blocks, counts, kv, kvt, qt, gt, everything):
    span, width = everything.shape
    vm = pl.BlockSpec(memory_space=pltpu.VMEM)
    sm = pl.BlockSpec(memory_space=pltpu.SMEM)
    return pl.pallas_call(
        partial(attention_kernel, 4),
        out_shape=(jax.ShapeDtypeStruct((4 * HD, span), BF16), jax.ShapeDtypeStruct((3 * HD, width), F32)),
        in_specs=[sm, sm, sm, sm, vm, vm, vm, vm, pl.BlockSpec(memory_space=pl.ANY)],
        out_specs=(vm, vm),
        scratch_shapes=[
            pltpu.VMEM((2 * HD, span), F32),
            pltpu.VMEM(everything.shape, BF16),
            pltpu.SemaphoreType.DMA,
        ],
        compiler_params=pltpu.CompilerParams(vmem_limit_bytes=VMEM_BYTES),
        name="attention",
    )(order, reach, blocks, counts, kv, kvt, qt, gt, everything)


ROWS = (256, 64, 16)


class Sum:
    def __init__(self, number, axes, columns, whole, sems, scratch, along, place_of, core):
        self.number, self.axes, self.columns, self.whole, self.sems = number, axes, columns, whole, sems
        self.total, self.out, self.quarters, self.parts, self.levels = scratch
        self.along = along
        self.place = [place_of[axis] for axis in axes]
        self.core = core
        self.waiting, self.sent = {}, []

    def send(self, phase, axis, source, target):
        copies = {}
        for offset in (2, 1, 3):
            copies[offset] = remote(
                source(offset), target(offset), self.sems, (self.number, phase, offset - 1), self.along(axis, offset)
            )
            copies[offset].start()
        self.waiting[phase] = copies
        self.sent += copies.values()

    def arrive(self, *phases):
        for phase in phases:
            for copy in self.waiting[phase].values():
                copy.wait_recv()

    def scatter_first(self, value):
        self.total[...] = value
        self.out[0 : ROWS[0], :] = value.astype(BF16)
        spot = lambda offset: part((self.place[0] + offset) % SIDE, ROWS[1])
        self.send(0, self.axes[0], lambda o: self.out.at[spot(o), :], lambda o: self.quarters.at[o - 1])

    def scatter_second(self):
        self.arrive(0)
        value = self.total[part(self.place[0], ROWS[1]), :] + self.quarters[0].astype(F32)
        value += self.quarters[1].astype(F32) + self.quarters[2].astype(F32)
        self.total[0 : ROWS[1], :] = value
        self.out[ROWS[0] :, :] = value.astype(BF16)
        spot = lambda offset: part(ROWS[0] // ROWS[2] + (self.place[1] + offset) % SIDE, ROWS[2])
        self.send(1, self.axes[1], lambda o: self.out.at[spot(o), :], lambda o: self.parts.at[o - 1])

    def scattered(self):
        self.arrive(1)
        value = self.total[part(self.place[1], ROWS[2]), :] + self.parts[0].astype(F32)
        return (value + (self.parts[1].astype(F32) + self.parts[2].astype(F32))).astype(BF16)

    def exchange(self, axis, place):
        self.levels[place] = self.scattered()
        here = self.levels.at[place]
        self.send(2, axis, lambda o: here, lambda o: here)

    def exchanged(self):
        self.arrive(2)
        value = [self.levels[k].astype(F32) for k in range(SIDE)]
        self.region()[...] = ((value[0] + value[1]) + (value[2] + value[3])).astype(BF16)

    def region(self, second=None, columns=None):
        second = self.place[1] if second is None else second
        first = self.core * ROWS[0] + self.place[0] * ROWS[1] + second * ROWS[2]
        rows = pl.ds(pl.multiple_of(first, ROWS[2]), ROWS[2])
        return self.whole.at[rows, self.columns if columns is None else columns]

    def gather(self):
        here = self.region()
        self.send(3, self.axes[1], lambda o: here, lambda o: here)
        self.send(4, self.axes[0], lambda o: here, lambda o: here)

    def gather_on(self):
        for offset, copy in self.waiting[3].items():
            copy.wait_recv()
            here = self.region((self.place[1] + SIDE - offset) % SIDE)
            self.send(4 + offset, self.axes[0], lambda o: here, lambda o: here)

    def gathered(self):
        self.arrive(4, 5, 6, 7)


def finish_kernel(
    grads_hbm, weight_hbm, x_hbm, g_hbm, wi_hbm, wo_hbm,
    layer_hbm, gradf_hbm, osum_hbm, isum_hbm,
    layer_ref, gradf_ref, osum_ref, isum_ref,
    x_ref, g_ref, wi_ref, wo_ref, attended_ref, rows_ref, merged_ref, theirs_ref, half_ref, total_ref,
    tot_a, tot_b, tot_c, tot_d, out_a, out_b, out_c, out_d, quarters_a, quarters_b, quarters_c, quarters_d,
    parts_a, parts_b, parts_c, parts_d, levels_c, levels_d,
    seq_send, seq_recv, core_send, core_recv, sum_send, sum_recv, spread_send, spread_recv, load_sem, store_sem,
):
    dp, seq = lax.axis_index("dp"), lax.axis_index("seq")
    z, x, y, core = dp // SIDE, dp % SIDE, seq // 2, seq % 2
    place_of = {"x": x, "y": y, "z": z}
    nodes, width = x_ref.shape
    half = nodes // 2
    other = (dp, y * 2 + (core + 1) % 2)
    seq_sems, core_sems = (seq_send, seq_recv), (core_send, core_recv)

    def along(axis, offset):
        if axis == "y":
            return (dp, ((y + offset) % SIDE) * 2 + core)
        if axis == "x":
            return (z * SIDE + (x + offset) % SIDE, seq)
        return (((z + offset) % SIDE) * SIDE + x, seq)

    peers = seq_peers(seq)
    met = greet([(dp, peer) for peer in peers] + [along(axis, offset) for axis in ("x", "z") for offset in (1, 2, 3)])
    loads = [
        pltpu.make_async_copy(source, target, load_sem.at[k])
        for k, (source, target) in enumerate(
            (
                (weight_hbm.at[:, :, part(core, ROWS[0])], merged_ref.at[:, part(core, HD), :]),
                (grads_hbm.at[0, :, part(seq, nodes)], attended_ref.at[part(seq, HD), :]),
                (g_hbm, g_ref),
                (x_hbm, x_ref),
                (wo_hbm, wo_ref),
                (wi_hbm, wi_ref),
                (grads_hbm.at[pl.ds(1, 3), :, part(seq, nodes)], rows_ref.at[:, part(seq, HD), :]),
            )
        )
    ]
    for load in loads:
        load.start()
    met()

    sent, stores = [], []

    def store(source, target):
        stores.append(pltpu.make_async_copy(source, target, store_sem.at[len(stores)]))
        stores[-1].start()

    def back(piece, source, target):
        copies = []
        for place, peer in enumerate(peers):
            copies.append(remote(source(peer), target, seq_sems, (piece, place), (dp, peer)))
            copies[-1].start()
        sent.extend(copies)
        return copies

    def back_rows(kind):
        return back(
            1 + kind, lambda peer: grads_hbm.at[1 + kind, :, part(peer, nodes)], rows_ref.at[kind, part(seq, HD), :]
        )

    swap = remote(weight_hbm.at[:, :, part(1 - core, ROWS[0])], theirs_ref, core_sems, 0, other)
    swap.start()
    sent.append(swap)
    back_attended = back(0, lambda peer: grads_hbm.at[0, :, part(peer, nodes)], attended_ref.at[part(seq, HD), :])

    sums = (sum_send, sum_recv)
    make = lambda *args: Sum(*args, along, place_of, core)
    both = make(0, ("z", "x"), pl.ds(0, 2 * width), isum_ref, sums, (tot_a, out_a, quarters_a, parts_a, None))
    last = make(1, ("x", "z"), pl.ds(2 * width, width), isum_ref, sums, (tot_b, out_b, quarters_b, parts_b, None))
    left = make(2, ("x", "z"), pl.ds(0, half), osum_ref, sums, (tot_c, out_c, quarters_c, parts_c, levels_c))
    right = make(3, ("z", "x"), pl.ds(half, half), osum_ref, sums, (tot_d, out_d, quarters_d, parts_d, levels_d))

    loads[0].wait()
    swap.wait_recv()
    merged_ref[:, part(1 - core, HD), :] = theirs_ref[...]
    both.scatter_first(jnp.concatenate([merged_ref[0].T, merged_ref[1].T], 1))
    last.scatter_first(merged_ref[2].T)
    back_q = back_rows(0)
    for load in loads[1:]:
        load.wait()
    both.scatter_second()
    last.scatter_second()

    for copy in back_attended:
        copy.wait_recv()
    half_ref[0] = dot(attended_ref[part(1 - core, ROWS[0]), :], g_ref[...]).astype(BF16)
    merge = remote(half_ref.at[0], half_ref.at[1], core_sems, 1, other)
    merge.start()
    sent.append(merge)
    total_ref[0 : ROWS[0], :] = dot(attended_ref[part(core, ROWS[0]), :], g_ref[...])

    merge.wait_recv()
    merged = total_ref[0 : ROWS[0], :] + half_ref[1].astype(F32)
    left.scatter_first(merged[:, :half])
    right.scatter_first(merged[:, half:])

    spread = []
    for job, kinds in ((both, (0, 1)), (last, (2,))):
        value = job.scattered()
        for k, kind in enumerate(kinds):
            columns = pl.ds(pl.multiple_of(kind * width + y * 2 * HD, 2 * HD), 2 * HD)
            here = job.region(columns=columns)
            here[...] = value[:, k * 2 * HD : (k + 1) * 2 * HD]
            for offset in (2, 1, 3):
                spread.append(remote(here, here, (spread_send, spread_recv), (kind, offset - 1), along("y", offset)))
                spread[-1].start()
    sent.extend(spread)
    back_k = back_rows(1)
    left.scatter_second()
    right.scatter_second()
    for copy in spread:
        copy.wait_recv()
    both.gather()
    last.gather()
    left.exchange("y", y)
    right.exchange("y", y)
    back_v = back_rows(2)
    both.gather_on()
    last.gather_on()
    layer_ref[...] = (x_ref[...].astype(F32) + dot(attended_ref[...], wo_ref[...], TN)).astype(BF16)
    store(layer_ref, layer_hbm)
    for copy in back_q:
        copy.wait_recv()
    total_ref[...] = dot(wi_ref[:, :width], rows_ref[0])
    left.exchanged()
    right.exchanged()
    left.gather()
    right.gather()
    both.gathered()
    last.gathered()

    def share(source, target, index):
        mine = part(core, ROWS[0])
        copy = remote(source.at[mine, :], target.at[mine, :], core_sems, index, other)
        copy.start()
        store(source.at[mine, :], target.at[mine, :])
        sent.append(copy)
        return copy

    share_i = share(isum_ref, isum_hbm, 2)
    left.gather_on()
    right.gather_on()
    for copy in back_k:
        copy.wait_recv()
    total_ref[...] += dot(wi_ref[:, width : 2 * width], rows_ref[1])
    late = {id(copy) for copy in back_v}
    settled = [copy for copy in sent if id(copy) not in late]
    for job in (both, last, left, right):
        settled.extend(job.sent)
    for copy in settled + back_v:
        copy.wait_send()
    for copy in back_v:
        copy.wait_recv()
    turned = (total_ref[...] + dot(wi_ref[:, 2 * width :], rows_ref[2])).T
    gradf_ref[...] = (g_ref[...].astype(F32) + turned).astype(BF16)
    store(gradf_ref, gradf_hbm)
    left.gathered()
    right.gathered()
    share_o = share(osum_ref, osum_hbm, 3)
    share_o.wait_send()
    for copy in stores:
        copy.wait()
    share_i.wait_recv()
    share_o.wait_recv()


def finish(grads, weight, x, g, wi, wo):
    nodes, width = x.shape
    anywhere = pl.BlockSpec(memory_space=pl.ANY)
    columns = (4 * HD, 2 * HD, width // 2, width // 2)
    dma = pltpu.SemaphoreType.DMA
    results = [(nodes, width), (nodes, width), (width, width), (width, 3 * width)]
    return pl.pallas_call(
        finish_kernel,
        out_shape=tuple(jax.ShapeDtypeStruct(shape, BF16) for shape in results),
        in_specs=[anywhere] * 6,
        out_specs=(anywhere,) * 4,
        scratch_shapes=[pltpu.VMEM(shape, BF16) for shape in results]
        + [
            pltpu.VMEM(x.shape, BF16),
            pltpu.VMEM(g.shape, BF16),
            pltpu.VMEM(wi.shape, BF16),
            pltpu.VMEM(wo.shape, BF16),
            pltpu.VMEM((width, nodes), BF16),
            pltpu.VMEM((3, width, nodes), BF16),
            pltpu.VMEM((3, 2 * HD, ROWS[0]), F32),
            pltpu.VMEM((3, HD, ROWS[0]), F32),
            pltpu.VMEM((2, ROWS[0], width), BF16),
            pltpu.VMEM((width, nodes), F32),
        ]
        + [pltpu.VMEM((ROWS[0], n), F32) for n in columns]
        + [pltpu.VMEM((ROWS[0] + ROWS[1], n), BF16) for n in columns]
        + [pltpu.VMEM((SIDE - 1, ROWS[1], n), BF16) for n in columns]
        + [pltpu.VMEM((SIDE - 1, ROWS[2], n), BF16) for n in columns]
        + [pltpu.VMEM((SIDE, ROWS[2], n), BF16) for n in columns[2:]]
        + [dma((4, H - 1))] * 2
        + [dma((4,))] * 2
        + [dma((4, 8, SIDE - 1))] * 2
        + [dma((3, SIDE - 1))] * 2
        + [dma((7,)), dma((4,))],
        compiler_params=pltpu.CompilerParams(collective_id=1, has_side_effects=True, vmem_limit_bytes=VMEM_BYTES),
        name="finish",
    )(grads.reshape(4, HD, -1), weight.reshape(3, HD, -1), x, g, wi, wo)


def emit_kernel(factor, layer_ref, gradf_ref, osum_ref, isum_ref, layer_out, gradf_out, osum_out, isum_out):
    layer_out[...] = layer_ref[...]
    gradf_out[...] = gradf_ref[...]
    osum_out[...] = osum_ref[...].astype(F32) * factor
    isum_out[...] = isum_ref[...].astype(F32) * factor


def emit(layer, gradf, osum, isum, factor):
    arrays = (layer, gradf, osum, isum)
    kinds = (BF16, BF16, F32, F32)
    rows = layer.shape[0] // 2
    specs = [pl.BlockSpec((rows, a.shape[1]), lambda i: (i, 0)) for a in arrays]
    return pl.pallas_call(
        partial(emit_kernel, factor),
        grid=(2,),
        out_shape=tuple(jax.ShapeDtypeStruct(a.shape, kind) for a, kind in zip(arrays, kinds)),
        in_specs=specs,
        out_specs=tuple(specs),
        compiler_params=pltpu.CompilerParams(vmem_limit_bytes=VMEM_BYTES),
        name="emit",
    )(*arrays)


def shards(features, input_weight, output_weight, key_blocks, key_count, cotangent):
    x, g = features[0], cotangent[0]
    order, reach, everything, kv, kvt, qt, gt = project(x, g, input_weight, output_weight, key_count[0])
    grads, weight = attention(order, reach, key_blocks[0, 0].T, key_count[0, 0], kv, kvt, qt, gt, everything)
    results = finish(grads, weight, x, g, input_weight, output_weight)
    factor = 1.0 / (lax.axis_size("dp") * lax.axis_size("seq") * x.shape[0]) ** 0.5
    layer_out, grad_features, output_total, input_total = emit(*results, factor)
    return (layer_out[None], grad_features[None], input_total, output_total)


def solution(mesh):
    in_specs = (
        P("dp", "seq", None),
        P(),
        P(),
        P("dp", "seq", None, None),
        P("dp", "seq", None),
        P("dp", "seq", None),
    )
    out_specs = (P("dp", "seq", None), P("dp", "seq", None), P(), P())
    return jax.shard_map(shards, mesh=mesh, in_specs=in_specs, out_specs=out_specs, check_vma=False)
```
